32 devices in a mesh: dp: 4 (over z), fsdp: 8 (over y, x, core).
Axes of the slice: x: 2, y: 2, z: 4, core: 2. Of those that a mesh axis runs over, the one named last changes fastest.
Arguments:
- global_tokens: bfloat16 [96, 14, 14, 512], P(('dp', 'fsdp')), may hold values from -6 to 6
- local_tokens: bfloat16 [288, 7, 7, 512], P(('dp', 'fsdp')), may hold values from -6 to 6
- crop_extent: int32 [288, 2], P(('dp', 'fsdp')), may hold values from 4 to 7
- conv_weight: bfloat16 [2, 9, 512], P(None, None, 'fsdp'), may hold values from -2 to 2
- vectors: bfloat16 [2, 7, 512], P(None, None, 'fsdp'), may hold values from -1 to 1
- gains: bfloat16 [2, 2, 512], P(None, None, 'fsdp'), may hold values from 0.5 to 1.5
- qkv_weight: bfloat16 [2, 512, 1536], P(None, 'fsdp'), may hold values from -0.25 to 0.25
- proj_weight: bfloat16 [2, 512, 512], P(None, 'fsdp'), may hold values from -0.625 to 0.625
- fc1_weight: bfloat16 [2, 512, 2048], P(None, 'fsdp'), may hold values from -0.25 to 0.25
- fc1_bias: bfloat16 [2, 2048], P(None, 'fsdp'), may hold values from -1 to 1
- fc2_weight: bfloat16 [2, 2048, 512], P(None, 'fsdp'), may hold values from -0.125 to 0.125
- global_cotangent: bfloat16 [96, 14, 14, 512], P(('dp', 'fsdp')), may hold values from -6 to 6
- local_cotangent: bfloat16 [288, 7, 7, 512], P(('dp', 'fsdp')), may hold values from -6 to 6
Outputs:
- global_out: bfloat16 [96, 14, 14, 512], P(('dp', 'fsdp'))
- local_out: bfloat16 [288, 7, 7, 512], P(('dp', 'fsdp'))
- global_grad: float32 [96, 14, 14, 512], P(('dp', 'fsdp'))
- local_grad: float32 [288, 7, 7, 512], P(('dp', 'fsdp'))
- conv_grad: float32 [2, 9, 512], P(None, None, 'fsdp')
- vectors_grad: float32 [2, 7, 512], P(None, None, 'fsdp')
- gains_grad: float32 [2, 2, 512], P(None, None, 'fsdp')
- qkv_grad: float32 [2, 512, 1536], P(None, 'fsdp')
- proj_grad: float32 [2, 512, 512], P(None, 'fsdp')
- fc1_grad: float32 [2, 512, 2048], P(None, 'fsdp')
- fc1_bias_grad: float32 [2, 2048], P(None, 'fsdp')
- fc2_grad: float32 [2, 2048, 512], P(None, 'fsdp')
The draws below stay inside these ranges and needn't reach their ends.
Inputs may be any that keep to these rules, and one draw needn't show every extreme that they name: `crop_extent`: for each local crop, the rows and the columns of its 7 x 7 canvas that hold patches, counted from the canvas's first row and column.
All inputs are finite; a program needn't handle non-finite values.
Results may differ from the reference program's by a relative error of at most 0.025.
Values may be sent and summed in bfloat16 or wider, within the bound.
No kernel may reach another device: no remote copies, remote signals or barrier semaphores. Data moves between devices by JAX's collectives and lax.ppermute only.
A program may use at most 256 MiB of HBM per device.

```python
import jax
import jax.numpy as jnp
from jax import lax

C = 512
FF = 2048
HEAD_DIM = 32
WIN = 7
SIDE = 14
CROP_SETS = 3
GLOBALS = 96
LOCALS = 288
DEVICES = 32


def plant(array, rng, least, high):
    spot = [jax.random.randint(jax.random.fold_in(rng, axis), (), 0, length) for axis, length in enumerate(array.shape)]
    widest = array.shape.index(max(array.shape))
    next_to = spot[:widest] + [(spot[widest] + 1) % array.shape[widest]] + spot[widest + 1:]
    return array.at[tuple(spot)].set(least).at[tuple(next_to)].set(high)


def levels(own_key, dims, shards, least, top_value):
    def one(dim, blocks):
        heights = jax.random.uniform(jax.random.fold_in(jax.random.fold_in(own_key, 6), dim), (blocks,), jnp.float32, least / len(shards), top_value / len(shards))
        return jnp.repeat(jnp.exp(heights), dims[dim] // blocks).reshape((-1,) + (1,) * (len(dims) - dim - 1))

    level = one(*shards[0])
    for cut in shards[1:]:
        level = level * one(*cut)
    return level


def gaussian(key, shape, deviation, limit, pieces=(), kind=jnp.bfloat16):
    drawn = jax.random.normal(key, shape, jnp.float32) * deviation
    if len(pieces) > 0:
        drawn = levels(key, shape, pieces, -0.22, 0.18) * drawn
    return jnp.clip(drawn, min=-limit, max=limit).astype(kind)


def setup_inputs(seed: int = 0) -> dict:
    key_of = jax.random.split(jax.random.key(seed), 14)
    global_tokens = gaussian(key_of[0], (GLOBALS, SIDE, SIDE, C), 1.0, 6.0, ((0, 32),))
    local_tokens = gaussian(key_of[1], (LOCALS, WIN, WIN, C), 1.0, 6.0, ((0, 32),))
    crop_extent = plant(jax.random.randint(key_of[2], (LOCALS, 2), 4, WIN + 1), jax.random.fold_in(key_of[2], 1), 4, WIN).astype(jnp.int32)
    conv_weight = gaussian(key_of[3], (2, 9, C), 9 ** -0.5, 2.0, ((2, 8),))
    vectors = gaussian(key_of[4], (2, 7, C), 0.2, 1.0, ((2, 8),))
    gains = jnp.clip(1.0 + 0.1 * jax.random.normal(key_of[5], (2, 2, C), jnp.float32), 0.5, 1.5).astype(jnp.bfloat16)
    qkv_weight = gaussian(key_of[6], (2, C, 3 * C), C ** -0.5, 0.25, ((1, 8),))
    proj_weight = gaussian(key_of[7], (2, C, C), (C // 6) ** -0.5, 0.625, ((1, 8),))
    fc1_weight = gaussian(key_of[8], (2, C, FF), C ** -0.5, 0.25, ((1, 8),))
    fc1_bias = gaussian(key_of[9], (2, FF), 0.2, 1.0, ((1, 8),))
    fc2_weight = gaussian(key_of[10], (2, FF, C), FF ** -0.5, 0.125, ((1, 8),))
    global_cotangent = gaussian(key_of[11], (GLOBALS, SIDE, SIDE, C), 1.0, 6.0, ((0, 32),))
    local_cotangent = gaussian(key_of[12], (LOCALS, WIN, WIN, C), 1.0, 6.0, ((0, 32),))
    return dict(global_tokens=global_tokens, local_tokens=local_tokens, crop_extent=crop_extent, conv_weight=conv_weight, vectors=vectors, gains=gains, qkv_weight=qkv_weight, proj_weight=proj_weight, fc1_weight=fc1_weight, fc1_bias=fc1_bias, fc2_weight=fc2_weight, global_cotangent=global_cotangent, local_cotangent=local_cotangent)


EPSILON = 1e-05
LINEAR_FORMS = ('...k,kd->...d', '...d,kd->...k', '...k,...d->kd')
WINDOW_SCORE = ('wqhd,wkhd->whqk', 'whqk,wkhd->wqhd', 'wqhd,whqk->wkhd')
WINDOW_MIX = ('whqk,wkhd->wqhd', 'wqhd,wkhd->whqk', 'whqk,wqhd->wkhd')
CHANNEL_SCORE = ('bngi,bngj->bgij', 'bgij,bngj->bngi', 'bngi,bgij->bngj')
CHANNEL_MIX = ('bgij,bngj->bngi', 'bngi,bngj->bgij', 'bgij,bngi->bngj')

@jax.custom_vjp
def low(v):
    return lax.optimization_barrier(v.astype(jnp.bfloat16)).astype(jnp.float32)

@jax.custom_vjp
def low_back(v):
    return v

def low_keep(v):
    return (low(v), None)

def low_pass(kept, grad):
    return (grad,)

def back_keep(v):
    return (v, None)

def back_low(kept, grad):
    return (low(grad),)
low.defvjp(low_keep, low_pass)
low_back.defvjp(back_keep, back_low)

def contract(forms, first_operand, second_operand):
    return jnp.einsum(forms[0], first_operand, second_operand, precision=lax.Precision.HIGHEST)

def layer_norm(values, gain, shift):
    center = lax.optimization_barrier(jnp.mean(values, axis=-1, keepdims=True))
    centred = values - center
    variance = lax.optimization_barrier(jnp.mean(centred * centred, axis=-1, keepdims=True))
    return centred * lax.rsqrt(variance + EPSILON) * gain + shift

def softmax_rows(scores):
    shifted = scores - lax.optimization_barrier(jnp.max(scores, axis=-1, keepdims=True))
    exponent = jnp.exp(shifted)
    return exponent / lax.optimization_barrier(jnp.sum(exponent, axis=-1, keepdims=True))

def linear(inputs, weight):
    return low_back(contract(LINEAR_FORMS, inputs, weight))

def position_conv(values, mask, kernel, shift):
    extent = values.shape[1]
    padded = jnp.pad(values, ((0, 0), (1, 1), (1, 1), (0, 0)))
    total = values + shift
    for index in range(9):
        row_start = index // 3
        col_start = index % 3
        total = total + kernel[index] * padded[:, row_start:row_start + extent, col_start:col_start + extent, :]
    return total * mask[..., None]

def to_windows(values):
    count, extent = (values.shape[0], values.shape[1])
    parts = extent // WIN
    shaped = values.reshape(count, parts, WIN, parts, WIN, -1)
    return shaped.transpose(0, 1, 3, 2, 4, 5).reshape(count * parts * parts, WIN * WIN, -1)

def from_windows(values, count, extent):
    parts = extent // WIN
    shaped = values.reshape(count, parts, parts, WIN, WIN, -1)
    return shaped.transpose(0, 1, 3, 2, 4, 5).reshape(count, extent, extent, -1)

def spatial_mix(query, key, value, mask):
    count, extent, width = (query.shape[0], query.shape[1], query.shape[3])
    heads = width // HEAD_DIM
    wq = to_windows(query).reshape(-1, WIN * WIN, heads, HEAD_DIM)
    wk = to_windows(key).reshape(-1, WIN * WIN, heads, HEAD_DIM)
    wv = to_windows(value).reshape(-1, WIN * WIN, heads, HEAD_DIM)
    valid = to_windows(mask[..., None])[:, :, 0]
    scores = low_back(contract(WINDOW_SCORE, wq, wk)) * HEAD_DIM ** (-0.5)
    scores = jnp.where(valid[:, None, None, :] > 0.5, scores, -1000000000.0)
    weights = low(softmax_rows(scores))
    mixed = low_back(contract(WINDOW_MIX, weights, wv))
    return from_windows(mixed.reshape(-1, WIN * WIN, width), count, extent)

def channel_mix(query, key, value, mask):
    count, width = (query.shape[0], query.shape[3])
    groups = width // HEAD_DIM
    valid = mask.reshape(count, -1, 1, 1)
    gq = query.reshape(count, -1, groups, HEAD_DIM)
    gk = key.reshape(count, -1, groups, HEAD_DIM) * valid
    gv = value.reshape(count, -1, groups, HEAD_DIM)
    scores = low_back(contract(CHANNEL_SCORE, gk, gv)) * HEAD_DIM ** (-0.5)
    weights = low(softmax_rows(scores))
    mixed = low_back(contract(CHANNEL_MIX, weights, gq))
    return mixed.reshape(query.shape)

def block(values, mask, params, mixer):
    kernel, shifts, norm_gains, qkv_w, proj_w, up_w, up_b, down_w = params
    width = values.shape[-1]
    conv = position_conv(values, mask, kernel, shifts[0])
    normed = low(layer_norm(conv, norm_gains[0], shifts[1]))
    joined = linear(normed, qkv_w)
    query = low(joined[..., :width] + shifts[2])
    key = low(joined[..., width:2 * width])
    value = low(joined[..., 2 * width:] + shifts[3])
    mixed = low(mixer(query, key, value, mask))
    resid = conv + linear(mixed, proj_w) + shifts[4]
    normed_two = low(layer_norm(resid, norm_gains[1], shifts[5]))
    hidden = linear(normed_two, up_w) + up_b
    hidden = low(0.5 * hidden * (1.0 + jnp.tanh(0.7978845608 * (hidden + 0.044715 * hidden * hidden * hidden))))
    return (resid + linear(hidden, down_w) + shifts[6]) * mask[..., None]

def block_pair(pair, masks, weights, index):
    params = tuple((w[index] for w in weights))
    mixer = spatial_mix if index == 0 else channel_mix
    return (block(pair[0], masks[0], params, mixer), block(pair[1], masks[1], params, mixer))

def crop_masks(extent, count):
    places = jnp.arange(WIN, dtype=jnp.int32)
    rows = places[None, :, None] < extent[:, 0][:, None, None]
    cols = places[None, None, :] < extent[:, 1][:, None, None]
    local_mask = jnp.logical_and(rows, cols).astype(jnp.float32)
    global_mask = jnp.ones((count, SIDE, SIDE), jnp.float32)
    return (global_mask, local_mask)

def reference(global_tokens, local_tokens, crop_extent, conv_weight, vectors, gains, qkv_weight, proj_weight, fc1_weight, fc1_bias, fc2_weight, global_cotangent, local_cotangent):
    weights = tuple((w.astype(jnp.float32) for w in (conv_weight, vectors, gains, qkv_weight, proj_weight, fc1_weight, fc1_bias, fc2_weight)))
    glob_all = global_tokens.reshape(DEVICES, CROP_SETS, SIDE, SIDE, -1)
    loc_all = local_tokens.reshape(DEVICES, 3 * CROP_SETS, WIN, WIN, -1)
    ext_all = crop_extent.reshape(DEVICES, 3 * CROP_SETS, 2).astype(jnp.int32)
    cot_glob = global_cotangent.reshape(DEVICES, CROP_SETS, SIDE, SIDE, -1)
    cot_loc = local_cotangent.reshape(DEVICES, 3 * CROP_SETS, WIN, WIN, -1)

    def group_step(totals, items):
        glob, loc, extent, cot_g, cot_l = items
        masks = crop_masks(extent, glob.shape[0])

        def forward(glob_in, loc_in, params):
            start = (glob_in * masks[0][..., None], loc_in * masks[1][..., None])
            middle = block_pair(start, masks, params, 0)
            return block_pair(middle, masks, params, 1)
        outputs, pullback = jax.vjp(forward, glob.astype(jnp.float32), loc.astype(jnp.float32), weights)
        grad_g, grad_l, grad_w = pullback((cot_g.astype(jnp.float32), cot_l.astype(jnp.float32)))
        totals = tuple((a + b for a, b in zip(totals, grad_w)))
        return (totals, (outputs[0].astype(jnp.bfloat16), outputs[1].astype(jnp.bfloat16), grad_g, grad_l))
    zeros = tuple((jnp.zeros(w.shape, jnp.float32) for w in weights))
    totals, stacked = lax.scan(group_step, zeros, (glob_all, loc_all, ext_all, cot_glob, cot_loc))
    global_out = stacked[0].reshape(global_tokens.shape)
    local_out = stacked[1].reshape(local_tokens.shape)
    global_grad = stacked[2].reshape(global_tokens.shape)
    local_grad = stacked[3].reshape(local_tokens.shape)
    return (global_out, local_out, global_grad, local_grad, totals[0], totals[1], totals[2], totals[3], totals[4], totals[5], totals[6], totals[7])
```

```python
import functools

import jax
import jax.numpy as jnp
from jax import lax
from jax.experimental import pallas as pl
from jax.experimental.pallas import tpu as pltpu
from jax.sharding import PartitionSpec as P

BF = jnp.bfloat16
F32 = jnp.float32
C = 512
FF = 2048
HEAD = 32
WIN = 7
SIDE = 14
CELL = 64
LANES = 128
GROUPS = C // LANES
PER = LANES // HEAD
EPS = 1e-5
SCALE = HEAD ** -0.5
VMEM = pl.BlockSpec(memory_space=pltpu.VMEM)
NT = (((1,), (1,)), ((), ()))
TN = (((0,), (0,)), ((), ()))
K_ROW, V_ROW, G_ROW, B_ROW, SMALL = 0, 9, 16, 18, 22


def mm(a, b):
    return jnp.dot(a, b, preferred_element_type=F32)


def mm_nt(a, b):
    return lax.dot_general(a, b, NT, preferred_element_type=F32)


def mm_tn(a, b):
    return lax.dot_general(a, b, TN, preferred_element_type=F32)


def call(kernel, outs, ins, scratch=(), limit=60):
    return pl.pallas_call(
        kernel,
        out_shape=outs,
        in_specs=[VMEM] * len(ins),
        out_specs=[VMEM] * len(outs),
        scratch_shapes=list(scratch),
        compiler_params=pltpu.CompilerParams(vmem_limit_bytes=limit * 2**20),
    )(*ins)


def shape(dims, kind):
    return jax.ShapeDtypeStruct(dims, kind)


def wide(m):
    return jnp.concatenate([m] * GROUPS, axis=1)


def fold8(v):
    return jnp.sum(v.reshape(v.shape[0] // 8, 8, v.shape[1]), axis=0)


def norm_parts(x):
    center = jnp.sum(x, axis=-1, keepdims=True) * (1.0 / C)
    xc = x - center
    var = jnp.sum(xc * xc, axis=-1, keepdims=True) * (1.0 / C)
    rstd = lax.rsqrt(var + EPS)
    return xc * rstd, rstd


def norm_back(dn, xhat, rstd, gain):
    gp = dn * gain
    m1 = jnp.sum(gp, axis=-1, keepdims=True) * (1.0 / C)
    m2 = jnp.sum(gp * xhat, axis=-1, keepdims=True) * (1.0 / C)
    return rstd * (gp - m1 - xhat * m2)


def head_masks(rows):
    lane = lax.broadcasted_iota(jnp.int32, (rows, LANES), 1) // HEAD
    return [lane == h for h in range(PER)]


def spread(v, masks):
    zero = jnp.zeros_like(v)
    return jnp.concatenate([jnp.where(m, v, zero) for m in masks], axis=0)


def gather_heads(full, masks):
    n = full.shape[0] // PER
    out = full[3 * n :]
    for h in (2, 1, 0):
        out = jnp.where(masks[h], full[h * n : (h + 1) * n], out)
    return out


def shifted_cols(left, right, j, step):
    if step == 0:
        return left, right
    if step == 1:
        return (
            jnp.where(j == 6, pltpu.roll(right, 6, 1), pltpu.roll(left, 7, 1)),
            pltpu.roll(right, 7, 1),
        )
    return (
        pltpu.roll(left, 1, 1),
        jnp.where(j == 0, pltpu.roll(left, 2, 1), pltpu.roll(right, 1, 1)),
    )


def canvas(ref, crop, lanes):
    base = crop * 32
    parts = [ref[pl.ds(base + 8 * w, 7), :, lanes] for w in range(4)]
    left = jnp.concatenate([parts[0], parts[2]], axis=0)
    right = jnp.concatenate([parts[1], parts[3]], axis=0)
    return left, right


def put_canvas(ref, crop, lanes, left, right, mask_ref):
    base = crop * 32
    zero = jnp.zeros((1, 8, LANES), F32)
    for w in range(4):
        side = right if w % 2 else left
        half = side[(w // 2) * 7 : (w // 2) * 7 + 7]
        rows = pl.ds(base + 8 * w, 8)
        ref[rows, :, lanes] = jnp.concatenate([half, zero], axis=0) * mask_ref[rows]


def conv_forward(u_ref, c_ref, small_ref, mask_ref, globals_, locals_):
    j14 = lax.broadcasted_iota(jnp.int32, (14, 8, LANES), 1)
    for g in range(GROUPS):
        lanes = pl.ds(g * LANES, LANES)
        taps = [small_ref[K_ROW + t : K_ROW + t + 1, lanes][None] for t in range(9)]
        shift = small_ref[V_ROW : V_ROW + 1, lanes][None]

        @pl.loop(0, globals_)
        def _(crop):
            left, right = canvas(u_ref, crop, lanes)
            zero = jnp.zeros((1, 8, LANES), F32)
            acc = [left + shift, right + shift]
            for e in (-1, 0, 1):
                for s, side in enumerate(shifted_cols(left, right, j14, e)):
                    tall = jnp.concatenate([zero, side, zero], axis=0)
                    for a in (-1, 0, 1):
                        acc[s] = acc[s] + taps[3 * (a + 1) + e + 1] * tall[1 + a : 15 + a]
            put_canvas(c_ref, crop, lanes, acc[0], acc[1], mask_ref)

        @pl.loop(0, locals_)
        def _(n):
            rows = pl.ds(globals_ * 32 + n * 8, 8)
            u = u_ref[rows, :, lanes]
            acc = u + shift
            for e in (-1, 0, 1):
                side = u if e == 0 else pltpu.roll(u, 7 if e == 1 else 1, 1)
                for a in (-1, 0, 1):
                    moved = side if a == 0 else jnp.roll(side, -a, axis=0)
                    acc = acc + taps[3 * (a + 1) + e + 1] * moved
            c_ref[rows, :, lanes] = acc * mask_ref[rows]


def conv_backward(d_ref, u_ref, du_ref, small_ref, acc_ref, globals_, locals_):
    j14 = lax.broadcasted_iota(jnp.int32, (14, 8, LANES), 1)
    for g in range(GROUPS):
        lanes = pl.ds(g * LANES, LANES)
        taps = [small_ref[K_ROW + t : K_ROW + t + 1, lanes][None] for t in range(9)]
        nothing = tuple(jnp.zeros((8, LANES), F32) for _ in range(10))

        def one_crop(crop, sums):
            sums = list(sums)
            left, right = canvas(d_ref, crop, lanes)
            own = canvas(u_ref, crop, lanes)
            zero = jnp.zeros((1, 8, LANES), F32)
            acc = [left, right]
            sums[9] = sums[9] + jnp.sum(left + right, axis=0)
            for e in (-1, 0, 1):
                for s, side in enumerate(shifted_cols(left, right, j14, -e)):
                    tall = jnp.concatenate([zero, side, zero], axis=0)
                    for a in (-1, 0, 1):
                        t = 3 * (a + 1) + e + 1
                        moved = tall[1 - a : 15 - a]
                        acc[s] = acc[s] + taps[t] * moved
                        sums[t] = sums[t] + jnp.sum(own[s] * moved, axis=0)
            base = crop * 32
            for w in range(4):
                side = acc[w % 2]
                half = side[(w // 2) * 7 : (w // 2) * 7 + 7]
                du_ref[pl.ds(base + 8 * w, 8), :, lanes] = jnp.concatenate([half, zero], axis=0)
            return tuple(sums)

        def one_local(n, sums):
            sums = list(sums)
            rows = pl.ds(globals_ * 32 + n * 8, 8)
            d = d_ref[rows, :, lanes]
            own = u_ref[rows, :, lanes]
            acc = d
            sums[9] = sums[9] + jnp.sum(d, axis=0)
            for e in (-1, 0, 1):
                side = d if e == 0 else pltpu.roll(d, 7 if e == -1 else 1, 1)
                for a in (-1, 0, 1):
                    t = 3 * (a + 1) + e + 1
                    moved = side if a == 0 else jnp.roll(side, a, axis=0)
                    acc = acc + taps[t] * moved
                    sums[t] = sums[t] + jnp.sum(own * moved, axis=0)
            du_ref[rows, :, lanes] = acc
            return tuple(sums)

        sums = lax.fori_loop(0, globals_, one_crop, nothing)
        sums = lax.fori_loop(0, locals_, one_local, sums)
        for t in range(10):
            acc_ref[t, :, lanes] = sums[t]


def spatial_forward(q_ref, k_ref, v_ref, mask_ref, o_ref, p_ref, windows):
    masks = head_masks(CELL)

    @pl.loop(0, windows)
    def _(w):
        rows = pl.ds(w * CELL, CELL)
        m = mask_ref[rows, :]
        valid = jnp.concatenate([m, m], axis=1) > 0.5
        for g in range(GROUPS):
            lanes = pl.ds(g * LANES, LANES)
            s = mm_nt(k_ref[rows, lanes], spread(q_ref[rows, lanes], masks))
            s = jnp.where(valid, s * SCALE, -1e9)
            e = jnp.exp(s - jnp.max(s, axis=0, keepdims=True))
            p = (e / jnp.sum(e, axis=0, keepdims=True)).astype(BF)
            p_ref[w, g] = p
            o_ref[rows, lanes] = gather_heads(mm_tn(p, v_ref[rows, lanes]), masks).astype(BF)


def spatial_backward(q_ref, k_ref, v_ref, p_ref, do_ref, dq_ref, dk_ref, dv_ref, acc_ref, windows):
    masks = head_masks(CELL)

    @pl.loop(0, windows)
    def _(w):
        rows = pl.ds(w * CELL, CELL)
        for g in range(GROUPS):
            lanes = pl.ds(g * LANES, LANES)
            p = p_ref[w, g]
            dos = spread(do_ref[rows, lanes], masks)
            dp = mm_nt(v_ref[rows, lanes], dos)
            pf = p.astype(F32)
            total = jnp.sum(pf * dp, axis=0, keepdims=True)
            ds = (pf * (dp - total) * SCALE).astype(BF)
            dv = mm(p, dos)
            dk = mm(ds, spread(q_ref[rows, lanes], masks))
            dq = gather_heads(mm_tn(ds, k_ref[rows, lanes]), masks)
            acc_ref[0, :, lanes] += fold8(dq)
            acc_ref[1, :, lanes] += fold8(dv)
            dq_ref[rows, lanes] = dq.astype(BF)
            dk_ref[rows, lanes] = dk.astype(BF)
            dv_ref[rows, lanes] = dv.astype(BF)


def same_head():
    a = lax.broadcasted_iota(jnp.int32, (LANES, LANES), 0) // HEAD
    b = lax.broadcasted_iota(jnp.int32, (LANES, LANES), 1) // HEAD
    return a == b


def over_crops(globals_, locals_, step):
    @pl.loop(0, globals_)
    def _(n):
        step(n, n * 4 * CELL, 4 * CELL)

    @pl.loop(0, locals_)
    def _(n):
        step(globals_ + n, globals_ * 4 * CELL + n * CELL, CELL)


def channel_forward(q_ref, k_ref, v_ref, mask_ref, o_ref, p_ref, globals_, locals_):
    same = same_head()

    def step(n, start, count):
        rows = pl.ds(start, count)
        m = mask_ref[rows, :].astype(BF)
        for g in range(GROUPS):
            lanes = pl.ds(g * LANES, LANES)
            s = mm_tn(v_ref[rows, lanes], k_ref[rows, lanes] * m)
            s = jnp.where(same, s * SCALE, -jnp.inf)
            e = jnp.exp(s - jnp.max(s, axis=0, keepdims=True))
            p = (e / jnp.sum(e, axis=0, keepdims=True)).astype(BF)
            p_ref[n, g] = p
            o_ref[rows, lanes] = mm(q_ref[rows, lanes], p).astype(BF)

    over_crops(globals_, locals_, step)


def channel_backward(
    q_ref, k_ref, v_ref, mask_ref, p_ref, do_ref, dq_ref, dk_ref, dv_ref, acc_ref, globals_, locals_
):
    def step(n, start, count):
        rows = pl.ds(start, count)
        mf = mask_ref[rows, :]
        m = mf.astype(BF)
        for g in range(GROUPS):
            lanes = pl.ds(g * LANES, LANES)
            p = p_ref[n, g]
            do = do_ref[rows, lanes]
            dq = mm_nt(do, p)
            dp = mm_tn(q_ref[rows, lanes], do)
            pf = p.astype(F32)
            total = jnp.sum(pf * dp, axis=0, keepdims=True)
            ds = (pf * (dp - total) * SCALE).astype(BF)
            dk = mm(v_ref[rows, lanes], ds) * mf
            dv = mm_nt(k_ref[rows, lanes] * m, ds)
            acc_ref[0, :, lanes] += fold8(dq)
            acc_ref[1, :, lanes] += fold8(dv)
            dq_ref[rows, lanes] = dq.astype(BF)
            dk_ref[rows, lanes] = dk.astype(BF)
            dv_ref[rows, lanes] = dv.astype(BF)

    over_crops(globals_, locals_, step)


def attention_forward(sizes, kind, u, mask, small, weights):
    globals_, locals_, shards = sizes
    windows = 4 * globals_ + locals_
    rows = windows * CELL
    chunk = rows // 3
    part = C // shards

    def kernel(u_ref, mask_ref, small_ref, w_ref, r_ref, c_ref, n_ref, q_ref, k_ref, v_ref, o_ref, p_ref):
        conv_forward(u_ref, c_ref, small_ref, mask_ref.reshape(windows * 8, 8, LANES), globals_, locals_)
        gain = small_ref[G_ROW : G_ROW + 1]
        shift = small_ref[V_ROW + 1 : V_ROW + 2]

        @pl.loop(0, windows)
        def _(w):
            x = c_ref[pl.ds(w * 8, 8)].reshape(CELL, C)
            xhat, _ = norm_parts(x)
            n_ref[pl.ds(w * CELL, CELL), :] = (xhat * gain + shift).astype(BF)

        def weight(i):
            return w_ref[:, i * part : (i + 1) * part, :].reshape(C, C)

        @pl.loop(0, 3)
        def _(i):
            here = pl.ds(i * chunk, chunk)
            n1 = n_ref[here, :]
            q_ref[here, :] = (mm(n1, weight(0)) + small_ref[V_ROW + 2 : V_ROW + 3]).astype(BF)
            k_ref[here, :] = mm(n1, weight(1)).astype(BF)
            v_ref[here, :] = (mm(n1, weight(2)) + small_ref[V_ROW + 3 : V_ROW + 4]).astype(BF)

        if kind == 0:
            spatial_forward(q_ref, k_ref, v_ref, mask_ref, o_ref, p_ref, windows)
        else:
            channel_forward(q_ref, k_ref, v_ref, mask_ref, o_ref, p_ref, globals_, locals_)

        @pl.loop(0, 3)
        def _(i):
            here = pl.ds(i * chunk, chunk)
            c = c_ref[pl.ds(i * (chunk // 8), chunk // 8)].reshape(chunk, C)
            r_ref[here, :] = c + mm(o_ref[here, :], weight(3)) + small_ref[V_ROW + 4 : V_ROW + 5]

    low = shape((rows, C), BF)
    probs = (windows, GROUPS, CELL, PER * CELL) if kind == 0 else (globals_ + locals_, GROUPS, LANES, LANES)
    outs = [shape((rows, C), F32), shape((windows * 8, 8, C), F32), low, low, low, low, low, shape(probs, BF)]
    return call(kernel, outs, (u, mask, small, weights))


def ffn_forward(sizes, r, mask, small, weights):
    globals_, locals_, shards = sizes
    windows = 4 * globals_ + locals_
    rows = windows * CELL
    chunk = rows // 3
    part = C // shards
    deep = FF // shards

    def kernel(r_ref, mask_ref, small_ref, w_ref, x_ref, n_ref, g_ref, s_ref):
        gain = small_ref[G_ROW + 1 : G_ROW + 2]
        shift = small_ref[V_ROW + 5 : V_ROW + 6]

        @pl.loop(0, windows)
        def _(w):
            here = pl.ds(w * CELL, CELL)
            xhat, _ = norm_parts(r_ref[here, :])
            n_ref[here, :] = (xhat * gain + shift).astype(BF)

        @pl.loop(0, 3)
        def _(i):
            here = pl.ds(i * chunk, chunk)
            n2 = n_ref[here, :]
            for t in range(FF // C):
                w = w_ref[:, t * part : (t + 1) * part, :].reshape(C, C)
                h = mm(n2, w) + small_ref[B_ROW + t : B_ROW + t + 1]
                h2 = h * h
                a = 0.5 + 0.5 * jnp.tanh(h * (0.7978845608 + (0.7978845608 * 0.044715) * h2))
                g = h * a
                slope = a + (2.0 * g) * (1.0 - a) * (0.7978845608 + (3 * 0.7978845608 * 0.044715) * h2)
                g_ref[here, t * C : (t + 1) * C] = g.astype(BF)
                s_ref[here, t * C : (t + 1) * C] = slope.astype(BF)
            w = w_ref[:, 4 * part :, :].reshape(FF, C)
            y = r_ref[here, :] + mm(g_ref[here, :], w) + small_ref[V_ROW + 6 : V_ROW + 7]
            x_ref[here, :] = y * wide(mask_ref[here, :])

    high = shape((rows, FF), BF)
    outs = [shape((rows, C), F32), shape((rows, C), BF), high, high]
    return call(kernel, outs, (r, mask, small, weights))


def ffn_backward(sizes, dy, r, n2, g, slope, mask, small, weights):
    globals_, locals_, shards = sizes
    windows = 4 * globals_ + locals_
    rows = windows * CELL
    chunk = rows // 3
    part = C // shards
    deep = FF // shards

    def kernel(dy_ref, r_ref, n_ref, g_ref, s_ref, mask_ref, small_ref, w_ref, dr_ref, dw_ref, ds_ref, dyl, dh, acc, acc1):
        acc[...] = jnp.zeros_like(acc)
        acc1[...] = jnp.zeros_like(acc1)

        @pl.loop(0, windows)
        def _(w):
            here = pl.ds(w * CELL, CELL)
            d = dy_ref[here, :] * wide(mask_ref[here, :])
            dyl[here, :] = d.astype(BF)
            acc[2] += fold8(d)

        @pl.loop(0, 3)
        def _(i):
            here = pl.ds(i * chunk, chunk)
            for t in range(FF // C):
                cols = slice(t * C, (t + 1) * C)
                w2 = w_ref[t * C // deep : (t + 1) * C // deep, 4 * part :, :].reshape(C, C)
                d = mm_nt(dyl[here, :], w2) * s_ref[here, cols].astype(F32)
                acc1[:, cols] += fold8(d)
                dh[here, cols] = d.astype(BF)
            dn = None
            for t in range(FF // C):
                w1 = w_ref[:, t * part : (t + 1) * part, :].reshape(C, C)
                one = mm_nt(dh[here, t * C : (t + 1) * C], w1)
                dn = one if dn is None else dn + one
            dr_ref[here, :] = dn

        gain = small_ref[G_ROW + 1 : G_ROW + 2]

        @pl.loop(0, windows)
        def _(w):
            here = pl.ds(w * CELL, CELL)
            dn = dr_ref[here, :]
            xhat, rstd = norm_parts(r_ref[here, :])
            acc[0] += fold8(dn * xhat)
            acc[1] += fold8(dn)
            dr_ref[here, :] = norm_back(dn, xhat, rstd, gain) + dy_ref[here, :] * wide(mask_ref[here, :])

        for t in range(FF // C):
            cols = slice(t * C, (t + 1) * C)
            dw_ref[:, t * part : (t + 1) * part, :] = (
                mm_tn(n_ref[...], dh[:, cols]).astype(BF).reshape(shards, part, C)
            )
            dw_ref[t * C // deep : (t + 1) * C // deep, 4 * part :, :] = (
                mm_tn(g_ref[:, cols], dyl[...]).astype(BF).reshape(C // deep, deep, C)
            )
        for i in range(3):
            ds_ref[i : i + 1, :] = jnp.sum(acc[i], axis=0, keepdims=True)
        for t in range(FF // C):
            ds_ref[3 + t : 4 + t, :] = jnp.sum(acc1[:, t * C : (t + 1) * C], axis=0, keepdims=True)
        ds_ref[7:8, :] = jnp.zeros((1, C), F32)

    outs = [shape((rows, C), F32), shape((shards, 4 * part + deep, C), BF), shape((8, C), F32)]
    scratch = [
        pltpu.VMEM((rows, C), BF),
        pltpu.VMEM((rows, FF), BF),
        pltpu.VMEM((3, 8, C), F32),
        pltpu.VMEM((8, FF), F32),
    ]
    return call(kernel, outs, (dy, r, n2, g, slope, mask, small, weights), scratch)


def attention_backward(sizes, kind, dr, u, c, n1, q, k, v, o, p, mask, small, weights):
    globals_, locals_, shards = sizes
    windows = 4 * globals_ + locals_
    rows = windows * CELL
    chunk = rows // 3
    part = C // shards

    def kernel(
        dr_ref, u_ref, c_ref, n_ref, q_ref, k_ref, v_ref, o_ref, p_ref, mask_ref, small_ref, w_ref,
        du_ref, dw_ref, ds_ref, drl, do, dq, dk, dv, dn, acc, acck,
    ):
        acc[...] = jnp.zeros_like(acc)

        def weight(i):
            return w_ref[:, i * part : (i + 1) * part, :].reshape(C, C)

        @pl.loop(0, windows)
        def _(w):
            here = pl.ds(w * CELL, CELL)
            d = dr_ref[here, :]
            drl[here, :] = d.astype(BF)
            acc[4] += fold8(d)

        @pl.loop(0, 3)
        def _(i):
            here = pl.ds(i * chunk, chunk)
            do[here, :] = mm_nt(drl[here, :], weight(3)).astype(BF)

        if kind == 0:
            spatial_backward(q_ref, k_ref, v_ref, p_ref, do, dq, dk, dv, acc, windows)
        else:
            channel_backward(
                q_ref, k_ref, v_ref, mask_ref, p_ref, do, dq, dk, dv, acc, globals_, locals_
            )

        @pl.loop(0, 3)
        def _(i):
            here = pl.ds(i * chunk, chunk)
            total = mm_nt(dq[here, :], weight(0)) + mm_nt(dk[here, :], weight(1)) + mm_nt(dv[here, :], weight(2))
            dn[pl.ds(i * (chunk // 8), chunk // 8)] = total.reshape(chunk // 8, 8, C)

        gain = small_ref[G_ROW : G_ROW + 1]

        @pl.loop(0, windows)
        def _(w):
            here = pl.ds(w * CELL, CELL)
            tiles = pl.ds(w * 8, 8)
            d = dn[tiles].reshape(CELL, C)
            xhat, rstd = norm_parts(c_ref[tiles].reshape(CELL, C))
            acc[2] += fold8(d * xhat)
            acc[3] += fold8(d)
            dc = norm_back(d, xhat, rstd, gain) + dr_ref[here, :]
            dn[tiles] = (dc * wide(mask_ref[here, :])).reshape(8, 8, C)

        conv_backward(dn, u_ref, du_ref, small_ref, acck, globals_, locals_)

        for i, (left, right) in enumerate(((n_ref, dq), (n_ref, dk), (n_ref, dv), (o_ref, drl))):
            dw_ref[:, i * part : (i + 1) * part, :] = (
                mm_tn(left[...], right[...]).astype(BF).reshape(shards, part, C)
            )
        for t in range(10):
            ds_ref[t : t + 1, :] = jnp.sum(acck[t], axis=0, keepdims=True)
        for t in range(5):
            ds_ref[10 + t : 11 + t, :] = jnp.sum(acc[t], axis=0, keepdims=True)
        ds_ref[15:16, :] = jnp.zeros((1, C), F32)

    outs = [shape((windows * 8, 8, C), F32), shape((shards, 4 * part, C), BF), shape((16, C), F32)]
    low = pltpu.VMEM((rows, C), BF)
    scratch = [
        low, low, low, low, low,
        pltpu.VMEM((windows * 8, 8, C), F32),
        pltpu.VMEM((5, 8, C), F32),
        pltpu.VMEM((10, 8, C), F32),
    ]
    return call(kernel, outs, (dr, u, c, n1, q, k, v, o, p, mask, small, weights), scratch)


def to_cells(glob, loc):
    count = glob.shape[0]
    wins = glob.reshape(count, 2, WIN, 2, WIN, C).transpose(0, 1, 3, 2, 4, 5).reshape(count * 4, WIN, WIN, C)
    both = jnp.concatenate([wins, loc], axis=0)
    return jnp.pad(both, ((0, 0), (0, 1), (0, 1), (0, 0))).astype(F32)


def from_cells(cells, globals_):
    cells = cells.reshape(-1, 8, 8, C)[:, :WIN, :WIN]
    wins = cells[: globals_ * 4].reshape(globals_, 2, 2, WIN, WIN, C)
    return wins.transpose(0, 1, 3, 2, 4, 5).reshape(globals_, SIDE, SIDE, C), cells[globals_ * 4 :]


def cell_mask(extent, globals_):
    places = jnp.arange(8, dtype=jnp.int32)
    size = jnp.concatenate([jnp.full((globals_ * 4, 2), WIN, jnp.int32), extent.astype(jnp.int32)], axis=0)
    rows = places[None, :, None] < size[:, 0][:, None, None]
    cols = places[None, None, :] < size[:, 1][:, None, None]
    return jnp.logical_and(rows, cols).astype(F32)


def layer(sizes, tokens, cotangent, mask4, small, w_att, w_ffn):
    windows = 4 * sizes[0] + sizes[1]
    rows = windows * CELL
    mask = jnp.broadcast_to(mask4.reshape(rows, 1), (rows, LANES))
    u = (tokens * mask4[..., None]).reshape(windows * 8, 8, C)
    dy = cotangent.reshape(rows, C)
    kept = []
    for b in range(2):
        r, *att = attention_forward(sizes, b, u, mask, small[b], w_att[b])
        x, *ffn = ffn_forward(sizes, r, mask, small[b], w_ffn[b])
        kept.append((u, r, att, ffn))
        u = x.reshape(windows * 8, 8, C)
    out = u
    grads = []
    for b in (1, 0):
        u, r, att, ffn = kept[b]
        dr, dw_ffn, ds_ffn = ffn_backward(sizes, dy, r, *ffn, mask, small[b], w_ffn[b])
        du, dw_att, ds_att = attention_backward(sizes, b, dr, u, *att, mask, small[b], w_att[b])
        dy = du.reshape(rows, C)
        table = jnp.concatenate(
            [ds_att[0:10], ds_att[13:14], ds_att[10:12], ds_att[14:15], ds_ffn[1:3], ds_att[12:13], ds_ffn[0:1], ds_ffn[3:7]]
        )
        grads.append((dw_att, dw_ffn, table))
    return out, du * mask4.reshape(windows * 8, 8, 1), grads[::-1]


def body(
    global_tokens,
    local_tokens,
    crop_extent,
    conv_weight,
    vectors,
    gains,
    qkv_weight,
    proj_weight,
    fc1_weight,
    fc1_bias,
    fc2_weight,
    global_cotangent,
    local_cotangent,
):
    shards = lax.axis_size("fsdp")
    part = C // shards
    globals_, locals_ = global_tokens.shape[0], local_tokens.shape[0]
    sizes = (globals_, locals_, shards)

    own_small = jnp.concatenate([conv_weight, vectors, gains], axis=1)
    small = lax.all_gather(own_small, "fsdp", axis=2, tiled=True)
    bias = lax.all_gather(fc1_bias, "fsdp", axis=1, tiled=True).reshape(2, FF // C, C)
    small = jnp.concatenate([small, bias], axis=1).astype(F32)
    small = jnp.pad(small, ((0, 0), (0, 2), (0, 0)))
    w_att, w_ffn = [], []
    for b in range(2):
        cols = lambda w, n: [w[b][:, i * C : (i + 1) * C] for i in range(n)]
        packed = jnp.concatenate(
            cols(qkv_weight, 3) + [proj_weight[b]] + cols(fc1_weight, 4) + [fc2_weight[b]], axis=0
        )
        whole = lax.all_gather(packed, "fsdp", axis=0)
        w_att.append(whole[:, : 4 * part])
        w_ffn.append(whole[:, 4 * part :])

    mask4 = cell_mask(crop_extent, globals_)
    out, grad, grads = layer(
        sizes,
        to_cells(global_tokens, local_tokens),
        to_cells(global_cotangent, local_cotangent),
        mask4, small, w_att, w_ffn,
    )
    out = from_cells(out.astype(BF), globals_)
    grad = from_cells(grad, globals_)
    final = []
    for b in range(2):
        dw_att, dw_ffn, _ = grads[b]
        both = jnp.concatenate([dw_att, dw_ffn], axis=1)
        own = lax.psum_scatter(both, "fsdp", scatter_dimension=0, tiled=True)[0]
        final.append(lax.psum(own, "dp").astype(F32))
    table = jnp.stack([grads[0][2], grads[1][2]]).astype(BF)
    main = lax.psum_scatter(table[:, :18], "fsdp", scatter_dimension=2, tiled=True)
    bias = lax.psum_scatter(table[:, 18:].reshape(2, FF), "fsdp", scatter_dimension=1, tiled=True)
    main = lax.psum(main, "dp").astype(F32)
    bias = lax.psum(bias, "dp").astype(F32)

    def cut(start, n, width):
        rows = width
        return jnp.stack(
            [jnp.concatenate([w[(start + i) * rows : (start + i + 1) * rows] for i in range(n)], axis=1) for w in final]
        )

    fc2 = jnp.stack([w[8 * part :] for w in final])
    return (
        out[0], out[1], grad[0], grad[1],
        main[:, 0:9], main[:, 9:16], main[:, 16:18],
        cut(0, 3, part), cut(3, 1, part), cut(4, 4, part), bias, fc2,
    )


def solution(mesh):
    crops = P(("dp", "fsdp"), None, None, None)
    last = P(None, None, "fsdp")
    middle = P(None, "fsdp", None)
    return jax.shard_map(
        body,
        mesh=mesh,
        in_specs=(
            crops, crops, P(("dp", "fsdp"), None), last, last, last, middle, middle, middle,
            P(None, "fsdp"), middle, crops, crops,
        ),
        out_specs=(
            crops, crops, crops, crops, last, last, last, middle, middle, middle, P(None, "fsdp"), middle,
        ),
        check_vma=False,
    )
```

```python
import functools

import jax
import jax.numpy as jnp
from jax import lax
from jax.experimental import pallas as pl
from jax.experimental.pallas import tpu as pltpu
from jax.sharding import PartitionSpec as P

BF = jnp.bfloat16
F32 = jnp.float32
C = 512
FF = 2048
HEAD = 32
WIN = 7
SIDE = 14
CELL = 64
LANES = 128
GROUPS = C // LANES
PER = LANES // HEAD
EPS = 1e-5
SCALE = HEAD ** -0.5
MIX_UNROLL = 7
NORM_UNROLL = 7
VMEM = pl.BlockSpec(memory_space=pltpu.VMEM)
HELD = pl.BlockSpec(memory_space=pl.ANY)
NT = (((1,), (1,)), ((), ()))
TN = (((0,), (0,)), ((), ()))
K_ROW, V_ROW, G_ROW, B_ROW, TAB = 0, 9, 16, 18, 32


def mm(a, b):
    return jnp.dot(a, b, preferred_element_type=F32)


def mm_nt(a, b):
    return lax.dot_general(a, b, NT, preferred_element_type=F32)


def mm_tn(a, b):
    return lax.dot_general(a, b, TN, preferred_element_type=F32)


class Copy:
    def __init__(self, src, dst, sems, ref):
        self.src, self.dst, self.sems, self.ref = src, dst, sems, ref
        self.open = {}

    def start(self, k=0, part=None):
        src, dst = (self.src, self.dst) if part is None else (self.src.at[part], self.dst.at[part])
        self.open[k] = pltpu.make_async_copy(src, dst, self.sems.at[k])
        self.open[k].start()

    def wait(self, k=0):
        self.open.pop(k).wait()
        return self.ref

    def wait_all(self):
        for k in list(self.open):
            self.wait(k)


PARTS = 4


def call(kernel, me, ins, outs, held=(), packs=(), scratch=(), flops=0, limit=62):
    n_in, n_out, n_held, n_pack = len(ins), len(outs), len(held), len(packs)

    def body(me_ref, *refs):
        src, refs = refs[:n_in], refs[n_in:]
        held_refs, refs = refs[:n_held], refs[n_held:]
        dst, refs = refs[:n_out], refs[n_out:]
        pack_refs, refs = refs[:n_pack], refs[n_pack:]
        in_vmem, refs = refs[:n_in], refs[n_in:]
        out_vmem, refs = refs[:n_out], refs[n_out:]
        in_sem, out_sem, refs = refs[0], refs[1], refs[2:]
        feeds = [Copy(s, v, in_sem.at[i], v) for i, (s, v) in enumerate(zip(src, in_vmem))]
        sends = [Copy(v, d, out_sem.at[i], v) for i, (d, v) in enumerate(zip(dst, out_vmem))]
        kernel(me_ref, feeds, sends, held_refs, pack_refs, *refs)
        for send in sends:
            send.wait_all()

    vmem = lambda v: pltpu.VMEM(v.shape, v.dtype)
    return pl.pallas_call(
        body,
        out_shape=list(outs) + list(packs),
        in_specs=[pl.BlockSpec(memory_space=pltpu.SMEM)] + [HELD] * (n_in + n_held),
        out_specs=[HELD] * (n_out + n_pack),
        scratch_shapes=[vmem(v) for v in ins]
        + [vmem(v) for v in outs]
        + [pltpu.SemaphoreType.DMA((max(n_in, 1), PARTS)), pltpu.SemaphoreType.DMA((max(n_out, 1), PARTS))]
        + list(scratch),
        compiler_params=pltpu.CompilerParams(vmem_limit_bytes=limit * 2**20),
        cost_estimate=pl.CostEstimate(flops=flops, bytes_accessed=20 * 2**20, transcendentals=0),
    )(me, *ins, *held)


def start_weights(bufs, me_ref, plan, sem):
    copies = []
    if len(bufs) == 1:
        sources = [(d, bufs[0].at[d]) for d in range(bufs[0].shape[0])]
    else:
        sources = [(me_ref[0] ^ k, buf) for k, buf in enumerate(bufs)]
    for d, src in sources:
        for first, rows, place in plan:
            copies.append(pltpu.make_async_copy(src.at[pl.ds(first, rows), :], place(d), sem))
    for copy in copies:
        copy.start()
    return copies


def rows_of(ref, i, rows):
    return lambda d: ref.at[i, pl.ds(pl.multiple_of(d * rows, rows), rows), :]


def slot_of(d, me_ref, relative):
    if not relative:
        return d
    turn = me_ref[0] ^ d
    return (turn & 1) * 4 + (turn >> 1)


def shape(dims, kind):
    return jax.ShapeDtypeStruct(dims, kind)


def wide(m):
    return jnp.concatenate([m] * GROUPS, axis=1)


def fold8(v):
    return jnp.sum(v.reshape(v.shape[0] // 8, 8, v.shape[1]), axis=0)


def norm_parts(x):
    center = jnp.sum(x, axis=-1, keepdims=True) * (1.0 / C)
    xc = x - center
    var = jnp.sum(xc * xc, axis=-1, keepdims=True) * (1.0 / C)
    rstd = lax.rsqrt(var + EPS)
    return xc * rstd, rstd


def norm_back(dn, xhat, rstd, gain):
    gp = dn * gain
    m1 = jnp.sum(gp, axis=-1, keepdims=True) * (1.0 / C)
    m2 = jnp.sum(gp * xhat, axis=-1, keepdims=True) * (1.0 / C)
    return rstd * (gp - m1 - xhat * m2)


def several(count, at_once, step):
    while count % at_once:
        at_once -= 1

    @pl.loop(0, count // at_once)
    def _(i):
        for j in range(at_once):
            step(i * at_once + j)


def head_masks(rows):
    lane = lax.broadcasted_iota(jnp.int32, (rows, LANES), 1) // HEAD
    return [lane == h for h in range(PER)]


def spread(v, masks):
    zero = jnp.zeros_like(v)
    return jnp.concatenate([jnp.where(m, v, zero) for m in masks], axis=0)


def gather_heads(full, masks):
    n = full.shape[0] // PER
    out = full[3 * n :]
    for h in (2, 1, 0):
        out = jnp.where(masks[h], full[h * n : (h + 1) * n], out)
    return out


def shifted_cols(left, right, j, step):
    if step == 0:
        return left, right
    if step == 1:
        return (
            jnp.where(j == 6, pltpu.roll(right, 6, 1), pltpu.roll(left, 7, 1)),
            pltpu.roll(right, 7, 1),
        )
    return (
        pltpu.roll(left, 1, 1),
        jnp.where(j == 0, pltpu.roll(left, 2, 1), pltpu.roll(right, 1, 1)),
    )


def canvas(ref, crop, lanes):
    base = crop * 32
    parts = [ref[pl.ds(base + 8 * w, 7), :, lanes] for w in range(4)]
    left = jnp.concatenate([parts[0], parts[2]], axis=0)
    right = jnp.concatenate([parts[1], parts[3]], axis=0)
    return left, right


def put_canvas(ref, crop, lanes, left, right, mask_ref):
    base = crop * 32
    zero = jnp.zeros((1, 8, LANES), F32)
    for w in range(4):
        side = right if w % 2 else left
        half = side[(w // 2) * 7 : (w // 2) * 7 + 7]
        rows = pl.ds(base + 8 * w, 8)
        ref[rows, :, lanes] = jnp.concatenate([half, zero], axis=0) * mask_ref[rows]


def conv_forward(u_ref, c_ref, small_ref, mask_ref, globals_, locals_):
    j14 = lax.broadcasted_iota(jnp.int32, (14, 8, LANES), 1)
    for g in range(GROUPS):
        lanes = pl.ds(g * LANES, LANES)
        taps = [small_ref[K_ROW + t : K_ROW + t + 1, lanes][None] for t in range(9)]
        shift = small_ref[V_ROW : V_ROW + 1, lanes][None]

        @pl.loop(0, globals_)
        def _(crop):
            left, right = canvas(u_ref, crop, lanes)
            zero = jnp.zeros((1, 8, LANES), F32)
            acc = [left + shift, right + shift]
            for e in (-1, 0, 1):
                for s, side in enumerate(shifted_cols(left, right, j14, e)):
                    tall = jnp.concatenate([zero, side, zero], axis=0)
                    for a in (-1, 0, 1):
                        acc[s] = acc[s] + taps[3 * (a + 1) + e + 1] * tall[1 + a : 15 + a]
            put_canvas(c_ref, crop, lanes, acc[0], acc[1], mask_ref)

        @pl.loop(0, locals_)
        def _(n):
            rows = pl.ds(globals_ * 32 + n * 8, 8)
            u = u_ref[rows, :, lanes]
            acc = u + shift
            for e in (-1, 0, 1):
                side = u if e == 0 else pltpu.roll(u, 7 if e == 1 else 1, 1)
                for a in (-1, 0, 1):
                    moved = side if a == 0 else jnp.roll(side, -a, axis=0)
                    acc = acc + taps[3 * (a + 1) + e + 1] * moved
            c_ref[rows, :, lanes] = acc * mask_ref[rows]


def conv_backward(d_ref, u_ref, du_ref, small_ref, acc_ref, globals_, locals_):
    j14 = lax.broadcasted_iota(jnp.int32, (14, 8, LANES), 1)
    for g in range(GROUPS):
        lanes = pl.ds(g * LANES, LANES)
        taps = [small_ref[K_ROW + t : K_ROW + t + 1, lanes][None] for t in range(9)]
        nothing = tuple(jnp.zeros((8, LANES), F32) for _ in range(10))

        def one_crop(crop, sums):
            sums = list(sums)
            left, right = canvas(d_ref, crop, lanes)
            own = canvas(u_ref, crop, lanes)
            zero = jnp.zeros((1, 8, LANES), F32)
            acc = [left, right]
            sums[9] = sums[9] + jnp.sum(left + right, axis=0)
            for e in (-1, 0, 1):
                for s, side in enumerate(shifted_cols(left, right, j14, -e)):
                    tall = jnp.concatenate([zero, side, zero], axis=0)
                    for a in (-1, 0, 1):
                        t = 3 * (a + 1) + e + 1
                        moved = tall[1 - a : 15 - a]
                        acc[s] = acc[s] + taps[t] * moved
                        sums[t] = sums[t] + jnp.sum(own[s] * moved, axis=0)
            base = crop * 32
            for w in range(4):
                side = acc[w % 2]
                half = side[(w // 2) * 7 : (w // 2) * 7 + 7]
                du_ref[pl.ds(base + 8 * w, 8), :, lanes] = jnp.concatenate([half, zero], axis=0)
            return tuple(sums)

        def one_local(n, sums):
            sums = list(sums)
            rows = pl.ds(globals_ * 32 + n * 8, 8)
            d = d_ref[rows, :, lanes]
            own = u_ref[rows, :, lanes]
            acc = d
            sums[9] = sums[9] + jnp.sum(d, axis=0)
            for e in (-1, 0, 1):
                side = d if e == 0 else pltpu.roll(d, 7 if e == -1 else 1, 1)
                for a in (-1, 0, 1):
                    t = 3 * (a + 1) + e + 1
                    moved = side if a == 0 else jnp.roll(side, a, axis=0)
                    acc = acc + taps[t] * moved
                    sums[t] = sums[t] + jnp.sum(own * moved, axis=0)
            du_ref[rows, :, lanes] = acc
            return tuple(sums)

        sums = lax.fori_loop(0, globals_, one_crop, nothing)
        sums = lax.fori_loop(0, locals_, one_local, sums)
        for t in range(10):
            acc_ref[t, :, lanes] = sums[t]


def spatial_forward(q_ref, k_ref, v_ref, mask_ref, o_ref, p_ref, windows):
    masks = head_masks(CELL)

    def step(w):
        rows = pl.ds(w * CELL, CELL)
        m = mask_ref[rows, :]
        valid = jnp.concatenate([m, m], axis=1) > 0.5
        for g in range(GROUPS):
            lanes = pl.ds(g * LANES, LANES)
            s = mm_nt(k_ref[rows, lanes], spread(q_ref[rows, lanes], masks))
            s = jnp.where(valid, s * SCALE, -1e9)
            e = jnp.exp(s - jnp.max(s, axis=0, keepdims=True))
            p = (e / jnp.sum(e, axis=0, keepdims=True)).astype(BF)
            p_ref[w, g] = p
            o_ref[rows, lanes] = gather_heads(mm_tn(p, v_ref[rows, lanes]), masks).astype(BF)

    several(windows, MIX_UNROLL, step)


def plus(a, b):
    return b if a is None else a + b


def pick(count, at_once):
    while count % at_once:
        at_once -= 1
    return at_once


def spatial_backward(q_ref, k_ref, v_ref, p_ref, do_ref, dq_ref, dk_ref, dv_ref, acc_ref, s_ref, windows, wait, send):
    masks = head_masks(CELL)
    lanes = [pl.ds(g * LANES, LANES) for g in range(GROUPS)]
    at_once = pick(windows, MIX_UNROLL)
    for ready in wait:
        ready()

    @pl.loop(0, windows // at_once)
    def _(i):
        sums = [None] * GROUPS
        for w in [i * at_once + j for j in range(at_once)]:
            rows = pl.ds(w * CELL, CELL)
            for g in range(GROUPS):
                p = p_ref[w, g]
                dos = spread(do_ref[rows, lanes[g]], masks)
                dp = mm_nt(v_ref[rows, lanes[g]], dos)
                pf = p.astype(F32)
                total = jnp.sum(pf * dp, axis=0, keepdims=True)
                ds = (pf * (dp - total) * SCALE).astype(BF)
                s_ref[w, g] = ds
                dv = mm(p, dos)
                sums[g] = plus(sums[g], fold8(dv))
                dv_ref[rows, lanes[g]] = dv.astype(BF)
                dk_ref[rows, lanes[g]] = mm(ds, spread(q_ref[rows, lanes[g]], masks)).astype(BF)
        for g in range(GROUPS):
            acc_ref[1, :, lanes[g]] += sums[g]

    send[1]()
    send[2]()

    @pl.loop(0, windows // at_once)
    def _(i):
        sums = [None] * GROUPS
        for w in [i * at_once + j for j in range(at_once)]:
            rows = pl.ds(w * CELL, CELL)
            for g in range(GROUPS):
                dq = gather_heads(mm_tn(s_ref[w, g], k_ref[rows, lanes[g]]), masks)
                sums[g] = plus(sums[g], fold8(dq))
                dq_ref[rows, lanes[g]] = dq.astype(BF)
        for g in range(GROUPS):
            acc_ref[0, :, lanes[g]] += sums[g]

    send[0]()


def same_head():
    a = lax.broadcasted_iota(jnp.int32, (LANES, LANES), 0) // HEAD
    b = lax.broadcasted_iota(jnp.int32, (LANES, LANES), 1) // HEAD
    return a == b


def over_crops(globals_, locals_, step):
    several(globals_, 3, lambda n: step(n, n * 4 * CELL, 4 * CELL))
    several(locals_, 9, lambda n: step(globals_ + n, globals_ * 4 * CELL + n * CELL, CELL))


def channel_forward(q_ref, k_ref, v_ref, mask_ref, o_ref, p_ref, globals_, locals_):
    same = same_head()
    lanes = [pl.ds(g * LANES, LANES) for g in range(GROUPS)]

    def weigh(n, start, count):
        rows = pl.ds(start, count)
        m = mask_ref[rows, :].astype(BF)
        for g in range(GROUPS):
            s = mm_tn(v_ref[rows, lanes[g]], k_ref[rows, lanes[g]] * m)
            s = jnp.where(same, s * SCALE, -jnp.inf)
            e = jnp.exp(s - jnp.max(s, axis=0, keepdims=True))
            p_ref[n, g] = (e / jnp.sum(e, axis=0, keepdims=True)).astype(BF)

    over_crops(globals_, locals_, weigh)

    def step(n, start, count):
        rows = pl.ds(start, count)
        for g in range(GROUPS):
            o_ref[rows, lanes[g]] = mm(q_ref[rows, lanes[g]], p_ref[n, g]).astype(BF)

    over_crops(globals_, locals_, step)


def channel_backward(
    q_ref, k_ref, v_ref, mask_ref, p_ref, do_ref, dq_ref, dk_ref, dv_ref, acc_ref, s_ref, globals_, locals_, wait, send
):
    lanes = [pl.ds(g * LANES, LANES) for g in range(GROUPS)]

    def slope(n, start, count):
        rows = pl.ds(start, count)
        for g in range(GROUPS):
            dp = mm_tn(q_ref[rows, lanes[g]], do_ref[rows, lanes[g]])
            pf = p_ref[n, g].astype(F32)
            total = jnp.sum(pf * dp, axis=0, keepdims=True)
            s_ref[n, g] = (pf * (dp - total) * SCALE).astype(BF)

    for ready in wait[:3]:
        ready()
    over_crops(globals_, locals_, slope)
    for ready in wait[3:]:
        ready()

    def step(n, start, count):
        rows = pl.ds(start, count)
        mf = mask_ref[rows, :]
        m = mf.astype(BF)
        for g in range(GROUPS):
            ds = s_ref[n, g]
            dq = mm_nt(do_ref[rows, lanes[g]], p_ref[n, g])
            dk = mm(v_ref[rows, lanes[g]], ds) * mf
            dv = mm_nt(k_ref[rows, lanes[g]] * m, ds)
            acc_ref[0, :, lanes[g]] += fold8(dq)
            acc_ref[1, :, lanes[g]] += fold8(dv)
            dq_ref[rows, lanes[g]] = dq.astype(BF)
            dk_ref[rows, lanes[g]] = dk.astype(BF)
            dv_ref[rows, lanes[g]] = dv.astype(BF)

    over_crops(globals_, locals_, step)
    for go in send:
        go()


def table_of(tabs):
    total = tabs[0].astype(F32)
    for d in range(1, tabs.shape[0]):
        total = total + tabs[d].astype(F32)
    return total


CHUNKS = 3


def chunks_of(rows):
    size = rows // CHUNKS
    return [pl.ds(i * size, size) for i in range(CHUNKS)]


def tiles_of(here):
    return pl.ds(here.start // 8, here.size // 8)


def attention_forward(sizes, kind, me, u, mask, bufs, first):
    globals_, locals_, shards = sizes
    windows = 4 * globals_ + locals_
    rows = windows * CELL
    part = C // shards
    chunks = chunks_of(rows)

    def kernel(me_ref, feeds, sends, held, packs, w, tabs, sem, sem2):
        u_in, m_in = feeds
        r_out, small_out, c_out, n_out, q_out, k_out, v_out, o_out, p_out = sends
        r_ref, small_ref, c_ref, n_ref, q_ref, k_ref, v_ref, o_ref, p_ref = [v.ref for v in sends]
        u_in.start()
        tab = start_weights(held, me_ref, [(first + 4 * part, TAB, lambda d: tabs.at[d])], sem2)
        m_in.start()
        plan = [(first + i * part, part, rows_of(w, i, part)) for i in range(4)]
        copies = start_weights(held, me_ref, plan, sem)
        for copy in tab:
            copy.wait()
        small_ref[...] = table_of(tabs)
        small_out.start()
        u_ref = u_in.wait()
        mask_ref = m_in.wait()
        conv_forward(u_ref, c_ref, small_ref, mask_ref.reshape(windows * 8, 8, LANES), globals_, locals_)
        c_out.start()
        gain = small_ref[G_ROW : G_ROW + 1]
        shift = small_ref[V_ROW + 1 : V_ROW + 2]

        def step(i):
            x = c_ref[pl.ds(i * 8, 8)].reshape(CELL, C)
            xhat, _ = norm_parts(x)
            n_ref[pl.ds(i * CELL, CELL), :] = (xhat * gain + shift).astype(BF)

        several(windows, NORM_UNROLL, step)
        n_out.start()
        for copy in copies:
            copy.wait()
        for here in chunks:
            n1 = n_ref[here, :]
            q_ref[here, :] = (mm(n1, w[0]) + small_ref[V_ROW + 2 : V_ROW + 3]).astype(BF)
            k_ref[here, :] = mm(n1, w[1]).astype(BF)
            v_ref[here, :] = (mm(n1, w[2]) + small_ref[V_ROW + 3 : V_ROW + 4]).astype(BF)
        for send in (q_out, k_out, v_out):
            send.start()
        if kind == 0:
            spatial_forward(q_ref, k_ref, v_ref, mask_ref, o_ref, p_ref, windows)
        else:
            channel_forward(q_ref, k_ref, v_ref, mask_ref, o_ref, p_ref, globals_, locals_)
        p_out.start()
        o_out.start()
        for i, here in enumerate(chunks):
            c = c_ref[tiles_of(here)].reshape(here.size, C)
            r_ref[here, :] = c + mm(o_ref[here, :], w[3]) + small_ref[V_ROW + 4 : V_ROW + 5]
            r_out.start(i, here)

    low = shape((rows, C), BF)
    probs = (windows, GROUPS, CELL, PER * CELL) if kind == 0 else (globals_ + locals_, GROUPS, LANES, LANES)
    outs = [
        shape((rows, C), F32), shape((TAB, C), F32), shape((windows * 8, 8, C), F32),
        low, low, low, low, low, shape(probs, BF),
    ]
    scratch = [
        pltpu.VMEM((4, C, C), BF),
        pltpu.VMEM((shards, TAB, C), BF),
        pltpu.SemaphoreType.DMA,
        pltpu.SemaphoreType.DMA,
    ]
    return call(kernel, me, [u, mask], outs, held=bufs, scratch=scratch, flops=12 * rows * C * C)


def ffn_plan(part, deep, w1, w2):
    plan = [(i * part, part, rows_of(w1, i, part)) for i in range(FF // C)]
    return plan + [((FF // C) * part, deep, lambda d: w2.at[pl.ds(pl.multiple_of(d * deep, deep), deep), :])]


def ffn_forward(sizes, me, r, mask, small, bufs):
    globals_, locals_, shards = sizes
    windows = 4 * globals_ + locals_
    rows = windows * CELL
    part = C // shards
    deep = FF // shards
    chunks = chunks_of(rows)

    def kernel(me_ref, feeds, sends, held, packs, w1, w2, sem):
        r_in, m_in, small_in = feeds
        x_out, n_out, g_out, s_out = sends
        x_ref, n_ref, g_ref, s_ref = [v.ref for v in sends]
        small_in.start()
        r_in.start()
        copies = start_weights(held, me_ref, ffn_plan(part, deep, w1, w2), sem)
        m_in.start()
        small_ref = small_in.wait()
        gain = small_ref[G_ROW + 1 : G_ROW + 2]
        shift = small_ref[V_ROW + 5 : V_ROW + 6]
        r_ref = r_in.wait()

        def step(i):
            here = pl.ds(i * CELL, CELL)
            xhat, _ = norm_parts(r_ref[here, :])
            n_ref[here, :] = (xhat * gain + shift).astype(BF)

        several(windows, NORM_UNROLL, step)
        n_out.start()
        mask_ref = m_in.wait()
        for copy in copies:
            copy.wait()
        for i, here in enumerate(chunks):
            n2 = n_ref[here, :]
            for t in range(FF // C):
                h = mm(n2, w1[t]) + small_ref[B_ROW + t : B_ROW + t + 1]
                h2 = h * h
                a = 0.5 + 0.5 * jnp.tanh(h * (0.7978845608 + (0.7978845608 * 0.044715) * h2))
                g = h * a
                slope = a + (2.0 * g) * (1.0 - a) * (0.7978845608 + (3 * 0.7978845608 * 0.044715) * h2)
                g_ref[here, t * C : (t + 1) * C] = g.astype(BF)
                s_ref[here, t * C : (t + 1) * C] = slope.astype(BF)
            g_out.start(i, here)
            s_out.start(i, here)
            y = r_ref[here, :] + mm(g_ref[here, :], w2[...]) + small_ref[V_ROW + 6 : V_ROW + 7]
            x_ref[here, :] = y * wide(mask_ref[here, :])
            x_out.start(i, here)

    high = shape((rows, FF), BF)
    outs = [shape((rows, C), F32), shape((rows, C), BF), high, high]
    scratch = [pltpu.VMEM((FF // C, C, C), BF), pltpu.VMEM((FF, C), BF), pltpu.SemaphoreType.DMA]
    return call(kernel, me, [r, mask, small], outs, held=bufs, scratch=scratch, flops=24 * rows * C * C)


def pack_outs(shards, count, relative):
    if relative:
        return [shape((4, count, C), BF)] * 2
    return [shape((shards, count, C), BF)]


def send_pack(dw, outs, rows, sem):
    each = len(outs) == 2
    copies = []
    for i, out in enumerate(outs):
        src = dw.at[pl.ds(4 * i, 4), rows] if each else dw.at[:, rows]
        copies.append(pltpu.make_async_copy(src, out.at[:, rows], sem))
    for copy in copies:
        copy.start()
    return copies


def ffn_backward(sizes, me, relative, dy, r, n2, g, slope, o, mask, small, w_ffn, w_att, first, deps):
    globals_, locals_, shards = sizes
    windows = 4 * globals_ + locals_
    rows = windows * CELL
    part = C // shards
    deep = FF // shards
    count = 4 * part + deep + part
    chunks = chunks_of(rows)
    packs = pack_outs(shards, count, relative)
    n_ffn, n_att = len(w_ffn), len(w_att)

    def kernel(me_ref, feeds, sends, held, dw_out, w1, w2, wp, dw, dyl, dh, acc, acc1, sem, sem2):
        dy_in, r_in, n_in, g_in, s_in, o_in, m_in, small_in = feeds
        dr_out, do_out, ds_out = sends
        dr_ref, do_ref, ds_ref = [v.ref for v in sends]
        dy_in.start()
        m_in.start()
        copies = start_weights(held[:n_ffn], me_ref, ffn_plan(part, deep, w1, w2), sem)
        for i, here in enumerate(chunks):
            s_in.start(i, here)
        copies += start_weights(
            held[n_ffn : n_ffn + n_att], me_ref, [(first + 3 * part, part, rows_of(wp, 0, part))], sem
        )
        small_in.start()
        acc[...] = jnp.zeros_like(acc)
        acc1[...] = jnp.zeros_like(acc1)
        dy_ref = dy_in.wait()
        mask_ref = m_in.wait()

        def step(i):
            here = pl.ds(i * CELL, CELL)
            d = dy_ref[here, :] * wide(mask_ref[here, :])
            dyl[here, :] = d.astype(BF)
            acc[2] += fold8(d)

        several(windows, NORM_UNROLL, step)
        for feed in (n_in, g_in, r_in, o_in):
            feed.start()
        for copy in copies:
            copy.wait()
        for i, here in enumerate(chunks):
            s_ref = s_in.wait(i)
            for t in range(FF // C):
                cols = slice(t * C, (t + 1) * C)
                d = mm_nt(dyl[here, :], w2[cols, :]) * s_ref[here, cols].astype(F32)
                acc1[:, cols] += fold8(d)
                dh[here, cols] = d.astype(BF)
            dn = None
            for t in range(FF // C):
                one = mm_nt(dh[here, t * C : (t + 1) * C], w1[t])
                dn = one if dn is None else dn + one
            dr_ref[here, :] = dn

        n_ref = n_in.wait()
        g_ref = g_in.wait()
        for t in range(FF // C):
            cols = slice(t * C, (t + 1) * C)
            one = mm_tn(n_ref[...], dh[:, cols]).astype(BF)
            for d in range(shards):
                dw[slot_of(d, me_ref, relative), t * part : (t + 1) * part, :] = one[d * part : (d + 1) * part]
            two = mm_tn(g_ref[:, cols], dyl[...]).astype(BF)
            for d in range(C // deep):
                here = pl.ds(4 * part, deep)
                dw[slot_of(t * (C // deep) + d, me_ref, relative), here, :] = two[d * deep : (d + 1) * deep]
        going = send_pack(dw, dw_out, pl.ds(0, 4 * part + deep), sem2)

        small_ref = small_in.wait()
        gain = small_ref[G_ROW + 1 : G_ROW + 2]
        r_ref = r_in.wait()

        def step(i):
            here = pl.ds(i * CELL, CELL)
            dn = dr_ref[here, :]
            xhat, rstd = norm_parts(r_ref[here, :])
            acc[0] += fold8(dn * xhat)
            acc[1] += fold8(dn)
            dr = norm_back(dn, xhat, rstd, gain) + dy_ref[here, :] * wide(mask_ref[here, :])
            acc[3] += fold8(dr)
            dr_ref[here, :] = dr
            dyl[here, :] = dr.astype(BF)

        several(windows, NORM_UNROLL, step)
        dr_out.start()
        for i, here in enumerate(chunks):
            do_ref[here, :] = mm_nt(dyl[here, :], wp[0]).astype(BF)
            do_out.start(i, here)
        o_ref = o_in.wait()
        one = mm_tn(o_ref[...], dyl[...]).astype(BF)
        for d in range(shards):
            dw[slot_of(d, me_ref, relative), 4 * part + deep :, :] = one[d * part : (d + 1) * part]
        going += send_pack(dw, dw_out, pl.ds(4 * part + deep, part), sem2)
        for i in range(3):
            ds_ref[i : i + 1, :] = jnp.sum(acc[i], axis=0, keepdims=True)
        for t in range(FF // C):
            ds_ref[3 + t : 4 + t, :] = jnp.sum(acc1[:, t * C : (t + 1) * C], axis=0, keepdims=True)
        ds_ref[7:8, :] = jnp.sum(acc[3], axis=0, keepdims=True)
        ds_out.start()
        for copy in going:
            copy.wait()

    outs = [shape((rows, C), F32), shape((rows, C), BF), shape((8, C), F32)]
    scratch = [
        pltpu.VMEM((FF // C, C, C), BF),
        pltpu.VMEM((FF, C), BF),
        pltpu.VMEM((1, C, C), BF),
        pltpu.VMEM((shards, count, C), BF),
        pltpu.VMEM((rows, C), BF),
        pltpu.VMEM((rows, FF), BF),
        pltpu.VMEM((4, 8, C), F32),
        pltpu.VMEM((8, FF), F32),
        pltpu.SemaphoreType.DMA,
        pltpu.SemaphoreType.DMA,
    ]
    return call(
        kernel, me, [dy, r, n2, g, slope, o, mask, small], outs, held=[*w_ffn, *w_att, *deps], packs=packs,
        scratch=scratch, flops=40 * rows * C * C,
    )


def mix_backward(sizes, kind, q, k, v, p, do, mask, me, deps):
    globals_, locals_, _ = sizes
    windows = 4 * globals_ + locals_
    rows = windows * CELL

    def kernel(me_ref, feeds, sends, held, packs, acc, slope):
        q_in, k_in, v_in, p_in, do_in, m_in = feeds
        q_ref, k_ref, v_ref, p_ref, do_ref, mask_ref = [v.ref for v in feeds]
        dq, dk, dv, ds_ref = [v.ref for v in sends]
        order = (v_in, do_in, p_in, q_in, k_in, m_in) if kind == 0 else (q_in, do_in, p_in, v_in, k_in, m_in)
        for feed in order:
            feed.start()
        acc[...] = jnp.zeros_like(acc)
        if kind == 0:
            spatial_backward(
                q_ref, k_ref, v_ref, p_ref, do_ref, dq, dk, dv, acc, slope, windows,
                [feed.wait for feed in order], [send.start for send in sends[:3]],
            )
        else:
            channel_backward(
                q_ref, k_ref, v_ref, mask_ref, p_ref, do_ref, dq, dk, dv, acc, slope, globals_, locals_,
                [feed.wait for feed in order], [send.start for send in sends[:3]],
            )
        for t in range(2):
            ds_ref[t : t + 1, :] = jnp.sum(acc[t], axis=0, keepdims=True)
        ds_ref[2:8, :] = jnp.zeros((6, C), F32)
        sends[3].start()

    low = shape((rows, C), BF)
    return call(
        kernel, me, [q, k, v, p, do, mask], [low, low, low, shape((8, C), F32)], held=deps,
        scratch=[pltpu.VMEM((2, 8, C), F32), pltpu.VMEM(p.shape, BF)], flops=16 * rows * C * C,
    )


def attention_backward(sizes, me, relative, dr, u, c, n1, dq, dk, dv, ds_ffn, ds_mix, mask, small, bufs, first, deps):
    globals_, locals_, shards = sizes
    windows = 4 * globals_ + locals_
    rows = windows * CELL
    part = C // shards
    count = 3 * part + TAB
    chunks = chunks_of(rows)
    packs = pack_outs(shards, count, relative)

    def kernel(me_ref, feeds, sends, held, dw_out, w, dw, dn, acc, acck, tab, sem, sem2):
        dr_in, u_in, c_in, n_in, dq_in, dk_in, dv_in, ffn_in, mix_in, m_in, small_in = feeds
        dr_ref, u_ref, c_ref, n_ref, dq, dk, dv, ffn_ref, mix_ref, mask_ref, small_ref = [v.ref for v in feeds]
        du_ref = sends[0].ref
        plan = [(first + i * part, part, rows_of(w, i, part)) for i in range(3)]
        copies = start_weights(held[: len(bufs)], me_ref, plan, sem)
        for i, here in enumerate(chunks):
            for feed in (dq_in, dk_in, dv_in):
                feed.start(i, here)
        for feed in (c_in, dr_in, m_in, small_in, u_in, n_in, ffn_in, mix_in):
            feed.start()
        acc[...] = jnp.zeros_like(acc)
        for copy in copies:
            copy.wait()
        for i, here in enumerate(chunks):
            for feed in (dq_in, dk_in, dv_in):
                feed.wait(i)
            total = mm_nt(dq[here, :], w[0]) + mm_nt(dk[here, :], w[1]) + mm_nt(dv[here, :], w[2])
            dn[tiles_of(here)] = total.reshape(here.size // 8, 8, C)

        for feed in (c_in, dr_in, m_in, small_in):
            feed.wait()
        gain = small_ref[G_ROW : G_ROW + 1]

        def step(i):
            here = pl.ds(i * CELL, CELL)
            tiles = pl.ds(i * 8, 8)
            d = dn[tiles].reshape(CELL, C)
            xhat, rstd = norm_parts(c_ref[tiles].reshape(CELL, C))
            acc[0] += fold8(d * xhat)
            acc[1] += fold8(d)
            dc = norm_back(d, xhat, rstd, gain) + dr_ref[here, :]
            dn[tiles] = (dc * wide(mask_ref[here, :])).reshape(8, 8, C)

        several(windows, NORM_UNROLL, step)
        u_in.wait()
        conv_backward(dn, u_ref, du_ref, small_ref, acck, globals_, locals_)
        sends[0].start()

        ffn_in.wait()
        mix_in.wait()
        rows_ = [jnp.sum(acck[t], axis=0, keepdims=True) for t in range(10)]
        rows_ += [jnp.sum(acc[1], axis=0, keepdims=True), mix_ref[0:1, :], mix_ref[1:2, :], ffn_ref[7:8, :]]
        rows_ += [ffn_ref[1:2, :], ffn_ref[2:3, :], jnp.sum(acc[0], axis=0, keepdims=True), ffn_ref[0:1, :]]
        rows_ += [ffn_ref[3 + t : 4 + t, :] for t in range(FF // C)]
        tab[...] = jnp.zeros_like(tab)
        for t, row in enumerate(rows_):
            tab[t : t + 1, :] = row
        low = tab[...].astype(BF)
        for d in range(shards):
            dw[d, 3 * part :, :] = low
        going = send_pack(dw, dw_out, pl.ds(3 * part, TAB), sem2)

        n_in.wait()
        for i, right in enumerate((dq, dk, dv)):
            one = mm_tn(n_ref[...], right[...]).astype(BF)
            for d in range(shards):
                dw[slot_of(d, me_ref, relative), i * part : (i + 1) * part, :] = one[d * part : (d + 1) * part]
            going += send_pack(dw, dw_out, pl.ds(i * part, part), sem2)
        for copy in going:
            copy.wait()

    outs = [shape((windows * 8, 8, C), F32)]
    scratch = [
        pltpu.VMEM((3, C, C), BF),
        pltpu.VMEM((shards, count, C), BF),
        pltpu.VMEM((windows * 8, 8, C), F32),
        pltpu.VMEM((2, 8, C), F32),
        pltpu.VMEM((10, 8, C), F32),
        pltpu.VMEM((TAB, C), F32),
        pltpu.SemaphoreType.DMA,
        pltpu.SemaphoreType.DMA,
    ]
    return call(
        kernel, me, [dr, u, c, n1, dq, dk, dv, ds_ffn, ds_mix, mask, small], outs, held=[*bufs, *deps],
        packs=packs, scratch=scratch, flops=20 * rows * C * C,
    )


def join(values, deps):
    values, deps = list(values), list(deps)

    def kernel(*refs):
        pass

    return pl.pallas_call(
        kernel,
        out_shape=[shape(v.shape, v.dtype) for v in values],
        in_specs=[HELD] * (len(values) + len(deps)),
        out_specs=[HELD] * len(values),
        input_output_aliases={i: i for i in range(len(values))},
    )(*values, *deps)


def to_cells(glob, loc):
    count = glob.shape[0]
    wins = glob.reshape(count, 2, WIN, 2, WIN, C).transpose(0, 1, 3, 2, 4, 5).reshape(count * 4, WIN, WIN, C)
    both = jnp.concatenate([wins, loc], axis=0)
    return jnp.pad(both, ((0, 0), (0, 1), (0, 1), (0, 0))).astype(F32)


def from_cells(cells, globals_):
    cells = cells.reshape(-1, 8, 8, C)[:, :WIN, :WIN]
    wins = cells[: globals_ * 4].reshape(globals_, 2, 2, WIN, WIN, C)
    return wins.transpose(0, 1, 3, 2, 4, 5).reshape(globals_, SIDE, SIDE, C), cells[globals_ * 4 :]


def cell_mask(extent, globals_):
    places = jnp.arange(8, dtype=jnp.int32)
    size = jnp.concatenate([jnp.full((globals_ * 4, 2), WIN, jnp.int32), extent.astype(jnp.int32)], axis=0)
    rows = places[None, :, None] < size[:, 0][:, None, None]
    cols = places[None, None, :] < size[:, 1][:, None, None]
    return jnp.logical_and(rows, cols).astype(F32)


def layer(sizes, me, tokens, cotangent, mask4, w_att, w_ffn, offsets, relative, plan):
    windows = 4 * sizes[0] + sizes[1]
    rows = windows * CELL
    mask = jnp.broadcast_to(mask4.reshape(rows, 1), (rows, LANES))
    u = (tokens * mask4[..., None]).reshape(windows * 8, 8, C)
    dy = cotangent.reshape(rows, C)
    kept = []
    for b in range(2):
        r, small, *att = attention_forward(sizes, b, me, u, mask, w_att[b], offsets[b])
        w_ffn[b] = plan.late_weights(b, w_ffn[b], r)
        x, *ffn = ffn_forward(sizes, me, r, mask, small, w_ffn[b])
        kept.append((u, r, small, att, ffn))
        u = x.reshape(windows * 8, 8, C)
    out = u
    for b in (1, 0):
        u, r, small, (c, n1, q, k, v, o, p), ffn = kept[b]
        dr, do, ds_ffn, *dw = ffn_backward(
            sizes, me, relative[b], dy, r, *ffn, o, mask, small, w_ffn[b], w_att[b], offsets[b], plan.deps(b, 0)
        )
        plan.ffn_pack(b, dw)
        dq, dk, dv, ds_mix = mix_backward(sizes, b, q, k, v, p, do, mask, me, plan.deps(b, 1))
        du, *dw = attention_backward(
            sizes, me, relative[b], dr, u, c, n1, dq, dk, dv, ds_ffn, ds_mix, mask, small, w_att[b], offsets[b],
            plan.deps(b, 2),
        )
        plan.att_pack(b, dw)
        dy = du.reshape(rows, C)
    return out, du * mask4.reshape(windows * 8, 8, 1)


def xor(v, axis, turn):
    size = lax.axis_size(axis)
    return lax.ppermute(v, axis, [(i, i ^ turn) for i in range(size)])


def gather_near(own):
    return [own, xor(own, "fsdp", 2), xor(own, "fsdp", 4), xor(own, "fsdp", 6)]


def gather_core(near):
    out = []
    for v in near:
        out += [v, xor(v, "fsdp", 1)]
    return out


def add(*terms):
    total = terms[0].astype(F32)
    for term in terms[1:]:
        total = total + term.astype(F32)
    return total.astype(BF)


class Direct:
    def __init__(self):
        self.sums = {}

    def late_weights(self, b, bufs, r):
        return gather_core(join(bufs, [r])) if b == 0 else bufs

    def core(self, pack):
        keep, send = pack
        got = xor(send, "fsdp", 1)
        return [add(keep[i], got[i]) for i in range(4)]

    def chips(self, parts):
        own, *away = parts
        return add(own, *[xor(v, "fsdp", 2 * i + 2) for i, v in enumerate(away)])

    def ffn_pack(self, b, dw):
        self.sums[b, "f"] = self.core(dw)

    def att_pack(self, b, dw):
        self.sums[b, "a"] = self.core(dw)

    def deps(self, b, stage):
        if b == 1 and stage == 2:
            return self.sums[1, "f"]
        if b == 0 and stage == 1:
            self.own_ffn = self.chips(self.sums[1, "f"])
            return [self.own_ffn] + self.sums[1, "a"]
        if b == 0 and stage == 2:
            self.own_att = self.chips(self.sums[1, "a"])
            return [self.own_att] + self.sums[0, "f"]
        return []

    def results(self):
        far = lax.psum((self.own_ffn, self.own_att), "dp")
        near = [self.chips(self.sums[0, "f"]), self.chips(self.sums[0, "a"])]
        for turn in (1, 2):
            near = [add(v, xor(v, "dp", turn)) for v in near]
        return [near, far]


class Plain:
    def __init__(self):
        self.packs = [[None, None], [None, None]]

    def late_weights(self, b, bufs, r):
        return bufs

    def ffn_pack(self, b, dw):
        self.packs[b][0] = dw[0]

    def att_pack(self, b, dw):
        self.packs[b][1] = dw[0]

    def deps(self, b, stage):
        return []

    def results(self):
        return [
            lax.psum([lax.psum_scatter(v, "fsdp", scatter_dimension=0, tiled=True)[0] for v in pair], "dp")
            for pair in self.packs
        ]


def body(
    global_tokens,
    local_tokens,
    crop_extent,
    conv_weight,
    vectors,
    gains,
    qkv_weight,
    proj_weight,
    fc1_weight,
    fc1_bias,
    fc2_weight,
    global_cotangent,
    local_cotangent,
):
    shards = lax.axis_size("fsdp")
    direct = shards == 8 and lax.axis_size("dp") == 4
    part = C // shards
    globals_, locals_ = global_tokens.shape[0], local_tokens.shape[0]
    sizes = (globals_, locals_, shards)
    index = lax.axis_index("fsdp")
    me = index.astype(jnp.int32).reshape(1)

    own_small = jnp.concatenate([conv_weight, vectors, gains], axis=1)
    own_bias = fc1_bias.reshape(2, 1, FF // shards)
    w_att, w_ffn = [], []
    for b in range(2):
        cols = lambda w, n: [w[b][:, i * C : (i + 1) * C] for i in range(n)]
        table = jnp.zeros((TAB, C), BF)
        table = lax.dynamic_update_slice(table, own_small[b], (0, index * part))
        start = index * (FF // shards)
        table = lax.dynamic_update_slice(table, own_bias[b], (B_ROW + start // C, start % C))
        att = cols(qkv_weight, 3) + [proj_weight[b], table]
        ffn = cols(fc1_weight, 4) + [fc2_weight[b]]
        if b == 0 and direct:
            w_att.append(gather_core(gather_near(jnp.concatenate(att, axis=0))))
            w_ffn.append(gather_near(jnp.concatenate(ffn, axis=0)))
        else:
            whole = lax.all_gather(jnp.concatenate(ffn + att, axis=0), "fsdp", axis=0)
            w_ffn.append([whole])
            w_att.append([whole])
    offsets = [0 if direct else 4 * part + FF // shards, 4 * part + FF // shards]

    plan = Direct() if direct else Plain()
    mask4 = cell_mask(crop_extent, globals_)
    out, grad = layer(
        sizes, me,
        to_cells(global_tokens, local_tokens),
        to_cells(global_cotangent, local_cotangent),
        mask4, w_att, w_ffn, offsets, (direct, direct), plan,
    )
    out = from_cells(out.astype(BF), globals_)
    grad = from_cells(grad, globals_)
    grads = plan.results()
    deep = FF // shards

    def cut(half, start, n):
        return jnp.stack(
            [
                jnp.concatenate([g[half][(start + i) * part : (start + i + 1) * part] for i in range(n)], axis=1)
                for g in grads
            ]
        ).astype(F32)

    table = jnp.stack([g[1][3 * part :] for g in grads]).astype(F32)
    main = lax.dynamic_slice(table, (0, 0, index * part), (2, 18, part))
    bias = lax.dynamic_slice(table[:, 18:22].reshape(2, FF), (0, index * deep), (2, deep))
    fc2 = jnp.stack([g[0][4 * part : 4 * part + deep] for g in grads]).astype(F32)
    proj = jnp.stack([g[0][4 * part + deep :] for g in grads]).astype(F32)
    return (
        out[0], out[1], grad[0], grad[1],
        main[:, 0:9], main[:, 9:16], main[:, 16:18],
        cut(1, 0, 3), proj, cut(0, 0, 4), bias, fc2,
    )


def solution(mesh):
    crops = P(("dp", "fsdp"), None, None, None)
    last = P(None, None, "fsdp")
    middle = P(None, "fsdp", None)
    return jax.shard_map(
        body,
        mesh=mesh,
        in_specs=(
            crops, crops, P(("dp", "fsdp"), None), last, last, last, middle, middle, middle,
            P(None, "fsdp"), middle, crops, crops,
        ),
        out_specs=(
            crops, crops, crops, crops, last, last, last, middle, middle, middle, P(None, "fsdp"), middle,
        ),
        check_vma=False,
    )
```

```python
import functools

import jax
import jax.numpy as jnp
from jax import lax
from jax.experimental import pallas as pl
from jax.experimental.pallas import tpu as pltpu
from jax.sharding import PartitionSpec as P

BF = jnp.bfloat16
F32 = jnp.float32
C = 512
FF = 2048
HEAD = 32
WIN = 7
SIDE = 14
CELL = 64
LANES = 128
GROUPS = C // LANES
PER = LANES // HEAD
EPS = 1e-5
SCALE = HEAD ** -0.5
MIX_UNROLL = 7
NORM_UNROLL = 7
VMEM = pl.BlockSpec(memory_space=pltpu.VMEM)
HELD = pl.BlockSpec(memory_space=pl.ANY)
NT = (((1,), (1,)), ((), ()))
TN = (((0,), (0,)), ((), ()))
K_ROW, V_ROW, G_ROW, B_ROW, TAB = 0, 9, 16, 18, 32


def mm(a, b):
    return jnp.dot(a, b, preferred_element_type=F32)


def mm_nt(a, b):
    return lax.dot_general(a, b, NT, preferred_element_type=F32)


def mm_tn(a, b):
    return lax.dot_general(a, b, TN, preferred_element_type=F32)


class Copy:
    def __init__(self, src, dst, sems, ref):
        self.src, self.dst, self.sems, self.ref = src, dst, sems, ref
        self.open = {}

    def start(self, k=0, part=None):
        src, dst = (self.src, self.dst) if part is None else (self.src.at[part], self.dst.at[part])
        self.open[k] = pltpu.make_async_copy(src, dst, self.sems.at[k])
        self.open[k].start()

    def wait(self, k=0):
        self.open.pop(k).wait()
        return self.ref

    def wait_all(self):
        for k in list(self.open):
            self.wait(k)


PARTS = 4


def call(kernel, me, ins, outs, held=(), packs=(), scratch=(), flops=0, limit=62):
    n_in, n_out, n_held, n_pack = len(ins), len(outs), len(held), len(packs)

    def body(me_ref, *refs):
        src, refs = refs[:n_in], refs[n_in:]
        held_refs, refs = refs[:n_held], refs[n_held:]
        dst, refs = refs[:n_out], refs[n_out:]
        pack_refs, refs = refs[:n_pack], refs[n_pack:]
        in_vmem, refs = refs[:n_in], refs[n_in:]
        out_vmem, refs = refs[:n_out], refs[n_out:]
        in_sem, out_sem, refs = refs[0], refs[1], refs[2:]
        feeds = [Copy(s, v, in_sem.at[i], v) for i, (s, v) in enumerate(zip(src, in_vmem))]
        sends = [Copy(v, d, out_sem.at[i], v) for i, (d, v) in enumerate(zip(dst, out_vmem))]
        kernel(me_ref, feeds, sends, held_refs, pack_refs, *refs)
        for send in sends:
            send.wait_all()

    vmem = lambda v: pltpu.VMEM(v.shape, v.dtype)
    return pl.pallas_call(
        body,
        out_shape=list(outs) + list(packs),
        in_specs=[pl.BlockSpec(memory_space=pltpu.SMEM)] + [HELD] * (n_in + n_held),
        out_specs=[HELD] * (n_out + n_pack),
        scratch_shapes=[vmem(v) for v in ins]
        + [vmem(v) for v in outs]
        + [pltpu.SemaphoreType.DMA((max(n_in, 1), PARTS)), pltpu.SemaphoreType.DMA((max(n_out, 1), PARTS))]
        + list(scratch),
        compiler_params=pltpu.CompilerParams(vmem_limit_bytes=limit * 2**20),
        cost_estimate=pl.CostEstimate(flops=flops, bytes_accessed=2**20, transcendentals=0),
    )(me, *ins, *held)


def start_weights(bufs, me_ref, plan, sem):
    copies = []
    if len(bufs) == 1:
        sources = [(d, bufs[0].at[d]) for d in range(bufs[0].shape[0])]
    else:
        sources = [(me_ref[0] ^ k, buf) for k, buf in enumerate(bufs)]
    for d, src in sources:
        for first, rows, place in plan:
            copies.append(pltpu.make_async_copy(src.at[pl.ds(first, rows), :], place(d), sem))
    for copy in copies:
        copy.start()
    return copies


def rows_of(ref, i, rows):
    return lambda d: ref.at[i, pl.ds(pl.multiple_of(d * rows, rows), rows), :]


def slot_of(d, me_ref, relative):
    if not relative:
        return d
    turn = me_ref[0] ^ d
    return (turn & 1) * 4 + (turn >> 1)


def shape(dims, kind):
    return jax.ShapeDtypeStruct(dims, kind)


def wide(m):
    return jnp.concatenate([m] * GROUPS, axis=1)


def fold8(v):
    return jnp.sum(v.reshape(v.shape[0] // 8, 8, v.shape[1]), axis=0)


def norm_parts(x):
    center = jnp.sum(x, axis=-1, keepdims=True) * (1.0 / C)
    xc = x - center
    var = jnp.sum(xc * xc, axis=-1, keepdims=True) * (1.0 / C)
    rstd = lax.rsqrt(var + EPS)
    return xc * rstd, rstd


def norm_back(dn, xhat, rstd, gain):
    gp = dn * gain
    m1 = jnp.sum(gp, axis=-1, keepdims=True) * (1.0 / C)
    m2 = jnp.sum(gp * xhat, axis=-1, keepdims=True) * (1.0 / C)
    return rstd * (gp - m1 - xhat * m2)


def several(count, at_once, step):
    while count % at_once:
        at_once -= 1

    @pl.loop(0, count // at_once)
    def _(i):
        for j in range(at_once):
            step(i * at_once + j)


def head_masks(rows):
    lane = lax.broadcasted_iota(jnp.int32, (rows, LANES), 1) // HEAD
    return [lane == h for h in range(PER)]


def spread(v, masks):
    zero = jnp.zeros_like(v)
    return jnp.concatenate([jnp.where(m, v, zero) for m in masks], axis=0)


def gather_heads(full, masks):
    n = full.shape[0] // PER
    out = full[3 * n :]
    for h in (2, 1, 0):
        out = jnp.where(masks[h], full[h * n : (h + 1) * n], out)
    return out


def shifted_cols(left, right, j, step):
    if step == 0:
        return left, right
    if step == 1:
        return (
            jnp.where(j == 6, pltpu.roll(right, 6, 1), pltpu.roll(left, 7, 1)),
            pltpu.roll(right, 7, 1),
        )
    return (
        pltpu.roll(left, 1, 1),
        jnp.where(j == 0, pltpu.roll(left, 2, 1), pltpu.roll(right, 1, 1)),
    )


def canvas(ref, crop, lanes):
    base = crop * 32
    parts = [ref[pl.ds(base + 8 * w, 7), :, lanes] for w in range(4)]
    left = jnp.concatenate([parts[0], parts[2]], axis=0)
    right = jnp.concatenate([parts[1], parts[3]], axis=0)
    return left, right


def put_canvas(ref, crop, lanes, left, right, mask_ref):
    base = crop * 32
    zero = jnp.zeros((1, 8, LANES), F32)
    for w in range(4):
        side = right if w % 2 else left
        half = side[(w // 2) * 7 : (w // 2) * 7 + 7]
        rows = pl.ds(base + 8 * w, 8)
        ref[rows, :, lanes] = jnp.concatenate([half, zero], axis=0) * mask_ref[rows]


def conv_forward(u_ref, c_ref, small_ref, mask_ref, globals_, locals_):
    j14 = lax.broadcasted_iota(jnp.int32, (14, 8, LANES), 1)
    for g in range(GROUPS):
        lanes = pl.ds(g * LANES, LANES)
        taps = [small_ref[K_ROW + t : K_ROW + t + 1, lanes][None] for t in range(9)]
        shift = small_ref[V_ROW : V_ROW + 1, lanes][None]

        @pl.loop(0, globals_)
        def _(crop):
            left, right = canvas(u_ref, crop, lanes)
            zero = jnp.zeros((1, 8, LANES), F32)
            acc = [left + shift, right + shift]
            for e in (-1, 0, 1):
                for s, side in enumerate(shifted_cols(left, right, j14, e)):
                    tall = jnp.concatenate([zero, side, zero], axis=0)
                    for a in (-1, 0, 1):
                        acc[s] = acc[s] + taps[3 * (a + 1) + e + 1] * tall[1 + a : 15 + a]
            put_canvas(c_ref, crop, lanes, acc[0], acc[1], mask_ref)

        @pl.loop(0, locals_)
        def _(n):
            rows = pl.ds(globals_ * 32 + n * 8, 8)
            u = u_ref[rows, :, lanes]
            acc = u + shift
            for e in (-1, 0, 1):
                side = u if e == 0 else pltpu.roll(u, 7 if e == 1 else 1, 1)
                for a in (-1, 0, 1):
                    moved = side if a == 0 else jnp.roll(side, -a, axis=0)
                    acc = acc + taps[3 * (a + 1) + e + 1] * moved
            c_ref[rows, :, lanes] = acc * mask_ref[rows]


def conv_backward(d_ref, u_ref, du_ref, small_ref, acc_ref, globals_, locals_):
    j14 = lax.broadcasted_iota(jnp.int32, (14, 8, LANES), 1)
    for g in range(GROUPS):
        lanes = pl.ds(g * LANES, LANES)
        taps = [small_ref[K_ROW + t : K_ROW + t + 1, lanes][None] for t in range(9)]
        nothing = tuple(jnp.zeros((8, LANES), F32) for _ in range(10))

        def one_crop(crop, sums):
            sums = list(sums)
            left, right = canvas(d_ref, crop, lanes)
            own = canvas(u_ref, crop, lanes)
            zero = jnp.zeros((1, 8, LANES), F32)
            acc = [left, right]
            sums[9] = sums[9] + jnp.sum(left + right, axis=0)
            for e in (-1, 0, 1):
                for s, side in enumerate(shifted_cols(left, right, j14, -e)):
                    tall = jnp.concatenate([zero, side, zero], axis=0)
                    for a in (-1, 0, 1):
                        t = 3 * (a + 1) + e + 1
                        moved = tall[1 - a : 15 - a]
                        acc[s] = acc[s] + taps[t] * moved
                        sums[t] = sums[t] + jnp.sum(own[s] * moved, axis=0)
            base = crop * 32
            for w in range(4):
                side = acc[w % 2]
                half = side[(w // 2) * 7 : (w // 2) * 7 + 7]
                du_ref[pl.ds(base + 8 * w, 8), :, lanes] = jnp.concatenate([half, zero], axis=0)
            return tuple(sums)

        def one_local(n, sums):
            sums = list(sums)
            rows = pl.ds(globals_ * 32 + n * 8, 8)
            d = d_ref[rows, :, lanes]
            own = u_ref[rows, :, lanes]
            acc = d
            sums[9] = sums[9] + jnp.sum(d, axis=0)
            for e in (-1, 0, 1):
                side = d if e == 0 else pltpu.roll(d, 7 if e == -1 else 1, 1)
                for a in (-1, 0, 1):
                    t = 3 * (a + 1) + e + 1
                    moved = side if a == 0 else jnp.roll(side, a, axis=0)
                    acc = acc + taps[t] * moved
                    sums[t] = sums[t] + jnp.sum(own * moved, axis=0)
            du_ref[rows, :, lanes] = acc
            return tuple(sums)

        sums = lax.fori_loop(0, globals_, one_crop, nothing)
        sums = lax.fori_loop(0, locals_, one_local, sums)
        for t in range(10):
            acc_ref[t, :, lanes] = sums[t]


def spatial_forward(q_ref, k_ref, v_ref, mask_ref, o_ref, p_ref, windows):
    masks = head_masks(CELL)

    def step(w):
        rows = pl.ds(w * CELL, CELL)
        m = mask_ref[rows, :]
        valid = jnp.concatenate([m, m], axis=1) > 0.5
        for g in range(GROUPS):
            lanes = pl.ds(g * LANES, LANES)
            s = mm_nt(k_ref[rows, lanes], spread(q_ref[rows, lanes], masks))
            s = jnp.where(valid, s * SCALE, -1e9)
            e = jnp.exp(s - jnp.max(s, axis=0, keepdims=True))
            p = (e / jnp.sum(e, axis=0, keepdims=True)).astype(BF)
            p_ref[w, g] = p
            o_ref[rows, lanes] = gather_heads(mm_tn(p, v_ref[rows, lanes]), masks).astype(BF)

    several(windows, MIX_UNROLL, step)


def plus(a, b):
    return b if a is None else a + b


def pick(count, at_once):
    while count % at_once:
        at_once -= 1
    return at_once


def spatial_backward(q_ref, k_ref, v_ref, p_ref, do_ref, dq_ref, dk_ref, dv_ref, acc_ref, s_ref, windows, wait, send):
    masks = head_masks(CELL)
    lanes = [pl.ds(g * LANES, LANES) for g in range(GROUPS)]
    at_once = pick(windows, MIX_UNROLL)
    for ready in wait:
        ready()

    @pl.loop(0, windows // at_once)
    def _(i):
        sums = [None] * GROUPS
        for w in [i * at_once + j for j in range(at_once)]:
            rows = pl.ds(w * CELL, CELL)
            for g in range(GROUPS):
                p = p_ref[w, g]
                dos = spread(do_ref[rows, lanes[g]], masks)
                dp = mm_nt(v_ref[rows, lanes[g]], dos)
                pf = p.astype(F32)
                total = jnp.sum(pf * dp, axis=0, keepdims=True)
                ds = (pf * (dp - total) * SCALE).astype(BF)
                s_ref[w, g] = ds
                dv = mm(p, dos)
                sums[g] = plus(sums[g], fold8(dv))
                dv_ref[rows, lanes[g]] = dv.astype(BF)
                dk_ref[rows, lanes[g]] = mm(ds, spread(q_ref[rows, lanes[g]], masks)).astype(BF)
        for g in range(GROUPS):
            acc_ref[1, :, lanes[g]] += sums[g]

    send[1]()
    send[2]()

    @pl.loop(0, windows // at_once)
    def _(i):
        sums = [None] * GROUPS
        for w in [i * at_once + j for j in range(at_once)]:
            rows = pl.ds(w * CELL, CELL)
            for g in range(GROUPS):
                dq = gather_heads(mm_tn(s_ref[w, g], k_ref[rows, lanes[g]]), masks)
                sums[g] = plus(sums[g], fold8(dq))
                dq_ref[rows, lanes[g]] = dq.astype(BF)
        for g in range(GROUPS):
            acc_ref[0, :, lanes[g]] += sums[g]

    send[0]()


def same_head():
    a = lax.broadcasted_iota(jnp.int32, (LANES, LANES), 0) // HEAD
    b = lax.broadcasted_iota(jnp.int32, (LANES, LANES), 1) // HEAD
    return a == b


def over_crops(globals_, locals_, step):
    several(globals_, 3, lambda n: step(n, n * 4 * CELL, 4 * CELL))
    several(locals_, 9, lambda n: step(globals_ + n, globals_ * 4 * CELL + n * CELL, CELL))


def channel_forward(q_ref, k_ref, v_ref, mask_ref, o_ref, p_ref, globals_, locals_):
    same = same_head()
    lanes = [pl.ds(g * LANES, LANES) for g in range(GROUPS)]

    def weigh(n, start, count):
        rows = pl.ds(start, count)
        m = mask_ref[rows, :].astype(BF)
        for g in range(GROUPS):
            s = mm_tn(v_ref[rows, lanes[g]], k_ref[rows, lanes[g]] * m)
            s = jnp.where(same, s * SCALE, -jnp.inf)
            e = jnp.exp(s - jnp.max(s, axis=0, keepdims=True))
            p_ref[n, g] = (e / jnp.sum(e, axis=0, keepdims=True)).astype(BF)

    over_crops(globals_, locals_, weigh)

    def step(n, start, count):
        rows = pl.ds(start, count)
        for g in range(GROUPS):
            o_ref[rows, lanes[g]] = mm(q_ref[rows, lanes[g]], p_ref[n, g]).astype(BF)

    over_crops(globals_, locals_, step)


def channel_backward(
    q_ref, k_ref, v_ref, mask_ref, p_ref, do_ref, dq_ref, dk_ref, dv_ref, acc_ref, s_ref, globals_, locals_, wait, send
):
    lanes = [pl.ds(g * LANES, LANES) for g in range(GROUPS)]

    def slope(n, start, count):
        rows = pl.ds(start, count)
        for g in range(GROUPS):
            dp = mm_tn(q_ref[rows, lanes[g]], do_ref[rows, lanes[g]])
            pf = p_ref[n, g].astype(F32)
            total = jnp.sum(pf * dp, axis=0, keepdims=True)
            s_ref[n, g] = (pf * (dp - total) * SCALE).astype(BF)

    for ready in wait[:3]:
        ready()
    over_crops(globals_, locals_, slope)
    for ready in wait[3:]:
        ready()

    def step(n, start, count):
        rows = pl.ds(start, count)
        mf = mask_ref[rows, :]
        m = mf.astype(BF)
        for g in range(GROUPS):
            ds = s_ref[n, g]
            dq = mm_nt(do_ref[rows, lanes[g]], p_ref[n, g])
            dk = mm(v_ref[rows, lanes[g]], ds) * mf
            dv = mm_nt(k_ref[rows, lanes[g]] * m, ds)
            acc_ref[0, :, lanes[g]] += fold8(dq)
            acc_ref[1, :, lanes[g]] += fold8(dv)
            dq_ref[rows, lanes[g]] = dq.astype(BF)
            dk_ref[rows, lanes[g]] = dk.astype(BF)
            dv_ref[rows, lanes[g]] = dv.astype(BF)

    over_crops(globals_, locals_, step)
    for go in send:
        go()


def table_of(tabs):
    total = tabs[0].astype(F32)
    for d in range(1, tabs.shape[0]):
        total = total + tabs[d].astype(F32)
    return total


CHUNKS = 3


def chunks_of(rows):
    size = rows // CHUNKS
    return [pl.ds(i * size, size) for i in range(CHUNKS)]


def tiles_of(here):
    return pl.ds(here.start // 8, here.size // 8)


def attention_forward(sizes, kind, me, u, mask, bufs, first):
    globals_, locals_, shards = sizes
    windows = 4 * globals_ + locals_
    rows = windows * CELL
    part = C // shards
    chunks = chunks_of(rows)

    def kernel(me_ref, feeds, sends, held, packs, w, tabs, sem, sem2):
        u_in, m_in = feeds
        r_out, small_out, c_out, n_out, q_out, k_out, v_out, o_out, p_out = sends
        r_ref, small_ref, c_ref, n_ref, q_ref, k_ref, v_ref, o_ref, p_ref = [v.ref for v in sends]
        u_in.start()
        tab = start_weights(held, me_ref, [(first + 4 * part, TAB, lambda d: tabs.at[d])], sem2)
        m_in.start()
        plan = [(first + i * part, part, rows_of(w, i, part)) for i in range(4)]
        copies = start_weights(held, me_ref, plan, sem)
        for copy in tab:
            copy.wait()
        small_ref[...] = table_of(tabs)
        small_out.start()
        u_ref = u_in.wait()
        mask_ref = m_in.wait()
        conv_forward(u_ref, c_ref, small_ref, mask_ref.reshape(windows * 8, 8, LANES), globals_, locals_)
        c_out.start()
        gain = small_ref[G_ROW : G_ROW + 1]
        shift = small_ref[V_ROW + 1 : V_ROW + 2]

        def step(i):
            x = c_ref[pl.ds(i * 8, 8)].reshape(CELL, C)
            xhat, _ = norm_parts(x)
            n_ref[pl.ds(i * CELL, CELL), :] = (xhat * gain + shift).astype(BF)

        several(windows, NORM_UNROLL, step)
        n_out.start()
        for copy in copies:
            copy.wait()
        for here in chunks:
            n1 = n_ref[here, :]
            q_ref[here, :] = (mm(n1, w[0]) + small_ref[V_ROW + 2 : V_ROW + 3]).astype(BF)
            k_ref[here, :] = mm(n1, w[1]).astype(BF)
            v_ref[here, :] = (mm(n1, w[2]) + small_ref[V_ROW + 3 : V_ROW + 4]).astype(BF)
        for send in (q_out, k_out, v_out):
            send.start()
        if kind == 0:
            spatial_forward(q_ref, k_ref, v_ref, mask_ref, o_ref, p_ref, windows)
        else:
            channel_forward(q_ref, k_ref, v_ref, mask_ref, o_ref, p_ref, globals_, locals_)
        p_out.start()
        o_out.start()
        for i, here in enumerate(chunks):
            c = c_ref[tiles_of(here)].reshape(here.size, C)
            r_ref[here, :] = c + mm(o_ref[here, :], w[3]) + small_ref[V_ROW + 4 : V_ROW + 5]
            r_out.start(i, here)

    low = shape((rows, C), BF)
    probs = (windows, GROUPS, CELL, PER * CELL) if kind == 0 else (globals_ + locals_, GROUPS, LANES, LANES)
    outs = [
        shape((rows, C), F32), shape((TAB, C), F32), shape((windows * 8, 8, C), F32),
        low, low, low, low, low, shape(probs, BF),
    ]
    scratch = [
        pltpu.VMEM((4, C, C), BF),
        pltpu.VMEM((shards, TAB, C), BF),
        pltpu.SemaphoreType.DMA,
        pltpu.SemaphoreType.DMA,
    ]
    return call(kernel, me, [u, mask], outs, held=bufs, scratch=scratch, flops=1)


def ffn_plan(part, deep, w1, w2):
    plan = [(i * part, part, rows_of(w1, i, part)) for i in range(FF // C)]
    return plan + [((FF // C) * part, deep, lambda d: w2.at[pl.ds(pl.multiple_of(d * deep, deep), deep), :])]


def ffn_forward(sizes, me, r, mask, small, bufs):
    globals_, locals_, shards = sizes
    windows = 4 * globals_ + locals_
    rows = windows * CELL
    part = C // shards
    deep = FF // shards
    chunks = chunks_of(rows)

    def kernel(me_ref, feeds, sends, held, packs, w1, w2, sem):
        r_in, m_in, small_in = feeds
        x_out, n_out, g_out, s_out = sends
        x_ref, n_ref, g_ref, s_ref = [v.ref for v in sends]
        small_in.start()
        r_in.start()
        copies = start_weights(held, me_ref, ffn_plan(part, deep, w1, w2), sem)
        m_in.start()
        small_ref = small_in.wait()
        gain = small_ref[G_ROW + 1 : G_ROW + 2]
        shift = small_ref[V_ROW + 5 : V_ROW + 6]
        r_ref = r_in.wait()

        def step(i):
            here = pl.ds(i * CELL, CELL)
            xhat, _ = norm_parts(r_ref[here, :])
            n_ref[here, :] = (xhat * gain + shift).astype(BF)

        several(windows, NORM_UNROLL, step)
        n_out.start()
        mask_ref = m_in.wait()
        for copy in copies:
            copy.wait()
        for i, here in enumerate(chunks):
            n2 = n_ref[here, :]
            for t in range(FF // C):
                h = mm(n2, w1[t]) + small_ref[B_ROW + t : B_ROW + t + 1]
                h2 = h * h
                a = 0.5 + 0.5 * jnp.tanh(h * (0.7978845608 + (0.7978845608 * 0.044715) * h2))
                g = h * a
                slope = a + (2.0 * g) * (1.0 - a) * (0.7978845608 + (3 * 0.7978845608 * 0.044715) * h2)
                g_ref[here, t * C : (t + 1) * C] = g.astype(BF)
                s_ref[here, t * C : (t + 1) * C] = slope.astype(BF)
            g_out.start(i, here)
            s_out.start(i, here)
            y = r_ref[here, :] + mm(g_ref[here, :], w2[...]) + small_ref[V_ROW + 6 : V_ROW + 7]
            x_ref[here, :] = y * wide(mask_ref[here, :])
            x_out.start(i, here)

    high = shape((rows, FF), BF)
    outs = [shape((rows, C), F32), shape((rows, C), BF), high, high]
    scratch = [pltpu.VMEM((FF // C, C, C), BF), pltpu.VMEM((FF, C), BF), pltpu.SemaphoreType.DMA]
    return call(kernel, me, [r, mask, small], outs, held=bufs, scratch=scratch, flops=1)


def pack_outs(shards, count, relative):
    if relative:
        return [shape((4, count, C), BF)] * 2
    return [shape((shards, count, C), BF)]


def send_pack(dw, outs, rows, sem):
    each = len(outs) == 2
    copies = []
    for i, out in enumerate(outs):
        src = dw.at[pl.ds(4 * i, 4), rows] if each else dw.at[:, rows]
        copies.append(pltpu.make_async_copy(src, out.at[:, rows], sem))
    for copy in copies:
        copy.start()
    return copies


def ffn_backward(sizes, me, relative, dy, r, n2, g, slope, o, mask, small, w_ffn, w_att, first, deps):
    globals_, locals_, shards = sizes
    windows = 4 * globals_ + locals_
    rows = windows * CELL
    part = C // shards
    deep = FF // shards
    count = 4 * part + deep + part
    chunks = chunks_of(rows)
    packs = pack_outs(shards, count, relative)
    n_ffn, n_att = len(w_ffn), len(w_att)

    def kernel(me_ref, feeds, sends, held, dw_out, w1, w2, wp, dw, dyl, dh, acc, acc1, sem, sem2):
        dy_in, r_in, n_in, g_in, s_in, o_in, m_in, small_in = feeds
        dr_out, do_out, ds_out = sends
        dr_ref, do_ref, ds_ref = [v.ref for v in sends]
        dy_in.start()
        m_in.start()
        copies = start_weights(held[:n_ffn], me_ref, ffn_plan(part, deep, w1, w2), sem)
        for i, here in enumerate(chunks):
            s_in.start(i, here)
        copies += start_weights(
            held[n_ffn : n_ffn + n_att], me_ref, [(first + 3 * part, part, rows_of(wp, 0, part))], sem
        )
        small_in.start()
        acc[...] = jnp.zeros_like(acc)
        acc1[...] = jnp.zeros_like(acc1)
        dy_ref = dy_in.wait()
        mask_ref = m_in.wait()

        def step(i):
            here = pl.ds(i * CELL, CELL)
            d = dy_ref[here, :] * wide(mask_ref[here, :])
            dyl[here, :] = d.astype(BF)
            acc[2] += fold8(d)

        several(windows, NORM_UNROLL, step)
        for feed in (n_in, g_in, r_in, o_in):
            feed.start()
        for copy in copies:
            copy.wait()
        for i, here in enumerate(chunks):
            s_ref = s_in.wait(i)
            for t in range(FF // C):
                cols = slice(t * C, (t + 1) * C)
                d = mm_nt(dyl[here, :], w2[cols, :]) * s_ref[here, cols].astype(F32)
                acc1[:, cols] += fold8(d)
                dh[here, cols] = d.astype(BF)
            dn = None
            for t in range(FF // C):
                one = mm_nt(dh[here, t * C : (t + 1) * C], w1[t])
                dn = one if dn is None else dn + one
            dr_ref[here, :] = dn

        n_ref = n_in.wait()
        g_ref = g_in.wait()
        for t in range(FF // C):
            cols = slice(t * C, (t + 1) * C)
            one = mm_tn(n_ref[...], dh[:, cols]).astype(BF)
            for d in range(shards):
                dw[slot_of(d, me_ref, relative), t * part : (t + 1) * part, :] = one[d * part : (d + 1) * part]
            two = mm_tn(g_ref[:, cols], dyl[...]).astype(BF)
            for d in range(C // deep):
                here = pl.ds(4 * part, deep)
                dw[slot_of(t * (C // deep) + d, me_ref, relative), here, :] = two[d * deep : (d + 1) * deep]
        going = send_pack(dw, dw_out, pl.ds(0, 4 * part + deep), sem2)

        small_ref = small_in.wait()
        gain = small_ref[G_ROW + 1 : G_ROW + 2]
        r_ref = r_in.wait()

        def step(i):
            here = pl.ds(i * CELL, CELL)
            dn = dr_ref[here, :]
            xhat, rstd = norm_parts(r_ref[here, :])
            acc[0] += fold8(dn * xhat)
            acc[1] += fold8(dn)
            dr = norm_back(dn, xhat, rstd, gain) + dy_ref[here, :] * wide(mask_ref[here, :])
            acc[3] += fold8(dr)
            dr_ref[here, :] = dr
            dyl[here, :] = dr.astype(BF)

        several(windows, NORM_UNROLL, step)
        dr_out.start()
        for i, here in enumerate(chunks):
            do_ref[here, :] = mm_nt(dyl[here, :], wp[0]).astype(BF)
            do_out.start(i, here)
        o_ref = o_in.wait()
        one = mm_tn(o_ref[...], dyl[...]).astype(BF)
        for d in range(shards):
            dw[slot_of(d, me_ref, relative), 4 * part + deep :, :] = one[d * part : (d + 1) * part]
        going += send_pack(dw, dw_out, pl.ds(4 * part + deep, part), sem2)
        for i in range(3):
            ds_ref[i : i + 1, :] = jnp.sum(acc[i], axis=0, keepdims=True)
        for t in range(FF // C):
            ds_ref[3 + t : 4 + t, :] = jnp.sum(acc1[:, t * C : (t + 1) * C], axis=0, keepdims=True)
        ds_ref[7:8, :] = jnp.sum(acc[3], axis=0, keepdims=True)
        ds_out.start()
        for copy in going:
            copy.wait()

    outs = [shape((rows, C), F32), shape((rows, C), BF), shape((8, C), F32)]
    scratch = [
        pltpu.VMEM((FF // C, C, C), BF),
        pltpu.VMEM((FF, C), BF),
        pltpu.VMEM((1, C, C), BF),
        pltpu.VMEM((shards, count, C), BF),
        pltpu.VMEM((rows, C), BF),
        pltpu.VMEM((rows, FF), BF),
        pltpu.VMEM((4, 8, C), F32),
        pltpu.VMEM((8, FF), F32),
        pltpu.SemaphoreType.DMA,
        pltpu.SemaphoreType.DMA,
    ]
    return call(
        kernel, me, [dy, r, n2, g, slope, o, mask, small], outs, held=[*w_ffn, *w_att, *deps], packs=packs,
        scratch=scratch, flops=160 * rows * C * C,
    )


def mix_backward(sizes, kind, q, k, v, p, do, mask, me, deps):
    globals_, locals_, _ = sizes
    windows = 4 * globals_ + locals_
    rows = windows * CELL

    def kernel(me_ref, feeds, sends, held, packs, acc, slope):
        q_in, k_in, v_in, p_in, do_in, m_in = feeds
        q_ref, k_ref, v_ref, p_ref, do_ref, mask_ref = [v.ref for v in feeds]
        dq, dk, dv, ds_ref = [v.ref for v in sends]
        order = (v_in, do_in, p_in, q_in, k_in, m_in) if kind == 0 else (q_in, do_in, p_in, v_in, k_in, m_in)
        for feed in order:
            feed.start()
        acc[...] = jnp.zeros_like(acc)
        if kind == 0:
            spatial_backward(
                q_ref, k_ref, v_ref, p_ref, do_ref, dq, dk, dv, acc, slope, windows,
                [feed.wait for feed in order], [send.start for send in sends[:3]],
            )
        else:
            channel_backward(
                q_ref, k_ref, v_ref, mask_ref, p_ref, do_ref, dq, dk, dv, acc, slope, globals_, locals_,
                [feed.wait for feed in order], [send.start for send in sends[:3]],
            )
        for t in range(2):
            ds_ref[t : t + 1, :] = jnp.sum(acc[t], axis=0, keepdims=True)
        ds_ref[2:8, :] = jnp.zeros((6, C), F32)
        sends[3].start()

    low = shape((rows, C), BF)
    return call(
        kernel, me, [q, k, v, p, do, mask], [low, low, low, shape((8, C), F32)], held=deps,
        scratch=[pltpu.VMEM((2, 8, C), F32), pltpu.VMEM(p.shape, BF)], flops=64 * rows * C * C,
    )


def attention_backward(sizes, me, relative, dr, u, c, n1, dq, dk, dv, ds_ffn, ds_mix, mask, small, bufs, first, deps):
    globals_, locals_, shards = sizes
    windows = 4 * globals_ + locals_
    rows = windows * CELL
    part = C // shards
    count = 3 * part + TAB
    chunks = chunks_of(rows)
    packs = pack_outs(shards, count, relative)

    def kernel(me_ref, feeds, sends, held, dw_out, w, dw, dn, acc, acck, tab, sem, sem2):
        dr_in, u_in, c_in, n_in, dq_in, dk_in, dv_in, ffn_in, mix_in, m_in, small_in = feeds
        dr_ref, u_ref, c_ref, n_ref, dq, dk, dv, ffn_ref, mix_ref, mask_ref, small_ref = [v.ref for v in feeds]
        du_ref = sends[0].ref
        plan = [(first + i * part, part, rows_of(w, i, part)) for i in range(3)]
        copies = start_weights(held[: len(bufs)], me_ref, plan, sem)
        for i, here in enumerate(chunks):
            for feed in (dq_in, dk_in, dv_in):
                feed.start(i, here)
        for feed in (c_in, dr_in, m_in, small_in, u_in, n_in, ffn_in, mix_in):
            feed.start()
        acc[...] = jnp.zeros_like(acc)
        for copy in copies:
            copy.wait()
        for i, here in enumerate(chunks):
            for feed in (dq_in, dk_in, dv_in):
                feed.wait(i)
            total = mm_nt(dq[here, :], w[0]) + mm_nt(dk[here, :], w[1]) + mm_nt(dv[here, :], w[2])
            dn[tiles_of(here)] = total.reshape(here.size // 8, 8, C)

        for feed in (c_in, dr_in, m_in, small_in):
            feed.wait()
        gain = small_ref[G_ROW : G_ROW + 1]

        def step(i):
            here = pl.ds(i * CELL, CELL)
            tiles = pl.ds(i * 8, 8)
            d = dn[tiles].reshape(CELL, C)
            xhat, rstd = norm_parts(c_ref[tiles].reshape(CELL, C))
            acc[0] += fold8(d * xhat)
            acc[1] += fold8(d)
            dc = norm_back(d, xhat, rstd, gain) + dr_ref[here, :]
            dn[tiles] = (dc * wide(mask_ref[here, :])).reshape(8, 8, C)

        several(windows, NORM_UNROLL, step)
        u_in.wait()
        conv_backward(dn, u_ref, du_ref, small_ref, acck, globals_, locals_)
        sends[0].start()

        ffn_in.wait()
        mix_in.wait()
        rows_ = [jnp.sum(acck[t], axis=0, keepdims=True) for t in range(10)]
        rows_ += [jnp.sum(acc[1], axis=0, keepdims=True), mix_ref[0:1, :], mix_ref[1:2, :], ffn_ref[7:8, :]]
        rows_ += [ffn_ref[1:2, :], ffn_ref[2:3, :], jnp.sum(acc[0], axis=0, keepdims=True), ffn_ref[0:1, :]]
        rows_ += [ffn_ref[3 + t : 4 + t, :] for t in range(FF // C)]
        tab[...] = jnp.zeros_like(tab)
        for t, row in enumerate(rows_):
            tab[t : t + 1, :] = row
        low = tab[...].astype(BF)
        for d in range(shards):
            dw[d, 3 * part :, :] = low
        going = send_pack(dw, dw_out, pl.ds(3 * part, TAB), sem2)

        n_in.wait()
        for i, right in enumerate((dq, dk, dv)):
            one = mm_tn(n_ref[...], right[...]).astype(BF)
            for d in range(shards):
                dw[slot_of(d, me_ref, relative), i * part : (i + 1) * part, :] = one[d * part : (d + 1) * part]
            going += send_pack(dw, dw_out, pl.ds(i * part, part), sem2)
        for copy in going:
            copy.wait()

    outs = [shape((windows * 8, 8, C), F32)]
    scratch = [
        pltpu.VMEM((3, C, C), BF),
        pltpu.VMEM((shards, count, C), BF),
        pltpu.VMEM((windows * 8, 8, C), F32),
        pltpu.VMEM((2, 8, C), F32),
        pltpu.VMEM((10, 8, C), F32),
        pltpu.VMEM((TAB, C), F32),
        pltpu.SemaphoreType.DMA,
        pltpu.SemaphoreType.DMA,
    ]
    return call(
        kernel, me, [dr, u, c, n1, dq, dk, dv, ds_ffn, ds_mix, mask, small], outs, held=[*bufs, *deps],
        packs=packs, scratch=scratch, flops=80 * rows * C * C,
    )


def join(values, deps):
    values, deps = list(values), list(deps)

    def kernel(*refs):
        pass

    return pl.pallas_call(
        kernel,
        out_shape=[shape(v.shape, v.dtype) for v in values],
        in_specs=[HELD] * (len(values) + len(deps)),
        out_specs=[HELD] * len(values),
        input_output_aliases={i: i for i in range(len(values))},
    )(*values, *deps)


def to_cells(glob, loc):
    count = glob.shape[0]
    wins = glob.reshape(count, 2, WIN, 2, WIN, C).transpose(0, 1, 3, 2, 4, 5).reshape(count * 4, WIN, WIN, C)
    both = jnp.concatenate([wins, loc], axis=0)
    return jnp.pad(both, ((0, 0), (0, 1), (0, 1), (0, 0))).astype(F32)


def from_cells(cells, globals_):
    cells = cells.reshape(-1, 8, 8, C)[:, :WIN, :WIN]
    wins = cells[: globals_ * 4].reshape(globals_, 2, 2, WIN, WIN, C)
    return wins.transpose(0, 1, 3, 2, 4, 5).reshape(globals_, SIDE, SIDE, C), cells[globals_ * 4 :]


def cell_mask(extent, globals_):
    places = jnp.arange(8, dtype=jnp.int32)
    size = jnp.concatenate([jnp.full((globals_ * 4, 2), WIN, jnp.int32), extent.astype(jnp.int32)], axis=0)
    rows = places[None, :, None] < size[:, 0][:, None, None]
    cols = places[None, None, :] < size[:, 1][:, None, None]
    return jnp.logical_and(rows, cols).astype(F32)


def layer(sizes, me, tokens, cotangent, mask4, w_att, w_ffn, offsets, relative, plan):
    windows = 4 * sizes[0] + sizes[1]
    rows = windows * CELL
    mask = jnp.broadcast_to(mask4.reshape(rows, 1), (rows, LANES))
    u = (tokens * mask4[..., None]).reshape(windows * 8, 8, C)
    dy = cotangent.reshape(rows, C)
    kept = []
    for b in range(2):
        w_att[b] = plan.weights(w_att[b], u if b else None)
        r, small, *att = attention_forward(sizes, b, me, u, mask, w_att[b], offsets[b])
        w_ffn[b] = plan.weights(w_ffn[b], r)
        x, *ffn = ffn_forward(sizes, me, r, mask, small, w_ffn[b])
        kept.append((u, r, small, att, ffn))
        u = x.reshape(windows * 8, 8, C)
    out = u
    for b in (1, 0):
        u, r, small, (c, n1, q, k, v, o, p), ffn = kept[b]
        dr, do, ds_ffn, *dw = ffn_backward(
            sizes, me, relative[b], dy, r, *ffn, o, mask, small, w_ffn[b], w_att[b], offsets[b], []
        )
        deps = plan.after_ffn(b, dw, dr)
        dq, dk, dv, ds_mix = mix_backward(sizes, b, q, k, v, p, do, mask, me, deps)
        deps = plan.after_mix(b, dq)
        du, *dw = attention_backward(
            sizes, me, relative[b], dr, u, c, n1, dq, dk, dv, ds_ffn, ds_mix, mask, small, w_att[b], offsets[b], deps
        )
        plan.after_att(b, dw, du)
        dy = du.reshape(rows, C)
    return out, du * mask4.reshape(windows * 8, 8, 1)


def xor(v, axis, turn):
    size = lax.axis_size(axis)
    return lax.ppermute(v, axis, [(i, i ^ turn) for i in range(size)])


def gather_near(own):
    return [own, xor(own, "fsdp", 2), xor(own, "fsdp", 4), xor(own, "fsdp", 6)]


def gather_core(near):
    out = []
    for v in near:
        out += [v, xor(v, "fsdp", 1)]
    return out


def add(*terms):
    total = terms[0].astype(F32)
    for term in terms[1:]:
        total = total + term.astype(F32)
    return total.astype(BF)


def to_core(pack):
    return xor(pack[1], "fsdp", 1)


def to_chips(parts):
    return [xor(v, "fsdp", 2 * i + 2) for i, v in enumerate(parts[1:])]


def core_sums(pack, got):
    return [add(pack[0][i], got[i]) for i in range(4)]


class Direct:
    def weights(self, near, token):
        return gather_core(near if token is None else join(near, [token]))

    def after_ffn(self, b, dw, token):
        if b == 1:
            self.f1, self.f1_core = dw, to_core(dw)
            return []
        self.f0, self.f0_core = dw, to_core(dw)
        *chips, core = join([*self.f1_chips, self.a1_core], [token])
        self.f1_sum = Spread(add(self.f1_sums[0], *chips))
        self.f1_sum.first()
        self.a1_sums = core_sums(self.a1, core)
        self.a1_chips = to_chips(self.a1_sums)
        return [self.f1_sum.keep, *self.a1_sums]

    def after_mix(self, b, token):
        if b == 1:
            (core,) = join([self.f1_core], [token])
            self.f1_sums = core_sums(self.f1, core)
            self.f1_chips = to_chips(self.f1_sums)
            return self.f1_sums
        *chips, core, self.f1_sum.got = join([*self.a1_chips, self.f0_core, self.f1_sum.got], [token])
        self.f1_sum.second()
        self.a1_sum = Spread(add(self.a1_sums[0], *chips))
        self.a1_sum.first()
        self.f0_sums = core_sums(self.f0, core)
        self.f0_chips = to_chips(self.f0_sums)
        return [self.f1_sum.half, self.a1_sum.keep, *self.f0_sums]

    def after_att(self, b, dw, token):
        if b == 1:
            self.a1, self.a1_core = dw, to_core(dw)
            return
        a0_core = to_core(dw)
        *chips, self.f1_sum.got, self.a1_sum.got = join([*self.f0_chips, self.f1_sum.got, self.a1_sum.got], [token])
        f0_sum = Spread(add(self.f0_sums[0], *chips))
        a0_sums = core_sums(dw, a0_core)
        a0_sum = Spread(add(a0_sums[0], *to_chips(a0_sums)))
        f0_sum.first()
        a0_sum.first()
        for one in (self.a1_sum, f0_sum, a0_sum):
            one.second()
        far = [one.third() for one in (self.f1_sum, self.a1_sum)]
        near = [one.third() for one in (f0_sum, a0_sum)]
        self.done = [near, far]

    def results(self):
        return self.done


class Spread:
    def __init__(self, v):
        n = v.shape[0] // 2
        self.low = (lax.axis_index("dp") & 1) == 0
        self.keep = jnp.where(self.low, v[:n], v[n:])
        self.send = jnp.where(self.low, v[n:], v[:n])

    def first(self):
        self.got = xor(self.send, "dp", 1)

    def second(self):
        self.half = add(self.keep, self.got)
        self.got = xor(self.half, "dp", 2)

    def third(self):
        whole = add(self.half, self.got)
        other = xor(whole, "dp", 1)
        return jnp.concatenate([jnp.where(self.low, whole, other), jnp.where(self.low, other, whole)])


class Plain:
    def __init__(self):
        self.packs = [[None, None], [None, None]]

    def weights(self, near, token):
        return near

    def after_ffn(self, b, dw, token):
        self.packs[b][0] = dw[0]
        return []

    def after_mix(self, b, token):
        return []

    def after_att(self, b, dw, token):
        self.packs[b][1] = dw[0]

    def results(self):
        return [
            lax.psum([lax.psum_scatter(v, "fsdp", scatter_dimension=0, tiled=True)[0] for v in pair], "dp")
            for pair in self.packs
        ]


def body(
    global_tokens,
    local_tokens,
    crop_extent,
    conv_weight,
    vectors,
    gains,
    qkv_weight,
    proj_weight,
    fc1_weight,
    fc1_bias,
    fc2_weight,
    global_cotangent,
    local_cotangent,
):
    shards = lax.axis_size("fsdp")
    direct = shards == 8 and lax.axis_size("dp") == 4
    part = C // shards
    globals_, locals_ = global_tokens.shape[0], local_tokens.shape[0]
    sizes = (globals_, locals_, shards)
    index = lax.axis_index("fsdp")
    me = index.astype(jnp.int32).reshape(1)

    own_small = jnp.concatenate([conv_weight, vectors, gains], axis=1)
    own_bias = fc1_bias.reshape(2, 1, FF // shards)
    w_att, w_ffn = [], []
    for b in range(2):
        cols = lambda w, n: [w[b][:, i * C : (i + 1) * C] for i in range(n)]
        table = jnp.zeros((TAB, C), BF)
        table = lax.dynamic_update_slice(table, own_small[b], (0, index * part))
        start = index * (FF // shards)
        table = lax.dynamic_update_slice(table, own_bias[b], (B_ROW + start // C, start % C))
        att = cols(qkv_weight, 3) + [proj_weight[b], table]
        ffn = cols(fc1_weight, 4) + [fc2_weight[b]]
        if direct:
            w_att.append(gather_near(jnp.concatenate(att, axis=0)))
            w_ffn.append(gather_near(jnp.concatenate(ffn, axis=0)))
        else:
            whole = lax.all_gather(jnp.concatenate(ffn + att, axis=0), "fsdp", axis=0)
            w_ffn.append([whole])
            w_att.append([whole])
    offsets = [0 if direct else 4 * part + FF // shards] * 2

    plan = Direct() if direct else Plain()
    mask4 = cell_mask(crop_extent, globals_)
    out, grad = layer(
        sizes, me,
        to_cells(global_tokens, local_tokens),
        to_cells(global_cotangent, local_cotangent),
        mask4, w_att, w_ffn, offsets, (direct, direct), plan,
    )
    out = from_cells(out.astype(BF), globals_)
    grad = from_cells(grad, globals_)
    grads = plan.results()
    deep = FF // shards

    def cut(half, start, n):
        return jnp.stack(
            [
                jnp.concatenate([g[half][(start + i) * part : (start + i + 1) * part] for i in range(n)], axis=1)
                for g in grads
            ]
        ).astype(F32)

    table = jnp.stack([g[1][3 * part :] for g in grads]).astype(F32)
    main = lax.dynamic_slice(table, (0, 0, index * part), (2, 18, part))
    bias = lax.dynamic_slice(table[:, 18:22].reshape(2, FF), (0, index * deep), (2, deep))
    fc2 = jnp.stack([g[0][4 * part : 4 * part + deep] for g in grads]).astype(F32)
    proj = jnp.stack([g[0][4 * part + deep :] for g in grads]).astype(F32)
    return (
        out[0], out[1], grad[0], grad[1],
        main[:, 0:9], main[:, 9:16], main[:, 16:18],
        cut(1, 0, 3), proj, cut(0, 0, 4), bias, fc2,
    )


def solution(mesh):
    crops = P(("dp", "fsdp"), None, None, None)
    last = P(None, None, "fsdp")
    middle = P(None, "fsdp", None)
    return jax.shard_map(
        body,
        mesh=mesh,
        in_specs=(
            crops, crops, P(("dp", "fsdp"), None), last, last, last, middle, middle, middle,
            P(None, "fsdp"), middle, crops, crops,
        ),
        out_specs=(
            crops, crops, crops, crops, last, last, last, middle, middle, middle, P(None, "fsdp"), middle,
        ),
        check_vma=False,
    )
```

```python
import functools

import jax
import jax.numpy as jnp
from jax import lax
from jax.experimental import pallas as pl
from jax.experimental.pallas import tpu as pltpu
from jax.sharding import PartitionSpec as P

BF = jnp.bfloat16
F32 = jnp.float32
C = 512
FF = 2048
HEAD = 32
WIN = 7
SIDE = 14
CELL = 64
LANES = 128
GROUPS = C // LANES
PER = LANES // HEAD
EPS = 1e-5
SCALE = HEAD ** -0.5
MIX_UNROLL = 7
NORM_UNROLL = 7
FORWARD, BACKWARD = 1, 3
VMEM = pl.BlockSpec(memory_space=pltpu.VMEM)
HELD = pl.BlockSpec(memory_space=pl.ANY)
NT = (((1,), (1,)), ((), ()))
TN = (((0,), (0,)), ((), ()))
K_ROW, V_ROW, G_ROW, B_ROW, TAB = 0, 9, 16, 18, 32


def mm(a, b):
    return jnp.dot(a, b, preferred_element_type=F32)


def mm_nt(a, b):
    return lax.dot_general(a, b, NT, preferred_element_type=F32)


def mm_tn(a, b):
    return lax.dot_general(a, b, TN, preferred_element_type=F32)


class Copy:
    def __init__(self, src, dst, sems, ref):
        self.src, self.dst, self.sems, self.ref = src, dst, sems, ref
        self.open = {}

    def start(self, k=0, part=None):
        src, dst = (self.src, self.dst) if part is None else (self.src.at[part], self.dst.at[part])
        self.open[k] = pltpu.make_async_copy(src, dst, self.sems.at[k])
        self.open[k].start()

    def wait(self, k=0):
        self.open.pop(k).wait()
        return self.ref

    def wait_all(self):
        for k in list(self.open):
            self.wait(k)


PARTS = 4


def call(kernel, me, ins, outs, held=(), packs=(), scratch=(), micros=1, alias=None, limit=62):
    n_in, n_out, n_held, n_pack = len(ins), len(outs), len(held), len(packs)

    def body(me_ref, *refs):
        src, refs = refs[:n_in], refs[n_in:]
        held_refs, refs = refs[:n_held], refs[n_held:]
        dst, refs = refs[:n_out], refs[n_out:]
        pack_refs, refs = refs[:n_pack], refs[n_pack:]
        in_vmem, refs = refs[:n_in], refs[n_in:]
        out_vmem, refs = refs[:n_out], refs[n_out:]
        in_sem, out_sem, refs = refs[0], refs[1], refs[2:]
        feeds = [Copy(s, v, in_sem.at[i], v) for i, (s, v) in enumerate(zip(src, in_vmem))]
        sends = [Copy(v, d, out_sem.at[i], v) for i, (d, v) in enumerate(zip(dst, out_vmem))]
        kernel(me_ref, feeds, sends, held_refs, pack_refs, *refs)
        for send in sends:
            send.wait_all()

    vmem = lambda v: pltpu.VMEM(v.shape, v.dtype)
    return pl.pallas_call(
        body,
        out_shape=list(outs) + list(packs),
        in_specs=[pl.BlockSpec(memory_space=pltpu.SMEM)] + [HELD] * (n_in + n_held),
        out_specs=[HELD] * (n_out + n_pack),
        scratch_shapes=[vmem(v) for v in ins]
        + [vmem(v) for v in outs]
        + [pltpu.SemaphoreType.DMA((max(n_in, 1), PARTS)), pltpu.SemaphoreType.DMA((max(n_out, 1), PARTS))]
        + list(scratch),
        compiler_params=pltpu.CompilerParams(vmem_limit_bytes=limit * 2**20),
        cost_estimate=pl.CostEstimate(flops=int(micros * 1.1e9), bytes_accessed=2**20, transcendentals=0),
        input_output_aliases=alias or {},
    )(me, *ins, *held)


def start_weights(bufs, me_ref, plan, sem):
    copies = []
    if len(bufs) == 1:
        sources = [(d, bufs[0].at[d]) for d in range(bufs[0].shape[0])]
    else:
        sources = [(me_ref[0] ^ k, buf) for k, buf in enumerate(bufs)]
    for d, src in sources:
        for first, rows, place in plan:
            copies.append(pltpu.make_async_copy(src.at[pl.ds(first, rows), :], place(d), sem))
    for copy in copies:
        copy.start()
    return copies


def rows_of(ref, i, rows):
    return lambda d: ref.at[i, pl.ds(pl.multiple_of(d * rows, rows), rows), :]


def slot_of(d, me_ref, relative):
    if not relative:
        return d
    turn = me_ref[0] ^ d
    return (turn & 1) * 4 + (turn >> 1)


def shape(dims, kind):
    return jax.ShapeDtypeStruct(dims, kind)


def wide(m):
    return jnp.concatenate([m] * GROUPS, axis=1)


def fold8(v):
    return jnp.sum(v.reshape(v.shape[0] // 8, 8, v.shape[1]), axis=0)


def norm_parts(x):
    center = jnp.sum(x, axis=-1, keepdims=True) * (1.0 / C)
    xc = x - center
    var = jnp.sum(xc * xc, axis=-1, keepdims=True) * (1.0 / C)
    rstd = lax.rsqrt(var + EPS)
    return xc * rstd, rstd


def norm_back(dn, xhat, rstd, gain):
    gp = dn * gain
    m1 = jnp.sum(gp, axis=-1, keepdims=True) * (1.0 / C)
    m2 = jnp.sum(gp * xhat, axis=-1, keepdims=True) * (1.0 / C)
    return rstd * (gp - m1 - xhat * m2)


def several(count, at_once, step):
    while count % at_once:
        at_once -= 1

    @pl.loop(0, count // at_once)
    def _(i):
        for j in range(at_once):
            step(i * at_once + j)


def head_masks(rows):
    lane = lax.broadcasted_iota(jnp.int32, (rows, LANES), 1) // HEAD
    return [lane == h for h in range(PER)]


def spread(v, masks):
    zero = jnp.zeros_like(v)
    return jnp.concatenate([jnp.where(m, v, zero) for m in masks], axis=0)


def gather_heads(full, masks):
    n = full.shape[0] // PER
    out = full[3 * n :]
    for h in (2, 1, 0):
        out = jnp.where(masks[h], full[h * n : (h + 1) * n], out)
    return out


def shifted_cols(left, right, j, step):
    if step == 0:
        return left, right
    if step == 1:
        return (
            jnp.where(j == 6, pltpu.roll(right, 6, 1), pltpu.roll(left, 7, 1)),
            pltpu.roll(right, 7, 1),
        )
    return (
        pltpu.roll(left, 1, 1),
        jnp.where(j == 0, pltpu.roll(left, 2, 1), pltpu.roll(right, 1, 1)),
    )


def canvas(ref, crop, lanes):
    base = crop * 32
    parts = [ref[pl.ds(base + 8 * w, 7), :, lanes] for w in range(4)]
    left = jnp.concatenate([parts[0], parts[2]], axis=0)
    right = jnp.concatenate([parts[1], parts[3]], axis=0)
    return left, right


def put_canvas(ref, crop, lanes, left, right, mask_ref):
    base = crop * 32
    zero = jnp.zeros((1, 8, LANES), F32)
    for w in range(4):
        side = right if w % 2 else left
        half = side[(w // 2) * 7 : (w // 2) * 7 + 7]
        rows = pl.ds(base + 8 * w, 8)
        ref[rows, :, lanes] = jnp.concatenate([half, zero], axis=0) * mask_ref[rows]


def conv_forward(u_ref, c_ref, small_ref, mask_ref, globals_, locals_):
    j14 = lax.broadcasted_iota(jnp.int32, (14, 8, LANES), 1)
    for g in range(GROUPS):
        lanes = pl.ds(g * LANES, LANES)
        taps = [small_ref[K_ROW + t : K_ROW + t + 1, lanes][None] for t in range(9)]
        shift = small_ref[V_ROW : V_ROW + 1, lanes][None]

        @pl.loop(0, globals_)
        def _(crop):
            left, right = canvas(u_ref, crop, lanes)
            zero = jnp.zeros((1, 8, LANES), F32)
            acc = [left + shift, right + shift]
            for e in (-1, 0, 1):
                for s, side in enumerate(shifted_cols(left, right, j14, e)):
                    tall = jnp.concatenate([zero, side, zero], axis=0)
                    for a in (-1, 0, 1):
                        acc[s] = acc[s] + taps[3 * (a + 1) + e + 1] * tall[1 + a : 15 + a]
            put_canvas(c_ref, crop, lanes, acc[0], acc[1], mask_ref)

        @pl.loop(0, locals_)
        def _(n):
            rows = pl.ds(globals_ * 32 + n * 8, 8)
            u = u_ref[rows, :, lanes]
            acc = u + shift
            for e in (-1, 0, 1):
                side = u if e == 0 else pltpu.roll(u, 7 if e == 1 else 1, 1)
                for a in (-1, 0, 1):
                    moved = side if a == 0 else jnp.roll(side, -a, axis=0)
                    acc = acc + taps[3 * (a + 1) + e + 1] * moved
            c_ref[rows, :, lanes] = acc * mask_ref[rows]


def conv_backward(d_ref, u_ref, du_ref, small_ref, acc_ref, globals_, locals_):
    j14 = lax.broadcasted_iota(jnp.int32, (14, 8, LANES), 1)
    for g in range(GROUPS):
        lanes = pl.ds(g * LANES, LANES)
        taps = [small_ref[K_ROW + t : K_ROW + t + 1, lanes][None] for t in range(9)]
        nothing = tuple(jnp.zeros((8, LANES), F32) for _ in range(10))

        def one_crop(crop, sums):
            sums = list(sums)
            left, right = canvas(d_ref, crop, lanes)
            own = canvas(u_ref, crop, lanes)
            zero = jnp.zeros((1, 8, LANES), F32)
            acc = [left, right]
            sums[9] = sums[9] + jnp.sum(left + right, axis=0)
            for e in (-1, 0, 1):
                for s, side in enumerate(shifted_cols(left, right, j14, -e)):
                    tall = jnp.concatenate([zero, side, zero], axis=0)
                    for a in (-1, 0, 1):
                        t = 3 * (a + 1) + e + 1
                        moved = tall[1 - a : 15 - a]
                        acc[s] = acc[s] + taps[t] * moved
                        sums[t] = sums[t] + jnp.sum(own[s] * moved, axis=0)
            base = crop * 32
            for w in range(4):
                side = acc[w % 2]
                half = side[(w // 2) * 7 : (w // 2) * 7 + 7]
                du_ref[pl.ds(base + 8 * w, 8), :, lanes] = jnp.concatenate([half, zero], axis=0)
            return tuple(sums)

        def one_local(n, sums):
            sums = list(sums)
            rows = pl.ds(globals_ * 32 + n * 8, 8)
            d = d_ref[rows, :, lanes]
            own = u_ref[rows, :, lanes]
            acc = d
            sums[9] = sums[9] + jnp.sum(d, axis=0)
            for e in (-1, 0, 1):
                side = d if e == 0 else pltpu.roll(d, 7 if e == -1 else 1, 1)
                for a in (-1, 0, 1):
                    t = 3 * (a + 1) + e + 1
                    moved = side if a == 0 else jnp.roll(side, a, axis=0)
                    acc = acc + taps[t] * moved
                    sums[t] = sums[t] + jnp.sum(own * moved, axis=0)
            du_ref[rows, :, lanes] = acc
            return tuple(sums)

        sums = lax.fori_loop(0, globals_, one_crop, nothing)
        sums = lax.fori_loop(0, locals_, one_local, sums)
        for t in range(10):
            acc_ref[t, :, lanes] = sums[t]


def spatial_forward(q_ref, k_ref, v_ref, mask_ref, o_ref, p_ref, windows):
    masks = head_masks(CELL)

    def step(w):
        rows = pl.ds(w * CELL, CELL)
        m = mask_ref[rows, :]
        valid = jnp.concatenate([m, m], axis=1) > 0.5
        for g in range(GROUPS):
            lanes = pl.ds(g * LANES, LANES)
            s = mm_nt(k_ref[rows, lanes], spread(q_ref[rows, lanes], masks))
            s = jnp.where(valid, s * SCALE, -1e9)
            e = jnp.exp(s - jnp.max(s, axis=0, keepdims=True))
            p = (e / jnp.sum(e, axis=0, keepdims=True)).astype(BF)
            p_ref[w, g] = p
            o_ref[rows, lanes] = gather_heads(mm_tn(p, v_ref[rows, lanes]), masks).astype(BF)

    several(windows, MIX_UNROLL, step)


def plus(a, b):
    return b if a is None else a + b


def pick(count, at_once):
    while count % at_once:
        at_once -= 1
    return at_once


def spatial_backward(q_ref, k_ref, v_ref, p_ref, do_ref, dq_ref, dk_ref, dv_ref, acc_ref, s_ref, windows, wait, send):
    masks = head_masks(CELL)
    lanes = [pl.ds(g * LANES, LANES) for g in range(GROUPS)]
    at_once = pick(windows, MIX_UNROLL)
    for ready in wait:
        ready()

    @pl.loop(0, windows // at_once)
    def _(i):
        sums = [None] * GROUPS
        for w in [i * at_once + j for j in range(at_once)]:
            rows = pl.ds(w * CELL, CELL)
            for g in range(GROUPS):
                p = p_ref[w, g]
                dos = spread(do_ref[rows, lanes[g]], masks)
                dp = mm_nt(v_ref[rows, lanes[g]], dos)
                pf = p.astype(F32)
                total = jnp.sum(pf * dp, axis=0, keepdims=True)
                ds = (pf * (dp - total) * SCALE).astype(BF)
                s_ref[w, g] = ds
                dv = mm(p, dos)
                sums[g] = plus(sums[g], fold8(dv))
                dv_ref[rows, lanes[g]] = dv.astype(BF)
                dk_ref[rows, lanes[g]] = mm(ds, spread(q_ref[rows, lanes[g]], masks)).astype(BF)
        for g in range(GROUPS):
            acc_ref[1, :, lanes[g]] += sums[g]

    send[1]()
    send[2]()

    @pl.loop(0, windows // at_once)
    def _(i):
        sums = [None] * GROUPS
        for w in [i * at_once + j for j in range(at_once)]:
            rows = pl.ds(w * CELL, CELL)
            for g in range(GROUPS):
                dq = gather_heads(mm_tn(s_ref[w, g], k_ref[rows, lanes[g]]), masks)
                sums[g] = plus(sums[g], fold8(dq))
                dq_ref[rows, lanes[g]] = dq.astype(BF)
        for g in range(GROUPS):
            acc_ref[0, :, lanes[g]] += sums[g]

    send[0]()


def same_head():
    a = lax.broadcasted_iota(jnp.int32, (LANES, LANES), 0) // HEAD
    b = lax.broadcasted_iota(jnp.int32, (LANES, LANES), 1) // HEAD
    return a == b


def over_crops(globals_, locals_, step):
    several(globals_, 3, lambda n: step(n, n * 4 * CELL, 4 * CELL))
    several(locals_, 9, lambda n: step(globals_ + n, globals_ * 4 * CELL + n * CELL, CELL))


def channel_forward(q_ref, k_ref, v_ref, mask_ref, o_ref, p_ref, globals_, locals_):
    same = same_head()
    lanes = [pl.ds(g * LANES, LANES) for g in range(GROUPS)]

    def weigh(n, start, count):
        rows = pl.ds(start, count)
        m = mask_ref[rows, :].astype(BF)
        for g in range(GROUPS):
            s = mm_tn(v_ref[rows, lanes[g]], k_ref[rows, lanes[g]] * m)
            s = jnp.where(same, s * SCALE, -jnp.inf)
            e = jnp.exp(s - jnp.max(s, axis=0, keepdims=True))
            p_ref[n, g] = (e / jnp.sum(e, axis=0, keepdims=True)).astype(BF)

    over_crops(globals_, locals_, weigh)

    def step(n, start, count):
        rows = pl.ds(start, count)
        for g in range(GROUPS):
            o_ref[rows, lanes[g]] = mm(q_ref[rows, lanes[g]], p_ref[n, g]).astype(BF)

    over_crops(globals_, locals_, step)


def channel_backward(
    q_ref, k_ref, v_ref, mask_ref, p_ref, do_ref, dq_ref, dk_ref, dv_ref, acc_ref, s_ref, globals_, locals_, wait, send
):
    lanes = [pl.ds(g * LANES, LANES) for g in range(GROUPS)]

    def slope(n, start, count):
        rows = pl.ds(start, count)
        for g in range(GROUPS):
            dp = mm_tn(q_ref[rows, lanes[g]], do_ref[rows, lanes[g]])
            pf = p_ref[n, g].astype(F32)
            total = jnp.sum(pf * dp, axis=0, keepdims=True)
            s_ref[n, g] = (pf * (dp - total) * SCALE).astype(BF)

    for ready in wait[:3]:
        ready()
    over_crops(globals_, locals_, slope)
    for ready in wait[3:]:
        ready()

    def step(n, start, count):
        rows = pl.ds(start, count)
        mf = mask_ref[rows, :]
        m = mf.astype(BF)
        for g in range(GROUPS):
            ds = s_ref[n, g]
            dq = mm_nt(do_ref[rows, lanes[g]], p_ref[n, g])
            dk = mm(v_ref[rows, lanes[g]], ds) * mf
            dv = mm_nt(k_ref[rows, lanes[g]] * m, ds)
            acc_ref[0, :, lanes[g]] += fold8(dq)
            acc_ref[1, :, lanes[g]] += fold8(dv)
            dq_ref[rows, lanes[g]] = dq.astype(BF)
            dk_ref[rows, lanes[g]] = dk.astype(BF)
            dv_ref[rows, lanes[g]] = dv.astype(BF)

    over_crops(globals_, locals_, step)
    for go in send:
        go()


def table_of(tabs):
    total = tabs[0].astype(F32)
    for d in range(1, tabs.shape[0]):
        total = total + tabs[d].astype(F32)
    return total


CHUNKS = 3


def crops_out(read, glob_ref, loc_ref, globals_, locals_, tmp):
    @pl.loop(0, globals_ * 2)
    def _(half):
        crop, below = half // 2, half % 2
        for i in range(WIN):
            tmp[i, 0:WIN, :] = read(half * 16 + i)[:WIN]
            tmp[i, WIN:SIDE, :] = read(half * 16 + 8 + i)[:WIN]
        for i in range(WIN):
            glob_ref[crop, below * WIN + i] = tmp[i].astype(glob_ref.dtype)

    @pl.loop(0, locals_)
    def _(n):
        for i in range(WIN):
            loc_ref[n, i] = read(globals_ * 32 + n * 8 + i)[:WIN].astype(loc_ref.dtype)


def crop_outs(globals_, locals_, kind):
    return [shape((globals_, SIDE, SIDE, C), kind), shape((locals_, WIN, WIN, C), kind)]


def chunks_of(rows):
    size = rows // CHUNKS
    return [pl.ds(i * size, size) for i in range(CHUNKS)]


def tiles_of(here):
    return pl.ds(here.start // 8, here.size // 8)


def attention_forward(sizes, kind, me, u, mask, bufs, first):
    globals_, locals_, shards = sizes
    windows = 4 * globals_ + locals_
    rows = windows * CELL
    part = C // shards
    chunks = chunks_of(rows)

    def kernel(me_ref, feeds, sends, held, packs, w, tabs, sem, sem2):
        r_out, small_out, c_out, n_out, q_out, k_out, v_out, o_out, p_out = sends[:9]
        r_ref, small_ref, c_ref, n_ref, q_ref, k_ref, v_ref, o_ref, p_ref = [v.ref for v in sends[:9]]
        feeds[0].start()
        tab = start_weights(held, me_ref, [(first + 4 * part, TAB, lambda d: tabs.at[d])], sem2)
        if mask is not None:
            feeds[1].start()
        plan = [(first + i * part, part, rows_of(w, i, part)) for i in range(4)]
        copies = start_weights(held, me_ref, plan, sem)
        if mask is not None:
            u_ref, mask_ref = feeds[0].wait(), feeds[1].wait()
        else:
            u_ref, mask_ref = sends[9].ref, sends[10].ref
            at = lax.broadcasted_iota(jnp.int32, (CELL, LANES), 0)
            for i in range(windows):
                inside = jnp.logical_and(at // 8 < me_ref[1 + 2 * i], at % 8 < me_ref[2 + 2 * i])
                mask_ref[i * CELL : (i + 1) * CELL, :] = jnp.where(inside, 1.0, 0.0)
            sends[10].start()
            x_ref = feeds[0].wait()

            def masked(i):
                here = pl.ds(i * CELL, CELL)
                x = x_ref[here, :].astype(F32) * wide(mask_ref[here, :])
                u_ref[pl.ds(i * 8, 8)] = x.reshape(8, 8, C)

            several(windows, 3, masked)
            sends[9].start()
        for copy in tab:
            copy.wait()
        small_ref[...] = table_of(tabs)
        small_out.start()
        conv_forward(u_ref, c_ref, small_ref, mask_ref.reshape(windows * 8, 8, LANES), globals_, locals_)
        c_out.start()
        gain = small_ref[G_ROW : G_ROW + 1]
        shift = small_ref[V_ROW + 1 : V_ROW + 2]

        def step(i):
            x = c_ref[pl.ds(i * 8, 8)].reshape(CELL, C)
            xhat, _ = norm_parts(x)
            n_ref[pl.ds(i * CELL, CELL), :] = (xhat * gain + shift).astype(BF)

        several(windows, NORM_UNROLL, step)
        n_out.start()
        for copy in copies:
            copy.wait()
        for here in chunks:
            n1 = n_ref[here, :]
            q_ref[here, :] = (mm(n1, w[0]) + small_ref[V_ROW + 2 : V_ROW + 3]).astype(BF)
            k_ref[here, :] = mm(n1, w[1]).astype(BF)
            v_ref[here, :] = (mm(n1, w[2]) + small_ref[V_ROW + 3 : V_ROW + 4]).astype(BF)
        for send in (q_out, k_out, v_out):
            send.start()
        if kind == 0:
            spatial_forward(q_ref, k_ref, v_ref, mask_ref, o_ref, p_ref, windows)
        else:
            channel_forward(q_ref, k_ref, v_ref, mask_ref, o_ref, p_ref, globals_, locals_)
        p_out.start()
        o_out.start()
        for i, here in enumerate(chunks):
            c = c_ref[tiles_of(here)].reshape(here.size, C)
            r_ref[here, :] = c + mm(o_ref[here, :], w[3]) + small_ref[V_ROW + 4 : V_ROW + 5]
            r_out.start(i, here)

    low = shape((rows, C), BF)
    probs = (windows, GROUPS, CELL, PER * CELL) if kind == 0 else (globals_ + locals_, GROUPS, LANES, LANES)
    outs = [
        shape((rows, C), F32), shape((TAB, C), F32), shape((windows * 8, 8, C), F32),
        low, low, low, low, low, shape(probs, BF),
    ]
    scratch = [
        pltpu.VMEM((4, C, C), BF),
        pltpu.VMEM((shards, TAB, C), BF),
        pltpu.SemaphoreType.DMA,
        pltpu.SemaphoreType.DMA,
    ]
    if mask is None:
        outs += [shape((windows * 8, 8, C), F32), shape((rows, LANES), F32)]
    ins = [u] if mask is None else [u, mask]
    return call(kernel, me, ins, outs, held=bufs, scratch=scratch, micros=FORWARD)


def start_ffn_weights(held, me_ref, where, part, deep, w1, w2, sem):
    n1, first1, n2, first2 = where
    plan1 = [(first1 + i * part, part, rows_of(w1, i, part)) for i in range(FF // C)]
    plan2 = [(first2, deep, lambda d: w2.at[pl.ds(pl.multiple_of(d * deep, deep), deep), :])]
    if n2 == 0:
        return start_weights(held[:n1], me_ref, plan1 + plan2, sem)
    return start_weights(held[:n1], me_ref, plan1, sem) + start_weights(held[n1 : n1 + n2], me_ref, plan2, sem)


def ffn_forward(sizes, me, r, mask, small, bufs, where, last):
    globals_, locals_, shards = sizes
    windows = 4 * globals_ + locals_
    rows = windows * CELL
    part = C // shards
    deep = FF // shards
    chunks = chunks_of(rows)

    def kernel(me_ref, feeds, sends, held, packs, w1, w2, sem, *more):
        r_in, m_in, small_in = feeds
        n_out, g_out, s_out = sends[:3]
        n_ref, g_ref, s_ref = [v.ref for v in sends[:3]]
        x_ref = more[0] if last else sends[3].ref
        small_in.start()
        r_in.start()
        copies = start_ffn_weights(held, me_ref, where, part, deep, w1, w2, sem)
        m_in.start()
        small_ref = small_in.wait()
        gain = small_ref[G_ROW + 1 : G_ROW + 2]
        shift = small_ref[V_ROW + 5 : V_ROW + 6]
        r_ref = r_in.wait()

        def step(i):
            here = pl.ds(i * CELL, CELL)
            xhat, _ = norm_parts(r_ref[here, :])
            n_ref[here, :] = (xhat * gain + shift).astype(BF)

        several(windows, NORM_UNROLL, step)
        n_out.start()
        mask_ref = m_in.wait()
        for copy in copies:
            copy.wait()
        for i, here in enumerate(chunks):
            n2 = n_ref[here, :]
            for t in range(FF // C):
                h = mm(n2, w1[t]) + small_ref[B_ROW + t : B_ROW + t + 1]
                h2 = h * h
                a = 0.5 + 0.5 * jnp.tanh(h * (0.7978845608 + (0.7978845608 * 0.044715) * h2))
                g = h * a
                slope = a + (2.0 * g) * (1.0 - a) * (0.7978845608 + (3 * 0.7978845608 * 0.044715) * h2)
                g_ref[here, t * C : (t + 1) * C] = g.astype(BF)
                s_ref[here, t * C : (t + 1) * C] = slope.astype(BF)
            g_out.start(i, here)
            s_out.start(i, here)
            y = r_ref[here, :] + mm(g_ref[here, :], w2[...]) + small_ref[V_ROW + 6 : V_ROW + 7]
            x_ref[here, :] = y * wide(mask_ref[here, :])
            if not last:
                sends[3].start(i, here)
        if last:
            crops_out(
                lambda tile: x_ref[pl.ds(pl.multiple_of(tile * 8, 8), 8), :],
                sends[3].ref, sends[4].ref, globals_, locals_, more[1],
            )
            sends[3].start()
            sends[4].start()

    high = shape((rows, FF), BF)
    outs = [shape((rows, C), BF), high, high]
    outs += crop_outs(globals_, locals_, BF) if last else [shape((rows, C), F32)]
    scratch = [pltpu.VMEM((FF // C, C, C), BF), pltpu.VMEM((FF, C), BF), pltpu.SemaphoreType.DMA]
    if last:
        scratch += [pltpu.VMEM((rows, C), F32), pltpu.VMEM((WIN, SIDE, C), F32)]
    return call(kernel, me, [r, mask, small], outs, held=bufs, scratch=scratch, micros=FORWARD)


def pack_outs(shards, count, relative):
    if relative:
        return [shape((4, count, C), BF)] * 2
    return [shape((shards, count, C), BF)]


def send_pack(dw, outs, rows, sem):
    each = len(outs) == 2
    copies = []
    for i, out in enumerate(outs):
        src = dw.at[pl.ds(4 * i, 4), rows] if each else dw.at[:, rows]
        copies.append(pltpu.make_async_copy(src, out.at[:, rows], sem))
    for copy in copies:
        copy.start()
    return copies


def ffn_backward(sizes, me, relative, dy, n2, g, slope, mask, w_ffn, where, deps):
    globals_, locals_, shards = sizes
    windows = 4 * globals_ + locals_
    rows = windows * CELL
    part = C // shards
    deep = FF // shards
    count = 4 * part + deep
    chunks = chunks_of(rows)
    packs = pack_outs(shards, count, relative)
    n_ffn = len(w_ffn)

    def kernel(me_ref, feeds, sends, held, dw_out, w1, w2, dw, dyl, dh, acc, acc1, sem, sem2):
        dy_in, n_in, g_in, s_in, m_in = feeds
        dn_out, ds_out = sends
        dn_ref, ds_ref = [v.ref for v in sends]
        for i, here in enumerate(chunks):
            dy_in.start(i, here)
        m_in.start()
        copies = start_ffn_weights(held[:n_ffn], me_ref, where, part, deep, w1, w2, sem)
        for i, here in enumerate(chunks):
            s_in.start(i, here)
        n_in.start()
        g_in.start()
        acc[...] = jnp.zeros_like(acc)
        acc1[...] = jnp.zeros_like(acc1)
        dy_in.wait_all()
        dy_ref, mask_ref = dy_in.ref, m_in.wait()

        def step(i):
            here = pl.ds(i * CELL, CELL)
            d = dy_ref[here, :] * wide(mask_ref[here, :])
            dyl[here, :] = d.astype(BF)
            acc[...] += fold8(d)

        several(windows, NORM_UNROLL, step)
        for copy in copies:
            copy.wait()
        for i, here in enumerate(chunks):
            s_ref = s_in.wait(i)
            for t in range(FF // C):
                cols = slice(t * C, (t + 1) * C)
                d = mm_nt(dyl[here, :], w2[cols, :]) * s_ref[here, cols].astype(F32)
                acc1[:, cols] += fold8(d)
                dh[here, cols] = d.astype(BF)
            dn = None
            for t in range(FF // C):
                one = mm_nt(dh[here, t * C : (t + 1) * C], w1[t])
                dn = one if dn is None else dn + one
            dn_ref[here, :] = dn
            dn_out.start(i, here)

        n_ref = n_in.wait()
        g_ref = g_in.wait()
        going = []
        for t in range(FF // C):
            cols = slice(t * C, (t + 1) * C)
            one = mm_tn(n_ref[...], dh[:, cols]).astype(BF)
            for d in range(shards):
                dw[slot_of(d, me_ref, relative), t * part : (t + 1) * part, :] = one[d * part : (d + 1) * part]
            going += send_pack(dw, dw_out, pl.ds(t * part, part), sem2)
        for t in range(FF // C):
            cols = slice(t * C, (t + 1) * C)
            two = mm_tn(g_ref[:, cols], dyl[...]).astype(BF)
            for d in range(C // deep):
                here = pl.ds(4 * part, deep)
                dw[slot_of(t * (C // deep) + d, me_ref, relative), here, :] = two[d * deep : (d + 1) * deep]
        going += send_pack(dw, dw_out, pl.ds(4 * part, deep), sem2)
        ds_ref[0:1, :] = jnp.sum(acc[...], axis=0, keepdims=True)
        for t in range(FF // C):
            ds_ref[1 + t : 2 + t, :] = jnp.sum(acc1[:, t * C : (t + 1) * C], axis=0, keepdims=True)
        ds_ref[5:8, :] = jnp.zeros((3, C), F32)
        ds_out.start()
        for copy in going:
            copy.wait()

    outs = [shape((rows, C), F32), shape((8, C), F32)]
    scratch = [
        pltpu.VMEM((FF // C, C, C), BF),
        pltpu.VMEM((FF, C), BF),
        pltpu.VMEM((shards, count, C), BF),
        pltpu.VMEM((rows, C), BF),
        pltpu.VMEM((rows, FF), BF),
        pltpu.VMEM((8, C), F32),
        pltpu.VMEM((8, FF), F32),
        pltpu.SemaphoreType.DMA,
        pltpu.SemaphoreType.DMA,
    ]
    return call(
        kernel, me, [dy, n2, g, slope, mask], outs, held=[*w_ffn, *deps], packs=packs,
        scratch=scratch, micros=BACKWARD,
    )


def norm_two_backward(sizes, me, dn, dy, r, mask, small, w_att, first, deps):
    globals_, locals_, shards = sizes
    windows = 4 * globals_ + locals_
    rows = windows * CELL
    part = C // shards
    chunks = chunks_of(rows)
    each = chunks[0].size // CELL

    def kernel(me_ref, feeds, sends, held, packs, wp, acc, sem):
        dn_in, dy_in, r_in, m_in, small_in = feeds
        dn_ref, dy_ref, r_ref, mask_ref, small_ref = [v.ref for v in feeds]
        dr_out, drl_out, do_out, ds_out = sends
        dr_ref, drl, do_ref, ds_ref = [v.ref for v in sends]
        small_in.start()
        for i, here in enumerate(chunks):
            for feed in (r_in, dn_in, dy_in, m_in):
                feed.start(i, here)
            if i == 0:
                copies = start_weights(
                    held[: len(w_att)], me_ref, [(first + 3 * part, part, rows_of(wp, 0, part))], sem
                )
        acc[...] = jnp.zeros_like(acc)
        small_in.wait()
        gain = small_ref[G_ROW + 1 : G_ROW + 2]
        for i, here in enumerate(chunks):
            for feed in (r_in, dn_in, dy_in, m_in):
                feed.wait(i)
            sums = [None] * 3
            for w in range(i * each, (i + 1) * each):
                at = pl.ds(w * CELL, CELL)
                dn = dn_ref[at, :]
                xhat, rstd = norm_parts(r_ref[at, :])
                dr = norm_back(dn, xhat, rstd, gain) + dy_ref[at, :] * wide(mask_ref[at, :])
                sums = [plus(a, fold8(v)) for a, v in zip(sums, (dn * xhat, dn, dr))]
                dr_ref[at, :] = dr
                drl[at, :] = dr.astype(BF)
            for t in range(3):
                acc[t] += sums[t]
            dr_out.start(i, here)
            drl_out.start(i, here)
            if i == 0:
                for copy in copies:
                    copy.wait()
            do_ref[here, :] = mm_nt(drl[here, :], wp[0]).astype(BF)
            do_out.start(i, here)
        for t in range(3):
            ds_ref[t : t + 1, :] = jnp.sum(acc[t], axis=0, keepdims=True)
        ds_ref[3:8, :] = jnp.zeros((5, C), F32)
        ds_out.start()

    low = shape((rows, C), BF)
    return call(
        kernel, me, [dn, dy, r, mask, small], [shape((rows, C), F32), low, low, shape((8, C), F32)],
        held=[*w_att, *deps], micros=BACKWARD,
        scratch=[pltpu.VMEM((1, C, C), BF), pltpu.VMEM((3, 8, C), F32), pltpu.SemaphoreType.DMA],
    )


def norm_one_stage(rows, feeds, gain, w, dq, dk, dv, acc, dc_out, ds_out):
    dr_in, c_in, m_in = feeds
    dr_ref, c_ref, mask_ref = [v.ref for v in feeds]
    dc, ds_ref = dc_out.ref, ds_out.ref
    chunks = chunks_of(rows)
    each = chunks[0].size // CELL
    for i, here in enumerate(chunks):
        total = mm_nt(dq(i)[here, :], w[0]) + mm_nt(dk(i)[here, :], w[1]) + mm_nt(dv(i)[here, :], w[2])
        for feed in feeds:
            feed.wait(i)
        sums = [None] * 2
        for j in range(each):
            window = i * each + j
            at, tiles = pl.ds(window * CELL, CELL), pl.ds(window * 8, 8)
            d = total[j * CELL : (j + 1) * CELL]
            xhat, rstd = norm_parts(c_ref[tiles].reshape(CELL, C))
            sums = [plus(a, fold8(v)) for a, v in zip(sums, (d * xhat, d))]
            full = norm_back(d, xhat, rstd, gain) + dr_ref[at, :]
            dc[tiles] = (full * wide(mask_ref[at, :])).reshape(8, 8, C)
        for t in range(2):
            acc[t] += sums[t]
        dc_out.start(i, tiles_of(here))
    for t in range(2):
        ds_ref[t : t + 1, :] = jnp.sum(acc[t], axis=0, keepdims=True)
    ds_ref[2:8, :] = jnp.zeros((6, C), F32)
    ds_out.start()


def start_norm_one(rows, feeds):
    dr_in, c_in, m_in = feeds
    for i, here in enumerate(chunks_of(rows)):
        dr_in.start(i, here)
        m_in.start(i, here)
        c_in.start(i, tiles_of(here))


def mix_backward(sizes, kind, me, relative, q, k, v, p, do, n1, o, drl, mask, rest, deps):
    globals_, locals_, shards = sizes
    windows = 4 * globals_ + locals_
    rows = windows * CELL
    part = C // shards
    packs = pack_outs(shards, 4 * part, relative)
    low = shape((rows, C), BF)
    eight = shape((8, C), F32)

    def kernel(me_ref, feeds, sends, held, dw_out, acc, slope, dw, sem, *more):
        q_in, k_in, v_in, p_in, do_in, n_in, o_in, drl_in, m_in = feeds[:9]
        q_ref, k_ref, v_ref, p_ref, do_ref, n_ref, o_ref, drl, mask_ref = [v.ref for v in feeds[:9]]
        if rest is None:
            dq, dk, dv = [v.ref for v in sends[:3]]
            go = [send.start for send in sends[:3]]
            ds_out = sends[3]
        else:
            dq, dk, dv, w, acc1, sem_w = more
            go = [lambda: None] * 3
            dc_out, ds_out, one_out = sends
        ds_ref = ds_out.ref
        order = (v_in, do_in, p_in, q_in, k_in) if kind == 0 else (q_in, do_in, p_in, v_in, k_in)
        waits = [feed.wait for feed in order]
        for feed in order:
            feed.start()
        if rest is None:
            m_in.start()
            waits.append(m_in.wait)
        else:
            for i, here in enumerate(chunks_of(rows)):
                m_in.start(i, here)
            plan = [(rest[4] + i * part, part, rows_of(w, i, part)) for i in range(3)]
            copies = start_weights(held[: len(rest[3])], me_ref, plan, sem_w)
            dr_in, c_in, small_in = feeds[9:]
            small_in.start()
            waits += [m_in.wait_all, small_in.wait]
        for feed in (n_in, o_in, drl_in):
            feed.start()
        if rest is not None:
            dr_in.start()
            c_in.start()
        acc[...] = jnp.zeros_like(acc)
        if kind == 0:
            spatial_backward(q_ref, k_ref, v_ref, p_ref, do_ref, dq, dk, dv, acc, slope, windows, waits, go)
        else:
            channel_backward(
                q_ref, k_ref, v_ref, mask_ref, p_ref, do_ref, dq, dk, dv, acc, slope, globals_, locals_, waits, go
            )
        for t in range(2):
            ds_ref[t : t + 1, :] = jnp.sum(acc[t], axis=0, keepdims=True)
        ds_ref[2:8, :] = jnp.zeros((6, C), F32)
        ds_out.start()
        for feed in (n_in, o_in, drl_in):
            feed.wait()
        going = []
        for i, left, right in ((1, n_ref, dk), (2, n_ref, dv), (0, n_ref, dq), (3, o_ref, drl)):
            one = mm_tn(left[...], right[...]).astype(BF)
            for d in range(shards):
                dw[slot_of(d, me_ref, relative), i * part : (i + 1) * part, :] = one[d * part : (d + 1) * part]
            going += send_pack(dw, dw_out, pl.ds(i * part, part), sem)
        if rest is not None:
            acc1[...] = jnp.zeros_like(acc1)
            for copy in copies:
                copy.wait()
            dr_in.wait()
            c_in.wait()
            feeds_one = [Ready(v.ref) for v in (dr_in, c_in, m_in)]
            gain = small_in.ref[G_ROW : G_ROW + 1]
            norm_one_stage(
                rows, feeds_one, gain, w, lambda i: dq, lambda i: dk, lambda i: dv, acc1, dc_out, one_out
            )
        for copy in going:
            copy.wait()

    scratch = [
        pltpu.VMEM((2, 8, C), F32), pltpu.VMEM(p.shape, BF), pltpu.VMEM((shards, 4 * part, C), BF),
        pltpu.SemaphoreType.DMA,
    ]
    ins = [q, k, v, p, do, n1, o, drl, mask]
    if rest is None:
        outs, held = [low, low, low, eight], list(deps)
    else:
        outs, held = [shape((windows * 8, 8, C), F32), eight, eight], [*rest[3], *deps]
        ins += [rest[0], rest[1], rest[2]]
        scratch += [pltpu.VMEM((rows, C), BF)] * 3
        scratch += [pltpu.VMEM((3, C, C), BF), pltpu.VMEM((2, 8, C), F32), pltpu.SemaphoreType.DMA]
    return call(kernel, me, ins, outs, held=held, packs=packs, scratch=scratch, micros=BACKWARD)


class Ready:
    def __init__(self, ref):
        self.ref = ref

    def wait(self, k=0):
        return self.ref


def norm_one_backward(sizes, me, dr, c, dq, dk, dv, mask, small, bufs, first, deps):
    globals_, locals_, shards = sizes
    windows = 4 * globals_ + locals_
    rows = windows * CELL
    part = C // shards

    def kernel(me_ref, feeds, sends, held, packs, w, acc, sem):
        dr_in, c_in, dq_in, dk_in, dv_in, m_in, small_in = feeds
        plan = [(first + i * part, part, rows_of(w, i, part)) for i in range(3)]
        copies = start_weights(held[: len(bufs)], me_ref, plan, sem)
        small_in.start()
        for i, here in enumerate(chunks_of(rows)):
            for feed in (dq_in, dk_in, dv_in):
                feed.start(i, here)
        start_norm_one(rows, (dr_in, c_in, m_in))
        acc[...] = jnp.zeros_like(acc)
        gain = small_in.wait()[G_ROW : G_ROW + 1]
        for copy in copies:
            copy.wait()
        norm_one_stage(rows, (dr_in, c_in, m_in), gain, w, dq_in.wait, dk_in.wait, dv_in.wait, acc, *sends)

    return call(
        kernel, me, [dr, c, dq, dk, dv, mask, small], [shape((windows * 8, 8, C), F32), shape((8, C), F32)],
        held=[*bufs, *deps], micros=BACKWARD,
        scratch=[pltpu.VMEM((3, C, C), BF), pltpu.VMEM((2, 8, C), F32), pltpu.SemaphoreType.DMA],
    )


def position_backward(sizes, me, dc, u, mask, small, ds_ffn, ds_two, ds_mix, ds_one, last, deps):
    globals_, locals_, _ = sizes
    windows = 4 * globals_ + locals_

    def kernel(me_ref, feeds, sends, held, packs, acck, *more):
        dc_ref, u_ref, small_ref, ffn, two, mix, one = [v.ref for v in feeds[:7]]
        tab = sends[0].ref
        du_ref = more[0] if last else sends[1].ref
        for feed in feeds:
            feed.start()
        for feed in feeds:
            feed.wait()
        conv_backward(dc_ref, u_ref, du_ref, small_ref, acck, globals_, locals_)
        if last:
            mask_ref = feeds[7].ref

            def read(tile):
                here = pl.ds(pl.multiple_of(tile * 8, 8), 8)
                return du_ref[tile] * wide(mask_ref[here, :])

            crops_out(read, sends[1].ref, sends[2].ref, globals_, locals_, more[1])
            sends[2].start()
        sends[1].start()
        rows_ = [jnp.sum(acck[t], axis=0, keepdims=True) for t in range(10)]
        rows_ += [one[1:2, :], mix[0:1, :], mix[1:2, :], two[2:3, :], two[1:2, :], ffn[0:1, :]]
        rows_ += [one[0:1, :], two[0:1, :]]
        rows_ += [ffn[1 + t : 2 + t, :] for t in range(FF // C)]
        tab[...] = jnp.zeros_like(tab)
        for t, row in enumerate(rows_):
            tab[t : t + 1, :] = row
        sends[0].start()

    full = (windows * 8, 8, C)
    ins = [dc, u, small, ds_ffn, ds_two, ds_mix, ds_one]
    outs = [shape((TAB, C), F32)]
    scratch = [pltpu.VMEM((10, 8, C), F32)]
    if last:
        ins.append(mask)
        outs += crop_outs(globals_, locals_, F32)
        scratch += [pltpu.VMEM(full, F32), pltpu.VMEM((WIN, SIDE, C), F32)]
    else:
        outs.append(shape(full, F32))
    return call(kernel, me, ins, outs, held=deps, scratch=scratch, micros=BACKWARD)


def join(values, deps):
    values, deps = list(values), list(deps)

    def kernel(*refs):
        pass

    return pl.pallas_call(
        kernel,
        out_shape=[shape(v.shape, v.dtype) for v in values],
        in_specs=[HELD] * (len(values) + len(deps)),
        out_specs=[HELD] * len(values),
        input_output_aliases={i: i for i in range(len(values))},
    )(*values, *deps)


def to_cells(glob, loc):
    count = glob.shape[0]
    wins = glob.reshape(count, 2, WIN, 2, WIN, C).transpose(0, 1, 3, 2, 4, 5).reshape(count * 4, WIN, WIN, C)
    both = jnp.concatenate([wins, loc], axis=0)
    return jnp.pad(both, ((0, 0), (0, 1), (0, 1), (0, 0)))


def place_and_extents(index, extent, globals_):
    sizes = jnp.concatenate([jnp.full((globals_ * 4, 2), WIN, jnp.int32), extent.astype(jnp.int32)], axis=0)
    return jnp.concatenate([index.astype(jnp.int32).reshape(1), sizes.reshape(-1)])


def layer(sizes, me, tokens, cotangent, plan):
    windows = 4 * sizes[0] + sizes[1]
    rows = windows * CELL
    dy = cotangent.reshape(rows, C)
    kept = []
    places = []
    mask = None
    u = tokens.reshape(rows, C)
    for b in range(2):
        att, att_first = plan.att_weights(b, u)
        r, small, *saved = attention_forward(sizes, b, me, u, mask, att, att_first)
        if b == 0:
            *saved, u, mask = saved
        ffn, where = plan.ffn_weights(b, r)
        places.append((att, att_first, ffn, where))
        n2, g, slope, *out = ffn_forward(sizes, me, r, mask, small, ffn, where, b == 1)
        kept.append((u, r, small, saved, (n2, g, slope)))
        if b == 0:
            u = out[0].reshape(windows * 8, 8, C)
    tables = [None, None]
    for b in (1, 0):
        u, r, small, (c, n1, q, k, v, o, p), (n2, g, slope) = kept[b]
        att, att_first, ffn, where = places[b]
        rel_ffn, rel_att = plan.relative[b]
        dn, ds_ffn, *dw = ffn_backward(sizes, me, rel_ffn, dy, n2, g, slope, mask, ffn, where, [])
        deps = plan.step(b, 0, dn, dw)
        dr, drl, do, ds_two = norm_two_backward(sizes, me, dn, dy, r, mask, small, att, att_first, deps)
        deps = plan.step(b, 1, dr)
        mixed = (q, k, v, p, do, n1, o, drl, mask)
        rest = (dr, c, small, att, att_first)
        dc, ds_mix, ds_one, *dw = mix_backward(sizes, b, me, rel_att, *mixed, rest, deps)
        deps = plan.step(b, 2, dc, dw)
        tables[b], *du = position_backward(
            sizes, me, dc, u, mask, small, ds_ffn, ds_two, ds_mix, ds_one, b == 0, deps
        )
        plan.step(b, 4, du[0], tables)
        if b == 1:
            dy = du[0].reshape(rows, C)
    return out, du


def xor(v, axis, turn):
    size = lax.axis_size(axis)
    return lax.ppermute(v, axis, [(i, i ^ turn) for i in range(size)])


def gather_near(own):
    return [own, xor(own, "fsdp", 2), xor(own, "fsdp", 4), xor(own, "fsdp", 6)]


def gather_core(near):
    out = []
    for v in near:
        out += [v, xor(v, "fsdp", 1)]
    return out


def add(*terms):
    total = terms[0].astype(F32)
    for term in terms[1:]:
        total = total + term.astype(F32)
    return total.astype(BF)


def to_core(pack):
    return xor(pack[1], "fsdp", 1)


def to_chips(parts):
    return [xor(v, "fsdp", 2 * i + 2) for i, v in enumerate(parts[1:])]


def core_sums(pack, got):
    return [add(pack[0][i], got[i]) for i in range(4)]


def own_lanes(table):
    shards, index = lax.axis_size("fsdp"), lax.axis_index("fsdp")
    part, deep = C // shards, FF // shards
    main = lax.dynamic_slice(table, (0, 0, index * part), (2, B_ROW, part)).reshape(2, B_ROW * part)
    bias = lax.dynamic_slice(table[:, B_ROW : B_ROW + FF // C].reshape(2, FF), (0, index * deep), (2, deep))
    return jnp.concatenate([main, bias], axis=1)


class Packs:
    def __init__(self, part, deep):
        self.part, self.deep = part, deep
        self.att, self.fc1, self.fc2 = [], [], []


class Direct:
    relative = ((True, True), (False, True))

    def __init__(self, packs):
        self.ffn_first = packs.part * 4
        self.att_first = packs.part * 4 + packs.deep
        self.att0 = gather_near(packs.att[0])
        self.ffn0 = gather_near(jnp.concatenate([packs.fc1[0], packs.fc2[0]], axis=0))
        self.whole1 = lax.all_gather(
            jnp.concatenate([packs.fc1[1], packs.fc2[1], packs.att[1]], axis=0), "fsdp", axis=0
        )

    def att_weights(self, b, u):
        if b == 0:
            return gather_core(self.att0), 0
        return [self.whole1], self.att_first

    def ffn_weights(self, b, r):
        if b == 0:
            bufs = gather_core(join(self.ffn0, [r]))
            return bufs, (len(bufs), 0, 0, self.ffn_first)
        return [self.whole1], (1, 0, 0, self.ffn_first)

    def step(self, b, stage, token, new=None):
        if (b, stage) == (1, 0):
            self.f1_own = lax.psum_scatter(new[0], "fsdp", scatter_dimension=0, tiled=True)[0]
        elif (b, stage) == (1, 2):
            self.a1, self.a1_core = new, to_core(new)
        elif (b, stage) == (1, 4):
            (core,) = join([self.a1_core], [token])
            self.a1_sums = core_sums(self.a1, core)
            self.a1_chips = to_chips(self.a1_sums)
        elif (b, stage) == (0, 0):
            self.f0, self.f0_core = new, to_core(new)
            (f1_own,) = join([self.f1_own], [token])
            self.f1_sum = Spread(f1_own)
            self.f1_sum.first()
            return [self.f1_sum.keep]
        elif (b, stage) == (0, 1):
            core, self.f1_sum.got, *chips = join([self.f0_core, self.f1_sum.got, *self.a1_chips], [token])
            self.f0_sums = core_sums(self.f0, core)
            self.f0_chips = to_chips(self.f0_sums)
            self.f1_sum.second()
            self.a1_sum = Spread(add(self.a1_sums[0], *chips))
            self.a1_sum.first()
            return [*self.f0_sums, self.f1_sum.half, self.a1_sum.keep]
        elif (b, stage) == (0, 2):
            self.a0, self.a0_core = new, to_core(new)
            *chips, self.f1_sum.got, self.a1_sum.got = join(
                [*self.f0_chips, self.f1_sum.got, self.a1_sum.got], [token]
            )
            self.f0_sum = Spread(add(self.f0_sums[0], *chips))
            self.f0_sum.first()
            self.f1_sum.third()
            self.a1_sum.second()
            return [self.f0_sum.keep, self.f1_sum.whole, self.a1_sum.half]
        elif (b, stage) == (0, 4):
            core, self.f0_sum.got, self.a1_sum.got = join([self.a0_core, self.f0_sum.got, self.a1_sum.got], [token])
            a0_sums = core_sums(self.a0, core)
            a0_chips = to_chips(a0_sums)
            self.f0_sum.second()
            self.a1_sum.third()
            table, f1_got = join([jnp.stack(new).astype(BF), self.f1_sum.got], [a0_sums[0], self.f0_sum.half])
            self.f1_sum.got = f1_got
            table = add(table, xor(table, "fsdp", 1))
            *a0_chips, self.f0_sum.got, table = join([*a0_chips, self.f0_sum.got, table], [table])
            a0_sum = Spread(add(a0_sums[0], *a0_chips))
            a0_sum.first()
            self.f0_sum.third()
            table = own_lanes(add(table, *[xor(table, "fsdp", turn) for turn in (2, 4, 6)]))
            a0_sum.got, table = join([a0_sum.got, table], [table])
            a0_sum.second()
            other, away, across = [xor(table, "dp", turn) for turn in (1, 2, 3)]
            two = [a.astype(F32) + b.astype(F32) for a, b in ((table, other), (away, across))]
            a0_sum.third()
            near = [self.f0_sum.result(), a0_sum.result()]
            self.done = [near, [self.f1_sum.result(), self.a1_sum.result()]], (two[0] + two[1]).astype(BF)
        return []

    def results(self):
        return self.done


class Spread:
    def __init__(self, v):
        n = v.shape[0] // 2
        self.low = (lax.axis_index("dp") & 1) == 0
        self.keep = jnp.where(self.low, v[:n], v[n:])
        self.send = jnp.where(self.low, v[n:], v[:n])

    def first(self):
        self.got = xor(self.send, "dp", 1)

    def second(self):
        self.half = add(self.keep, self.got)
        self.got = xor(self.half, "dp", 2)

    def third(self):
        self.whole = add(self.half, self.got)
        self.got = xor(self.whole, "dp", 1)

    def result(self):
        whole, other = self.whole, self.got
        return jnp.concatenate([jnp.where(self.low, whole, other), jnp.where(self.low, other, whole)])


class Plain:
    relative = ((False, False), (False, False))

    def __init__(self, packs):
        self.packs = [[None, None], [None, None]]
        self.first = 4 * packs.part
        self.cut = 4 * packs.part + packs.deep
        self.whole = [
            lax.all_gather(jnp.concatenate(all_, axis=0), "fsdp", axis=0)
            for all_ in zip(packs.fc1, packs.fc2, packs.att)
        ]

    def att_weights(self, b, u):
        return [self.whole[b]], self.cut

    def ffn_weights(self, b, r):
        return [self.whole[b]], (1, 0, 0, self.first)

    def step(self, b, stage, token, new=None):
        if stage in (0, 2):
            self.packs[b][stage // 2] = new[0]
        if (b, stage) == (0, 4):
            self.table = new
        return []

    def results(self):
        grads = [
            lax.psum([lax.psum_scatter(v, "fsdp", scatter_dimension=0, tiled=True)[0] for v in pair], "dp")
            for pair in self.packs
        ]
        return grads, own_lanes(lax.psum(jnp.stack(self.table).astype(BF), ("dp", "fsdp")))


def body(
    global_tokens,
    local_tokens,
    crop_extent,
    conv_weight,
    vectors,
    gains,
    qkv_weight,
    proj_weight,
    fc1_weight,
    fc1_bias,
    fc2_weight,
    global_cotangent,
    local_cotangent,
):
    shards = lax.axis_size("fsdp")
    direct = shards == 8 and lax.axis_size("dp") == 4
    part = C // shards
    globals_, locals_ = global_tokens.shape[0], local_tokens.shape[0]
    sizes = (globals_, locals_, shards)
    index = lax.axis_index("fsdp")
    me = place_and_extents(index, crop_extent, globals_)

    own_small = jnp.concatenate([conv_weight, vectors, gains], axis=1)
    own_bias = fc1_bias.reshape(2, 1, FF // shards)
    packs = Packs(part, FF // shards)
    for b in range(2):
        table = jnp.zeros((TAB, C), BF)
        table = lax.dynamic_update_slice(table, own_small[b], (0, index * part))
        start = index * (FF // shards)
        table = lax.dynamic_update_slice(table, own_bias[b], (B_ROW + start // C, start % C))
        cols = lambda w, n: [w[b][:, i * C : (i + 1) * C] for i in range(n)]
        packs.att.append(jnp.concatenate(cols(qkv_weight, 3) + [proj_weight[b], table], axis=0))
        packs.fc1.append(jnp.concatenate(cols(fc1_weight, 4), axis=0))
        packs.fc2.append(fc2_weight[b])
    plan = (Direct if direct else Plain)(packs)
    out, grad = layer(
        sizes, me,
        to_cells(global_tokens, local_tokens),
        to_cells(global_cotangent, local_cotangent).astype(F32),
        plan,
    )
    grads, table = plan.results()
    deep = FF // shards

    def cut(half, start, n):
        return jnp.stack(
            [
                jnp.concatenate([g[half][(start + i) * part : (start + i + 1) * part] for i in range(n)], axis=1)
                for g in grads
            ]
        ).astype(F32)

    table = table.astype(F32)
    main = table[:, : B_ROW * part].reshape(2, B_ROW, part)
    bias = table[:, B_ROW * part :]
    fc2 = jnp.stack([g[0][4 * part :] for g in grads]).astype(F32)
    proj = jnp.stack([g[1][3 * part :] for g in grads]).astype(F32)
    return (
        out[0], out[1], grad[0], grad[1],
        main[:, 0:9], main[:, 9:16], main[:, 16:18],
        cut(1, 0, 3), proj, cut(0, 0, 4), bias, fc2,
    )


def solution(mesh):
    crops = P(("dp", "fsdp"), None, None, None)
    last = P(None, None, "fsdp")
    middle = P(None, "fsdp", None)
    return jax.shard_map(
        body,
        mesh=mesh,
        in_specs=(
            crops, crops, P(("dp", "fsdp"), None), last, last, last, middle, middle, middle,
            P(None, "fsdp"), middle, crops, crops,
        ),
        out_specs=(
            crops, crops, crops, crops, last, last, last, middle, middle, middle, P(None, "fsdp"), middle,
        ),
        check_vma=False,
    )
```

```python
import functools

import jax
import jax.numpy as jnp
from jax import lax
from jax.experimental import pallas as pl
from jax.experimental.pallas import tpu as pltpu
from jax.sharding import PartitionSpec as P

BF = jnp.bfloat16
F32 = jnp.float32
C = 512
FF = 2048
HEAD = 32
WIN = 7
SIDE = 14
CELL = 64
LANES = 128
GROUPS = C // LANES
PER = LANES // HEAD
EPS = 1e-5
SCALE = HEAD ** -0.5
MIX_UNROLL = 7
NORM_UNROLL = 7
FORWARD, BACKWARD = 1, 3
VMEM = pl.BlockSpec(memory_space=pltpu.VMEM)
HELD = pl.BlockSpec(memory_space=pl.ANY)
NT = (((1,), (1,)), ((), ()))
TN = (((0,), (0,)), ((), ()))
K_ROW, V_ROW, G_ROW, B_ROW, TAB = 0, 9, 16, 18, 32


def mm(a, b):
    return jnp.dot(a, b, preferred_element_type=F32)


def mm_nt(a, b):
    return lax.dot_general(a, b, NT, preferred_element_type=F32)


def mm_tn(a, b):
    return lax.dot_general(a, b, TN, preferred_element_type=F32)


class Copy:
    def __init__(self, src, dst, sems, ref):
        self.src, self.dst, self.sems, self.ref = src, dst, sems, ref
        self.open = {}

    def start(self, k=0, part=None):
        src, dst = (self.src, self.dst) if part is None else (self.src.at[part], self.dst.at[part])
        self.open[k] = pltpu.make_async_copy(src, dst, self.sems.at[k])
        self.open[k].start()

    def wait(self, k=0):
        self.open.pop(k).wait()
        return self.ref

    def wait_all(self):
        for k in list(self.open):
            self.wait(k)


PARTS = 4


def call(kernel, me, ins, outs, held=(), packs=(), scratch=(), micros=1, alias=None, limit=62):
    n_in, n_out, n_held, n_pack = len(ins), len(outs), len(held), len(packs)

    def body(me_ref, *refs):
        src, refs = refs[:n_in], refs[n_in:]
        held_refs, refs = refs[:n_held], refs[n_held:]
        dst, refs = refs[:n_out], refs[n_out:]
        pack_refs, refs = refs[:n_pack], refs[n_pack:]
        in_vmem, refs = refs[:n_in], refs[n_in:]
        out_vmem, refs = refs[:n_out], refs[n_out:]
        in_sem, out_sem, refs = refs[0], refs[1], refs[2:]
        feeds = [Copy(s, v, in_sem.at[i], v) for i, (s, v) in enumerate(zip(src, in_vmem))]
        sends = [Copy(v, d, out_sem.at[i], v) for i, (d, v) in enumerate(zip(dst, out_vmem))]
        kernel(me_ref, feeds, sends, held_refs, pack_refs, *refs)
        for send in sends:
            send.wait_all()

    vmem = lambda v: pltpu.VMEM(v.shape, v.dtype)
    return pl.pallas_call(
        body,
        out_shape=list(outs) + list(packs),
        in_specs=[pl.BlockSpec(memory_space=pltpu.SMEM)] + [HELD] * (n_in + n_held),
        out_specs=[HELD] * (n_out + n_pack),
        scratch_shapes=[vmem(v) for v in ins]
        + [vmem(v) for v in outs]
        + [pltpu.SemaphoreType.DMA((max(n_in, 1), PARTS)), pltpu.SemaphoreType.DMA((max(n_out, 1), PARTS))]
        + list(scratch),
        compiler_params=pltpu.CompilerParams(vmem_limit_bytes=limit * 2**20),
        cost_estimate=pl.CostEstimate(flops=int(micros * 1.1e9), bytes_accessed=2**20, transcendentals=0),
        input_output_aliases=alias or {},
    )(me, *ins, *held)


def start_weights(bufs, me_ref, plan, sem):
    copies = []
    if len(bufs) == 1:
        sources = [(d, bufs[0].at[d]) for d in range(bufs[0].shape[0])]
    else:
        sources = [(me_ref[0] ^ k, buf) for k, buf in enumerate(bufs)]
    for d, src in sources:
        for first, rows, place in plan:
            copies.append(pltpu.make_async_copy(src.at[pl.ds(first, rows), :], place(d), sem))
    for copy in copies:
        copy.start()
    return copies


def rows_of(ref, i, rows):
    return lambda d: ref.at[i, pl.ds(pl.multiple_of(d * rows, rows), rows), :]


def slot_of(d, me_ref, relative):
    if not relative:
        return d
    turn = me_ref[0] ^ d
    return (turn & 1) * 4 + (turn >> 1)


def shape(dims, kind):
    return jax.ShapeDtypeStruct(dims, kind)


def wide(m):
    return jnp.concatenate([m] * GROUPS, axis=1)


def fold8(v):
    return jnp.sum(v.reshape(v.shape[0] // 8, 8, v.shape[1]), axis=0)


def norm_parts(x):
    center = jnp.sum(x, axis=-1, keepdims=True) * (1.0 / C)
    xc = x - center
    var = jnp.sum(xc * xc, axis=-1, keepdims=True) * (1.0 / C)
    rstd = lax.rsqrt(var + EPS)
    return xc * rstd, rstd


def norm_back(dn, xhat, rstd, gain):
    gp = dn * gain
    m1 = jnp.sum(gp, axis=-1, keepdims=True) * (1.0 / C)
    m2 = jnp.sum(gp * xhat, axis=-1, keepdims=True) * (1.0 / C)
    return rstd * (gp - m1 - xhat * m2)


def several(count, at_once, step):
    while count % at_once:
        at_once -= 1

    @pl.loop(0, count // at_once)
    def _(i):
        for j in range(at_once):
            step(i * at_once + j)


def head_masks(rows):
    lane = lax.broadcasted_iota(jnp.int32, (rows, LANES), 1) // HEAD
    return [lane == h for h in range(PER)]


def spread(v, masks):
    zero = jnp.zeros_like(v)
    return jnp.concatenate([jnp.where(m, v, zero) for m in masks], axis=0)


def gather_heads(full, masks):
    n = full.shape[0] // PER
    out = full[3 * n :]
    for h in (2, 1, 0):
        out = jnp.where(masks[h], full[h * n : (h + 1) * n], out)
    return out


def shifted_cols(left, right, j, step):
    if step == 0:
        return left, right
    if step == 1:
        return (
            jnp.where(j == 6, pltpu.roll(right, 6, 1), pltpu.roll(left, 7, 1)),
            pltpu.roll(right, 7, 1),
        )
    return (
        pltpu.roll(left, 1, 1),
        jnp.where(j == 0, pltpu.roll(left, 2, 1), pltpu.roll(right, 1, 1)),
    )


def canvas(ref, crop, lanes):
    base = crop * 32
    parts = [ref[pl.ds(base + 8 * w, 7), :, lanes] for w in range(4)]
    left = jnp.concatenate([parts[0], parts[2]], axis=0)
    right = jnp.concatenate([parts[1], parts[3]], axis=0)
    return left, right


def put_canvas(ref, crop, lanes, left, right, mask_ref):
    base = crop * 32
    zero = jnp.zeros((1, 8, LANES), F32)
    for w in range(4):
        side = right if w % 2 else left
        half = side[(w // 2) * 7 : (w // 2) * 7 + 7]
        rows = pl.ds(base + 8 * w, 8)
        ref[rows, :, lanes] = jnp.concatenate([half, zero], axis=0) * mask_ref[rows]


def conv_forward(u_ref, c_ref, small_ref, mask_ref, globals_, locals_):
    j14 = lax.broadcasted_iota(jnp.int32, (14, 8, LANES), 1)
    for g in range(GROUPS):
        lanes = pl.ds(g * LANES, LANES)
        taps = [small_ref[K_ROW + t : K_ROW + t + 1, lanes][None] for t in range(9)]
        shift = small_ref[V_ROW : V_ROW + 1, lanes][None]

        @pl.loop(0, globals_)
        def _(crop):
            left, right = canvas(u_ref, crop, lanes)
            zero = jnp.zeros((1, 8, LANES), F32)
            acc = [left + shift, right + shift]
            for e in (-1, 0, 1):
                for s, side in enumerate(shifted_cols(left, right, j14, e)):
                    tall = jnp.concatenate([zero, side, zero], axis=0)
                    for a in (-1, 0, 1):
                        acc[s] = acc[s] + taps[3 * (a + 1) + e + 1] * tall[1 + a : 15 + a]
            put_canvas(c_ref, crop, lanes, acc[0], acc[1], mask_ref)

        @pl.loop(0, locals_)
        def _(n):
            rows = pl.ds(globals_ * 32 + n * 8, 8)
            u = u_ref[rows, :, lanes]
            acc = u + shift
            for e in (-1, 0, 1):
                side = u if e == 0 else pltpu.roll(u, 7 if e == 1 else 1, 1)
                for a in (-1, 0, 1):
                    moved = side if a == 0 else jnp.roll(side, -a, axis=0)
                    acc = acc + taps[3 * (a + 1) + e + 1] * moved
            c_ref[rows, :, lanes] = acc * mask_ref[rows]


def conv_backward(d_ref, u_ref, du_ref, small_ref, acc_ref, globals_, locals_):
    j14 = lax.broadcasted_iota(jnp.int32, (14, 8, LANES), 1)
    for g in range(GROUPS):
        lanes = pl.ds(g * LANES, LANES)
        taps = [small_ref[K_ROW + t : K_ROW + t + 1, lanes][None] for t in range(9)]
        nothing = tuple(jnp.zeros((8, LANES), F32) for _ in range(10))

        def one_crop(crop, sums):
            sums = list(sums)
            left, right = canvas(d_ref, crop, lanes)
            own = canvas(u_ref, crop, lanes)
            zero = jnp.zeros((1, 8, LANES), F32)
            acc = [left, right]
            sums[9] = sums[9] + jnp.sum(left + right, axis=0)
            for e in (-1, 0, 1):
                for s, side in enumerate(shifted_cols(left, right, j14, -e)):
                    tall = jnp.concatenate([zero, side, zero], axis=0)
                    for a in (-1, 0, 1):
                        t = 3 * (a + 1) + e + 1
                        moved = tall[1 - a : 15 - a]
                        acc[s] = acc[s] + taps[t] * moved
                        sums[t] = sums[t] + jnp.sum(own[s] * moved, axis=0)
            base = crop * 32
            for w in range(4):
                side = acc[w % 2]
                half = side[(w // 2) * 7 : (w // 2) * 7 + 7]
                du_ref[pl.ds(base + 8 * w, 8), :, lanes] = jnp.concatenate([half, zero], axis=0)
            return tuple(sums)

        def one_local(n, sums):
            sums = list(sums)
            rows = pl.ds(globals_ * 32 + n * 8, 8)
            d = d_ref[rows, :, lanes]
            own = u_ref[rows, :, lanes]
            acc = d
            sums[9] = sums[9] + jnp.sum(d, axis=0)
            for e in (-1, 0, 1):
                side = d if e == 0 else pltpu.roll(d, 7 if e == -1 else 1, 1)
                for a in (-1, 0, 1):
                    t = 3 * (a + 1) + e + 1
                    moved = side if a == 0 else jnp.roll(side, a, axis=0)
                    acc = acc + taps[t] * moved
                    sums[t] = sums[t] + jnp.sum(own * moved, axis=0)
            du_ref[rows, :, lanes] = acc
            return tuple(sums)

        sums = lax.fori_loop(0, globals_, one_crop, nothing)
        sums = lax.fori_loop(0, locals_, one_local, sums)
        for t in range(10):
            acc_ref[t, :, lanes] = sums[t]


def spatial_forward(q_ref, k_ref, v_ref, mask_ref, o_ref, p_ref, windows):
    masks = head_masks(CELL)

    def step(w):
        rows = pl.ds(w * CELL, CELL)
        m = mask_ref[rows, :]
        valid = jnp.concatenate([m, m], axis=1) > 0.5
        for g in range(GROUPS):
            lanes = pl.ds(g * LANES, LANES)
            s = mm_nt(k_ref[rows, lanes], spread(q_ref[rows, lanes], masks))
            s = jnp.where(valid, s * SCALE, -1e9)
            e = jnp.exp(s - jnp.max(s, axis=0, keepdims=True))
            p = (e / jnp.sum(e, axis=0, keepdims=True)).astype(BF)
            p_ref[w, g] = p
            o_ref[rows, lanes] = gather_heads(mm_tn(p, v_ref[rows, lanes]), masks).astype(BF)

    several(windows, MIX_UNROLL, step)


def plus(a, b):
    return b if a is None else a + b


def pick(count, at_once):
    while count % at_once:
        at_once -= 1
    return at_once


def spatial_backward(q_ref, k_ref, v_ref, p_ref, do_ref, dq_ref, dk_ref, dv_ref, acc_ref, s_ref, windows, wait, send):
    masks = head_masks(CELL)
    lanes = [pl.ds(g * LANES, LANES) for g in range(GROUPS)]
    at_once = pick(windows, MIX_UNROLL)
    for ready in wait:
        ready()

    @pl.loop(0, windows // at_once)
    def _(i):
        sums = [None] * GROUPS
        for w in [i * at_once + j for j in range(at_once)]:
            rows = pl.ds(w * CELL, CELL)
            for g in range(GROUPS):
                p = p_ref[w, g]
                dos = spread(do_ref[rows, lanes[g]], masks)
                dp = mm_nt(v_ref[rows, lanes[g]], dos)
                pf = p.astype(F32)
                total = jnp.sum(pf * dp, axis=0, keepdims=True)
                ds = (pf * (dp - total) * SCALE).astype(BF)
                s_ref[w, g] = ds
                dv = mm(p, dos)
                sums[g] = plus(sums[g], fold8(dv))
                dv_ref[rows, lanes[g]] = dv.astype(BF)
                dk_ref[rows, lanes[g]] = mm(ds, spread(q_ref[rows, lanes[g]], masks)).astype(BF)
        for g in range(GROUPS):
            acc_ref[1, :, lanes[g]] += sums[g]

    send[1]()
    send[2]()

    @pl.loop(0, windows // at_once)
    def _(i):
        sums = [None] * GROUPS
        for w in [i * at_once + j for j in range(at_once)]:
            rows = pl.ds(w * CELL, CELL)
            for g in range(GROUPS):
                dq = gather_heads(mm_tn(s_ref[w, g], k_ref[rows, lanes[g]]), masks)
                sums[g] = plus(sums[g], fold8(dq))
                dq_ref[rows, lanes[g]] = dq.astype(BF)
        for g in range(GROUPS):
            acc_ref[0, :, lanes[g]] += sums[g]

    send[0]()


def same_head():
    a = lax.broadcasted_iota(jnp.int32, (LANES, LANES), 0) // HEAD
    b = lax.broadcasted_iota(jnp.int32, (LANES, LANES), 1) // HEAD
    return a == b


def over_crops(globals_, locals_, step):
    several(globals_, 3, lambda n: step(n, n * 4 * CELL, 4 * CELL))
    several(locals_, 9, lambda n: step(globals_ + n, globals_ * 4 * CELL + n * CELL, CELL))


def channel_forward(q_ref, k_ref, v_ref, mask_ref, o_ref, p_ref, globals_, locals_):
    same = same_head()
    lanes = [pl.ds(g * LANES, LANES) for g in range(GROUPS)]

    def weigh(n, start, count):
        rows = pl.ds(start, count)
        m = mask_ref[rows, :].astype(BF)
        for g in range(GROUPS):
            s = mm_tn(v_ref[rows, lanes[g]], k_ref[rows, lanes[g]] * m)
            s = jnp.where(same, s * SCALE, -jnp.inf)
            e = jnp.exp(s - jnp.max(s, axis=0, keepdims=True))
            p_ref[n, g] = (e / jnp.sum(e, axis=0, keepdims=True)).astype(BF)

    over_crops(globals_, locals_, weigh)

    def step(n, start, count):
        rows = pl.ds(start, count)
        for g in range(GROUPS):
            o_ref[rows, lanes[g]] = mm(q_ref[rows, lanes[g]], p_ref[n, g]).astype(BF)

    over_crops(globals_, locals_, step)


def channel_backward(
    q_ref, k_ref, v_ref, mask_ref, p_ref, do_ref, dq_ref, dk_ref, dv_ref, acc_ref, s_ref, globals_, locals_, wait, send
):
    lanes = [pl.ds(g * LANES, LANES) for g in range(GROUPS)]

    def slope(n, start, count):
        rows = pl.ds(start, count)
        for g in range(GROUPS):
            dp = mm_tn(q_ref[rows, lanes[g]], do_ref[rows, lanes[g]])
            pf = p_ref[n, g].astype(F32)
            total = jnp.sum(pf * dp, axis=0, keepdims=True)
            s_ref[n, g] = (pf * (dp - total) * SCALE).astype(BF)

    for ready in wait[:3]:
        ready()
    over_crops(globals_, locals_, slope)
    for ready in wait[3:]:
        ready()

    def step(n, start, count):
        rows = pl.ds(start, count)
        mf = mask_ref[rows, :]
        m = mf.astype(BF)
        for g in range(GROUPS):
            ds = s_ref[n, g]
            dq = mm_nt(do_ref[rows, lanes[g]], p_ref[n, g])
            dk = mm(v_ref[rows, lanes[g]], ds) * mf
            dv = mm_nt(k_ref[rows, lanes[g]] * m, ds)
            acc_ref[0, :, lanes[g]] += fold8(dq)
            acc_ref[1, :, lanes[g]] += fold8(dv)
            dq_ref[rows, lanes[g]] = dq.astype(BF)
            dk_ref[rows, lanes[g]] = dk.astype(BF)
            dv_ref[rows, lanes[g]] = dv.astype(BF)

    over_crops(globals_, locals_, step)
    for go in send:
        go()


def table_of(tabs):
    total = tabs[0].astype(F32)
    for d in range(1, tabs.shape[0]):
        total = total + tabs[d].astype(F32)
    return total


CHUNKS = 3


def crops_out(read, glob_ref, loc_ref, globals_, locals_, tmp):
    @pl.loop(0, globals_ * 2)
    def _(half):
        crop, below = half // 2, half % 2
        for i in range(WIN):
            tmp[i, 0:WIN, :] = read(half * 16 + i)[:WIN]
            tmp[i, WIN:SIDE, :] = read(half * 16 + 8 + i)[:WIN]
        for i in range(WIN):
            glob_ref[crop, below * WIN + i] = tmp[i].astype(glob_ref.dtype)

    @pl.loop(0, locals_)
    def _(n):
        for i in range(WIN):
            loc_ref[n, i] = read(globals_ * 32 + n * 8 + i)[:WIN].astype(loc_ref.dtype)


def crops_in(glob_ref, loc_ref, write, globals_, locals_, tmp):
    tmp[...] = jnp.zeros_like(tmp)
    patch = lax.broadcasted_iota(jnp.int32, (8, C), 0) < WIN
    empty = jnp.zeros((8, C), F32)

    @pl.loop(0, globals_ * 2)
    def _(half):
        crop, below = half // 2, half % 2
        for i in range(WIN):
            tmp[i, 0:SIDE, :] = glob_ref[crop, below * WIN + i].astype(F32)
        for i in range(WIN):
            write(half * 16 + i, jnp.where(patch, tmp[i, 0:8, :], 0.0))
            write(half * 16 + 8 + i, jnp.where(patch, tmp[i, WIN : WIN + 8, :], 0.0))
        write(half * 16 + WIN, empty)
        write(half * 16 + 8 + WIN, empty)

    tmp[...] = jnp.zeros_like(tmp)

    @pl.loop(0, locals_)
    def _(n):
        for i in range(WIN):
            tmp[i, 0:WIN, :] = loc_ref[n, i].astype(F32)
        for i in range(WIN):
            write(globals_ * 32 + n * 8 + i, tmp[i, 0:8, :])
        write(globals_ * 32 + n * 8 + WIN, empty)


CROP_TMP = pltpu.VMEM((WIN, 16, C), F32)


def crop_outs(globals_, locals_, kind):
    return [shape((globals_, SIDE, SIDE, C), kind), shape((locals_, WIN, WIN, C), kind)]


def chunks_of(rows):
    size = rows // CHUNKS
    return [pl.ds(i * size, size) for i in range(CHUNKS)]


def tiles_of(here):
    return pl.ds(here.start // 8, here.size // 8)


def attention_forward(sizes, kind, me, u, mask, bufs, first):
    globals_, locals_, shards = sizes
    windows = 4 * globals_ + locals_
    rows = windows * CELL
    part = C // shards
    chunks = chunks_of(rows)

    def kernel(me_ref, feeds, sends, held, packs, w, tabs, sem, sem2, *more):
        r_out, small_out, c_out, n_out, q_out, k_out, v_out, o_out, p_out = sends[:9]
        r_ref, small_ref, c_ref, n_ref, q_ref, k_ref, v_ref, o_ref, p_ref = [v.ref for v in sends[:9]]
        feeds[0].start()
        tab = start_weights(held, me_ref, [(first + 4 * part, TAB, lambda d: tabs.at[d])], sem2)
        feeds[1].start()
        plan = [(first + i * part, part, rows_of(w, i, part)) for i in range(4)]
        copies = start_weights(held, me_ref, plan, sem)
        if mask is not None:
            u_ref, mask_ref = feeds[0].wait(), feeds[1].wait()
        else:
            u_ref, mask_ref = sends[9].ref, sends[10].ref
            at = lax.broadcasted_iota(jnp.int32, (CELL, LANES), 0)
            for i in range(windows):
                inside = jnp.logical_and(at // 8 < me_ref[1 + 2 * i], at % 8 < me_ref[2 + 2 * i])
                mask_ref[i * CELL : (i + 1) * CELL, :] = jnp.where(inside, 1.0, 0.0)
            sends[10].start()
            glob_ref, loc_ref = feeds[0].wait(), feeds[1].wait()

            def write(tile, v):
                u_ref[tile] = v * wide(mask_ref[pl.ds(pl.multiple_of(tile * 8, 8), 8), :])

            crops_in(glob_ref, loc_ref, write, globals_, locals_, more[0])
            sends[9].start()
        for copy in tab:
            copy.wait()
        small_ref[...] = table_of(tabs)
        small_out.start()
        conv_forward(u_ref, c_ref, small_ref, mask_ref.reshape(windows * 8, 8, LANES), globals_, locals_)
        c_out.start()
        gain = small_ref[G_ROW : G_ROW + 1]
        shift = small_ref[V_ROW + 1 : V_ROW + 2]

        def step(i):
            x = c_ref[pl.ds(i * 8, 8)].reshape(CELL, C)
            xhat, _ = norm_parts(x)
            n_ref[pl.ds(i * CELL, CELL), :] = (xhat * gain + shift).astype(BF)

        several(windows, NORM_UNROLL, step)
        n_out.start()
        for copy in copies:
            copy.wait()
        for here in chunks:
            n1 = n_ref[here, :]
            q_ref[here, :] = (mm(n1, w[0]) + small_ref[V_ROW + 2 : V_ROW + 3]).astype(BF)
            k_ref[here, :] = mm(n1, w[1]).astype(BF)
            v_ref[here, :] = (mm(n1, w[2]) + small_ref[V_ROW + 3 : V_ROW + 4]).astype(BF)
        for send in (q_out, k_out, v_out):
            send.start()
        if kind == 0:
            spatial_forward(q_ref, k_ref, v_ref, mask_ref, o_ref, p_ref, windows)
        else:
            channel_forward(q_ref, k_ref, v_ref, mask_ref, o_ref, p_ref, globals_, locals_)
        p_out.start()
        o_out.start()
        for i, here in enumerate(chunks):
            c = c_ref[tiles_of(here)].reshape(here.size, C)
            r_ref[here, :] = c + mm(o_ref[here, :], w[3]) + small_ref[V_ROW + 4 : V_ROW + 5]
            r_out.start(i, here)

    low = shape((rows, C), BF)
    probs = (windows, GROUPS, CELL, PER * CELL) if kind == 0 else (globals_ + locals_, GROUPS, LANES, LANES)
    outs = [
        shape((rows, C), F32), shape((TAB, C), F32), shape((windows * 8, 8, C), F32),
        low, low, low, low, low, shape(probs, BF),
    ]
    scratch = [
        pltpu.VMEM((4, C, C), BF),
        pltpu.VMEM((shards, TAB, C), BF),
        pltpu.SemaphoreType.DMA,
        pltpu.SemaphoreType.DMA,
    ]
    if mask is None:
        outs += [shape((windows * 8, 8, C), F32), shape((rows, LANES), F32)]
        scratch.append(CROP_TMP)
    ins = list(u) if mask is None else [u, mask]
    return call(kernel, me, ins, outs, held=bufs, scratch=scratch, micros=FORWARD)


def start_ffn_weights(held, me_ref, where, part, deep, w1, w2, sem):
    n1, first1, n2, first2 = where
    plan1 = [(first1 + i * part, part, rows_of(w1, i, part)) for i in range(FF // C)]
    plan2 = [(first2, deep, lambda d: w2.at[pl.ds(pl.multiple_of(d * deep, deep), deep), :])]
    if n2 == 0:
        return start_weights(held[:n1], me_ref, plan1 + plan2, sem)
    return start_weights(held[:n1], me_ref, plan1, sem) + start_weights(held[n1 : n1 + n2], me_ref, plan2, sem)


def ffn_forward(sizes, me, r, mask, small, bufs, where, last):
    globals_, locals_, shards = sizes
    windows = 4 * globals_ + locals_
    rows = windows * CELL
    part = C // shards
    deep = FF // shards
    chunks = chunks_of(rows)

    def kernel(me_ref, feeds, sends, held, packs, w1, w2, sem, *more):
        r_in, m_in, small_in = feeds
        n_out, g_out, s_out = sends[:3]
        n_ref, g_ref, s_ref = [v.ref for v in sends[:3]]
        x_ref = more[0] if last else sends[3].ref
        small_in.start()
        r_in.start()
        copies = start_ffn_weights(held, me_ref, where, part, deep, w1, w2, sem)
        m_in.start()
        small_ref = small_in.wait()
        gain = small_ref[G_ROW + 1 : G_ROW + 2]
        shift = small_ref[V_ROW + 5 : V_ROW + 6]
        r_ref = r_in.wait()

        def step(i):
            here = pl.ds(i * CELL, CELL)
            xhat, _ = norm_parts(r_ref[here, :])
            n_ref[here, :] = (xhat * gain + shift).astype(BF)

        several(windows, NORM_UNROLL, step)
        n_out.start()
        mask_ref = m_in.wait()
        for copy in copies:
            copy.wait()
        for i, here in enumerate(chunks):
            n2 = n_ref[here, :]
            for t in range(FF // C):
                h = mm(n2, w1[t]) + small_ref[B_ROW + t : B_ROW + t + 1]
                h2 = h * h
                a = 0.5 + 0.5 * jnp.tanh(h * (0.7978845608 + (0.7978845608 * 0.044715) * h2))
                g = h * a
                slope = a + (2.0 * g) * (1.0 - a) * (0.7978845608 + (3 * 0.7978845608 * 0.044715) * h2)
                g_ref[here, t * C : (t + 1) * C] = g.astype(BF)
                s_ref[here, t * C : (t + 1) * C] = slope.astype(BF)
            g_out.start(i, here)
            s_out.start(i, here)
            y = r_ref[here, :] + mm(g_ref[here, :], w2[...]) + small_ref[V_ROW + 6 : V_ROW + 7]
            x_ref[here, :] = y * wide(mask_ref[here, :])
            if not last:
                sends[3].start(i, here)
        if last:
            crops_out(
                lambda tile: x_ref[pl.ds(pl.multiple_of(tile * 8, 8), 8), :],
                sends[3].ref, sends[4].ref, globals_, locals_, more[1],
            )
            sends[3].start()
            sends[4].start()

    high = shape((rows, FF), BF)
    outs = [shape((rows, C), BF), high, high]
    outs += crop_outs(globals_, locals_, BF) if last else [shape((rows, C), F32)]
    scratch = [pltpu.VMEM((FF // C, C, C), BF), pltpu.VMEM((FF, C), BF), pltpu.SemaphoreType.DMA]
    if last:
        scratch += [pltpu.VMEM((rows, C), F32), pltpu.VMEM((WIN, SIDE, C), F32)]
    return call(kernel, me, [r, mask, small], outs, held=bufs, scratch=scratch, micros=FORWARD)


def pack_outs(shards, count, relative):
    if relative:
        return [shape((4, count, C), BF)] * 2
    return [shape((shards, count, C), BF)]


def send_pack(dw, outs, rows, sem):
    each = len(outs) == 2
    copies = []
    for i, out in enumerate(outs):
        src = dw.at[pl.ds(4 * i, 4), rows] if each else dw.at[:, rows]
        copies.append(pltpu.make_async_copy(src, out.at[:, rows], sem))
    for copy in copies:
        copy.start()
    return copies


def ffn_backward(sizes, me, relative, dy, n2, g, slope, mask, w_ffn, where, rest, deps):
    raw = isinstance(dy, tuple)
    globals_, locals_, shards = sizes
    windows = 4 * globals_ + locals_
    rows = windows * CELL
    part = C // shards
    deep = FF // shards
    count = 4 * part + deep
    chunks = chunks_of(rows)
    packs = pack_outs(shards, count, relative)
    n_ffn = len(w_ffn)

    def kernel(me_ref, feeds, sends, held, dw_out, w1, w2, dw, dyl, dh, acc, acc1, sem, sem2, *more):
        n_in, g_in, s_in, m_in = feeds[:4]
        dy_feeds = feeds[4 : 6 if raw else 5]
        ds_out = sends[0]
        ds_ref = ds_out.ref
        more = list(more)
        tmp = more.pop(0) if raw else None
        dy_ref = more.pop(0) if raw else dy_feeds[0].ref
        dn_ref = sends[1].ref if rest is None else more.pop(0)
        for feed in dy_feeds:
            feed.start()
        m_in.start()
        copies = start_ffn_weights(held[:n_ffn], me_ref, where, part, deep, w1, w2, sem)
        for i, here in enumerate(chunks):
            s_in.start(i, here)
        n_in.start()
        g_in.start()
        acc[...] = jnp.zeros_like(acc)
        acc1[...] = jnp.zeros_like(acc1)
        mask_ref = m_in.wait()
        if raw:

            def write(tile, v):
                dy_ref[pl.ds(pl.multiple_of(tile * 8, 8), 8), :] = v

            crops_in(dy_feeds[0].wait(), dy_feeds[1].wait(), write, globals_, locals_, tmp)
        else:
            dy_feeds[0].wait()

        def step(i):
            here = pl.ds(i * CELL, CELL)
            d = dy_ref[here, :] * wide(mask_ref[here, :])
            dyl[here, :] = d.astype(BF)
            acc[...] += fold8(d)

        several(windows, NORM_UNROLL, step)
        for copy in copies:
            copy.wait()
        for i, here in enumerate(chunks):
            s_ref = s_in.wait(i)
            for t in range(FF // C):
                cols = slice(t * C, (t + 1) * C)
                d = mm_nt(dyl[here, :], w2[cols, :]) * s_ref[here, cols].astype(F32)
                acc1[:, cols] += fold8(d)
                dh[here, cols] = d.astype(BF)
            dn = None
            for t in range(FF // C):
                one = mm_nt(dh[here, t * C : (t + 1) * C], w1[t])
                dn = one if dn is None else dn + one
            dn_ref[here, :] = dn
            if rest is None:
                sends[1].start(i, here)

        if rest is not None:
            wp, acc2, sem3 = more
            r_in, small_in = feeds[-2:]
            r_in.start()
            small_in.start()
            plan = [(rest[3] + 3 * part, part, rows_of(wp, 0, part))]
            late = start_weights(held[n_ffn : n_ffn + len(rest[2])], me_ref, plan, sem3)
        n_ref = n_in.wait()
        g_ref = g_in.wait()
        going = []
        for t in range(FF // C):
            cols = slice(t * C, (t + 1) * C)
            one = mm_tn(n_ref[...], dh[:, cols]).astype(BF)
            for d in range(shards):
                dw[slot_of(d, me_ref, relative), t * part : (t + 1) * part, :] = one[d * part : (d + 1) * part]
            going += send_pack(dw, dw_out, pl.ds(t * part, part), sem2)
        for t in range(FF // C):
            cols = slice(t * C, (t + 1) * C)
            two = mm_tn(g_ref[:, cols], dyl[...]).astype(BF)
            for d in range(C // deep):
                here = pl.ds(4 * part, deep)
                dw[slot_of(t * (C // deep) + d, me_ref, relative), here, :] = two[d * deep : (d + 1) * deep]
        going += send_pack(dw, dw_out, pl.ds(4 * part, deep), sem2)
        ds_ref[0:1, :] = jnp.sum(acc[...], axis=0, keepdims=True)
        for t in range(FF // C):
            ds_ref[1 + t : 2 + t, :] = jnp.sum(acc1[:, t * C : (t + 1) * C], axis=0, keepdims=True)
        ds_ref[5:8, :] = jnp.zeros((3, C), F32)
        ds_out.start()
        if rest is not None:
            r_in.wait()
            gain = small_in.wait()[G_ROW + 1 : G_ROW + 2]
            ready = [Ready(v) for v in (dn_ref, dy_ref, r_in.ref, mask_ref)]
            norm_two_stage(rows, ready, gain, wp, late, acc2, sends[1:])
        for copy in going:
            copy.wait()

    full = pltpu.VMEM((rows, C), F32)
    outs = [shape((8, C), F32)] + ([shape((rows, C), F32)] if rest is None else norm_two_outs(rows))
    scratch = [
        pltpu.VMEM((FF // C, C, C), BF),
        pltpu.VMEM((FF, C), BF),
        pltpu.VMEM((shards, count, C), BF),
        pltpu.VMEM((rows, C), BF),
        pltpu.VMEM((rows, FF), BF),
        pltpu.VMEM((8, C), F32),
        pltpu.VMEM((8, FF), F32),
        pltpu.SemaphoreType.DMA,
        pltpu.SemaphoreType.DMA,
    ] + ([CROP_TMP, full] if raw else [])
    ins = [n2, g, slope, mask, *(dy if raw else [dy])]
    held = list(w_ffn)
    if rest is not None:
        scratch += [full, *NORM_TWO]
        ins += rest[:2]
        held += rest[2]
    return call(
        kernel, me, ins, outs, held=held + list(deps), packs=packs, scratch=scratch, micros=BACKWARD,
    )


def norm_two_stage(rows, feeds, gain, wp, copies, acc, sends):
    dn_in, dy_in, r_in, m_in = feeds
    dn_ref, dy_ref, r_ref, mask_ref = [v.ref for v in feeds]
    dr_out, drl_out, do_out, ds_out = sends
    dr_ref, drl, do_ref, ds_ref = [v.ref for v in sends]
    chunks = chunks_of(rows)
    each = chunks[0].size // CELL
    acc[...] = jnp.zeros_like(acc)
    for i, here in enumerate(chunks):
        for feed in feeds:
            feed.wait(i)
        sums = [None] * 3
        for w in range(i * each, (i + 1) * each):
            at = pl.ds(w * CELL, CELL)
            dn = dn_ref[at, :]
            xhat, rstd = norm_parts(r_ref[at, :])
            dr = norm_back(dn, xhat, rstd, gain) + dy_ref[at, :] * wide(mask_ref[at, :])
            sums = [plus(a, fold8(v)) for a, v in zip(sums, (dn * xhat, dn, dr))]
            dr_ref[at, :] = dr
            drl[at, :] = dr.astype(BF)
        for t in range(3):
            acc[t] += sums[t]
        dr_out.start(i, here)
        drl_out.start(i, here)
        if i == 0:
            for copy in copies:
                copy.wait()
        do_ref[here, :] = mm_nt(drl[here, :], wp[0]).astype(BF)
        do_out.start(i, here)
    for t in range(3):
        ds_ref[t : t + 1, :] = jnp.sum(acc[t], axis=0, keepdims=True)
    ds_ref[3:8, :] = jnp.zeros((5, C), F32)
    ds_out.start()


def norm_two_outs(rows):
    low = shape((rows, C), BF)
    return [shape((rows, C), F32), low, low, shape((8, C), F32)]


NORM_TWO = [pltpu.VMEM((1, C, C), BF), pltpu.VMEM((3, 8, C), F32), pltpu.SemaphoreType.DMA]


def norm_two_backward(sizes, me, dn, dy, r, mask, small, w_att, first, deps):
    globals_, locals_, shards = sizes
    rows = (4 * globals_ + locals_) * CELL
    part = C // shards

    def kernel(me_ref, feeds, sends, held, packs, wp, acc, sem):
        dn_in, dy_in, r_in, m_in, small_in = feeds
        small_in.start()
        for i, here in enumerate(chunks_of(rows)):
            for feed in (r_in, dn_in, dy_in, m_in):
                feed.start(i, here)
            if i == 0:
                plan = [(first + 3 * part, part, rows_of(wp, 0, part))]
                copies = start_weights(held[: len(w_att)], me_ref, plan, sem)
        gain = small_in.wait()[G_ROW + 1 : G_ROW + 2]
        norm_two_stage(rows, feeds[:4], gain, wp, copies, acc, sends)

    return call(
        kernel, me, [dn, dy, r, mask, small], norm_two_outs(rows), held=[*w_att, *deps], micros=BACKWARD,
        scratch=NORM_TWO,
    )


def norm_one_stage(rows, feeds, gain, w, dq, dk, dv, acc, dc_out, ds_out):
    dr_in, c_in, m_in = feeds
    dr_ref, c_ref, mask_ref = [v.ref for v in feeds]
    dc, ds_ref = dc_out.ref, ds_out.ref
    chunks = chunks_of(rows)
    each = chunks[0].size // CELL
    for i, here in enumerate(chunks):
        total = mm_nt(dq(i)[here, :], w[0]) + mm_nt(dk(i)[here, :], w[1]) + mm_nt(dv(i)[here, :], w[2])
        for feed in feeds:
            feed.wait(i)
        sums = [None] * 2
        for j in range(each):
            window = i * each + j
            at, tiles = pl.ds(window * CELL, CELL), pl.ds(window * 8, 8)
            d = total[j * CELL : (j + 1) * CELL]
            xhat, rstd = norm_parts(c_ref[tiles].reshape(CELL, C))
            sums = [plus(a, fold8(v)) for a, v in zip(sums, (d * xhat, d))]
            full = norm_back(d, xhat, rstd, gain) + dr_ref[at, :]
            dc[tiles] = (full * wide(mask_ref[at, :])).reshape(8, 8, C)
        for t in range(2):
            acc[t] += sums[t]
        dc_out.start(i, tiles_of(here))
    for t in range(2):
        ds_ref[t : t + 1, :] = jnp.sum(acc[t], axis=0, keepdims=True)
    ds_ref[2:8, :] = jnp.zeros((6, C), F32)
    ds_out.start()


def start_norm_one(rows, feeds):
    dr_in, c_in, m_in = feeds
    for i, here in enumerate(chunks_of(rows)):
        dr_in.start(i, here)
        m_in.start(i, here)
        c_in.start(i, tiles_of(here))


def mix_backward(sizes, kind, me, relative, q, k, v, p, do, n1, o, drl, mask, rest, deps):
    globals_, locals_, shards = sizes
    windows = 4 * globals_ + locals_
    rows = windows * CELL
    part = C // shards
    packs = pack_outs(shards, 4 * part, relative)
    low = shape((rows, C), BF)
    eight = shape((8, C), F32)

    def kernel(me_ref, feeds, sends, held, dw_out, acc, slope, dw, sem, *more):
        q_in, k_in, v_in, p_in, do_in, n_in, o_in, drl_in, m_in = feeds[:9]
        q_ref, k_ref, v_ref, p_ref, do_ref, n_ref, o_ref, drl, mask_ref = [v.ref for v in feeds[:9]]
        if rest is None:
            dq, dk, dv = [v.ref for v in sends[:3]]
            go = [send.start for send in sends[:3]]
            ds_out = sends[3]
        else:
            dq, dk, dv, w, acc1, sem_w = more
            go = [lambda: None] * 3
            dc_out, ds_out, one_out = sends
        ds_ref = ds_out.ref
        order = (v_in, do_in, p_in, q_in, k_in) if kind == 0 else (q_in, do_in, p_in, v_in, k_in)
        waits = [feed.wait for feed in order]
        for feed in order:
            feed.start()
        if rest is None:
            m_in.start()
            waits.append(m_in.wait)
        else:
            for i, here in enumerate(chunks_of(rows)):
                m_in.start(i, here)
            plan = [(rest[4] + i * part, part, rows_of(w, i, part)) for i in range(3)]
            copies = start_weights(held[: len(rest[3])], me_ref, plan, sem_w)
            dr_in, c_in, small_in = feeds[9:]
            small_in.start()
            waits += [m_in.wait_all, small_in.wait]
        for feed in (n_in, o_in, drl_in):
            feed.start()
        if rest is not None:
            dr_in.start()
            c_in.start()
        acc[...] = jnp.zeros_like(acc)
        if kind == 0:
            spatial_backward(q_ref, k_ref, v_ref, p_ref, do_ref, dq, dk, dv, acc, slope, windows, waits, go)
        else:
            channel_backward(
                q_ref, k_ref, v_ref, mask_ref, p_ref, do_ref, dq, dk, dv, acc, slope, globals_, locals_, waits, go
            )
        for t in range(2):
            ds_ref[t : t + 1, :] = jnp.sum(acc[t], axis=0, keepdims=True)
        ds_ref[2:8, :] = jnp.zeros((6, C), F32)
        ds_out.start()
        for feed in (n_in, o_in, drl_in):
            feed.wait()
        going = []
        for i, left, right in ((1, n_ref, dk), (2, n_ref, dv), (0, n_ref, dq), (3, o_ref, drl)):
            one = mm_tn(left[...], right[...]).astype(BF)
            for d in range(shards):
                dw[slot_of(d, me_ref, relative), i * part : (i + 1) * part, :] = one[d * part : (d + 1) * part]
            going += send_pack(dw, dw_out, pl.ds(i * part, part), sem)
        if rest is not None:
            acc1[...] = jnp.zeros_like(acc1)
            for copy in copies:
                copy.wait()
            dr_in.wait()
            c_in.wait()
            feeds_one = [Ready(v.ref) for v in (dr_in, c_in, m_in)]
            gain = small_in.ref[G_ROW : G_ROW + 1]
            norm_one_stage(
                rows, feeds_one, gain, w, lambda i: dq, lambda i: dk, lambda i: dv, acc1, dc_out, one_out
            )
        for copy in going:
            copy.wait()

    scratch = [
        pltpu.VMEM((2, 8, C), F32), pltpu.VMEM(p.shape, BF), pltpu.VMEM((shards, 4 * part, C), BF),
        pltpu.SemaphoreType.DMA,
    ]
    ins = [q, k, v, p, do, n1, o, drl, mask]
    if rest is None:
        outs, held = [low, low, low, eight], list(deps)
    else:
        outs, held = [shape((windows * 8, 8, C), F32), eight, eight], [*rest[3], *deps]
        ins += [rest[0], rest[1], rest[2]]
        scratch += [pltpu.VMEM((rows, C), BF)] * 3
        scratch += [pltpu.VMEM((3, C, C), BF), pltpu.VMEM((2, 8, C), F32), pltpu.SemaphoreType.DMA]
    return call(kernel, me, ins, outs, held=held, packs=packs, scratch=scratch, micros=BACKWARD)


class Ready:
    def __init__(self, ref):
        self.ref = ref

    def wait(self, k=0):
        return self.ref


def norm_one_backward(sizes, me, dr, c, dq, dk, dv, mask, small, bufs, first, deps):
    globals_, locals_, shards = sizes
    windows = 4 * globals_ + locals_
    rows = windows * CELL
    part = C // shards

    def kernel(me_ref, feeds, sends, held, packs, w, acc, sem):
        dr_in, c_in, dq_in, dk_in, dv_in, m_in, small_in = feeds
        plan = [(first + i * part, part, rows_of(w, i, part)) for i in range(3)]
        copies = start_weights(held[: len(bufs)], me_ref, plan, sem)
        small_in.start()
        for i, here in enumerate(chunks_of(rows)):
            for feed in (dq_in, dk_in, dv_in):
                feed.start(i, here)
        start_norm_one(rows, (dr_in, c_in, m_in))
        acc[...] = jnp.zeros_like(acc)
        gain = small_in.wait()[G_ROW : G_ROW + 1]
        for copy in copies:
            copy.wait()
        norm_one_stage(rows, (dr_in, c_in, m_in), gain, w, dq_in.wait, dk_in.wait, dv_in.wait, acc, *sends)

    return call(
        kernel, me, [dr, c, dq, dk, dv, mask, small], [shape((windows * 8, 8, C), F32), shape((8, C), F32)],
        held=[*bufs, *deps], micros=BACKWARD,
        scratch=[pltpu.VMEM((3, C, C), BF), pltpu.VMEM((2, 8, C), F32), pltpu.SemaphoreType.DMA],
    )


def position_backward(sizes, me, dc, u, mask, small, ds_ffn, ds_two, ds_mix, ds_one, last, deps):
    globals_, locals_, _ = sizes
    windows = 4 * globals_ + locals_

    def kernel(me_ref, feeds, sends, held, packs, acck, *more):
        dc_ref, u_ref, small_ref, ffn, two, mix, one = [v.ref for v in feeds[:7]]
        tab = sends[0].ref
        du_ref = more[0] if last else sends[1].ref
        for feed in feeds:
            feed.start()
        for feed in feeds:
            feed.wait()
        conv_backward(dc_ref, u_ref, du_ref, small_ref, acck, globals_, locals_)
        if last:
            mask_ref = feeds[7].ref

            def read(tile):
                here = pl.ds(pl.multiple_of(tile * 8, 8), 8)
                return du_ref[tile] * wide(mask_ref[here, :])

            crops_out(read, sends[1].ref, sends[2].ref, globals_, locals_, more[1])
            sends[2].start()
        sends[1].start()
        rows_ = [jnp.sum(acck[t], axis=0, keepdims=True) for t in range(10)]
        rows_ += [one[1:2, :], mix[0:1, :], mix[1:2, :], two[2:3, :], two[1:2, :], ffn[0:1, :]]
        rows_ += [one[0:1, :], two[0:1, :]]
        rows_ += [ffn[1 + t : 2 + t, :] for t in range(FF // C)]
        tab[...] = jnp.zeros_like(tab)
        for t, row in enumerate(rows_):
            tab[t : t + 1, :] = row
        sends[0].start()

    full = (windows * 8, 8, C)
    ins = [dc, u, small, ds_ffn, ds_two, ds_mix, ds_one]
    outs = [shape((TAB, C), F32)]
    scratch = [pltpu.VMEM((10, 8, C), F32)]
    if last:
        ins.append(mask)
        outs += crop_outs(globals_, locals_, F32)
        scratch += [pltpu.VMEM(full, F32), pltpu.VMEM((WIN, SIDE, C), F32)]
    else:
        outs.append(shape(full, F32))
    return call(kernel, me, ins, outs, held=deps, scratch=scratch, micros=BACKWARD)


def join(values, deps):
    values, deps = list(values), list(deps)

    def kernel(*refs):
        pass

    return pl.pallas_call(
        kernel,
        out_shape=[shape(v.shape, v.dtype) for v in values],
        in_specs=[HELD] * (len(values) + len(deps)),
        out_specs=[HELD] * len(values),
        input_output_aliases={i: i for i in range(len(values))},
    )(*values, *deps)


def place_and_extents(index, extent, globals_):
    sizes = jnp.concatenate([jnp.full((globals_ * 4, 2), WIN, jnp.int32), extent.astype(jnp.int32)], axis=0)
    return jnp.concatenate([index.astype(jnp.int32).reshape(1), sizes.reshape(-1)])


def layer(sizes, me, tokens, cotangent, plan):
    windows = 4 * sizes[0] + sizes[1]
    rows = windows * CELL
    dy = cotangent
    kept = []
    places = []
    mask = None
    u = tokens
    for b in range(2):
        att, att_first = plan.att_weights(b, u)
        r, small, *saved = attention_forward(sizes, b, me, u, mask, att, att_first)
        if b == 0:
            *saved, u, mask = saved
        ffn, where = plan.ffn_weights(b, r)
        places.append((att, att_first, ffn, where))
        n2, g, slope, *out = ffn_forward(sizes, me, r, mask, small, ffn, where, b == 1)
        kept.append((u, r, small, saved, (n2, g, slope)))
        if b == 0:
            u = out[0].reshape(windows * 8, 8, C)
    tables = [None, None]
    deps = []
    for b in (1, 0):
        u, r, small, (c, n1, q, k, v, o, p), (n2, g, slope) = kept[b]
        att, att_first, ffn, where = places[b]
        rel_ffn, rel_att = plan.relative[b]
        rest = (r, small, att, att_first)
        ds_ffn, dr, drl, do, ds_two, *dw = ffn_backward(
            sizes, me, rel_ffn, dy, n2, g, slope, mask, ffn, where, rest, deps
        )
        deps = plan.step(b, 0, dr, dw)
        mixed = (q, k, v, p, do, n1, o, drl, mask)
        rest = (dr, c, small, att, att_first)
        dc, ds_mix, ds_one, *dw = mix_backward(sizes, b, me, rel_att, *mixed, rest, deps)
        deps = plan.step(b, 2, dc, dw)
        tables[b], *du = position_backward(
            sizes, me, dc, u, mask, small, ds_ffn, ds_two, ds_mix, ds_one, b == 0, deps
        )
        deps = plan.step(b, 4, du[0], tables)
        if b == 1:
            dy = du[0].reshape(rows, C)
    return out, du


def xor(v, axis, turn):
    size = lax.axis_size(axis)
    return lax.ppermute(v, axis, [(i, i ^ turn) for i in range(size)])


def gather_near(own):
    return [own, xor(own, "fsdp", 2), xor(own, "fsdp", 4), xor(own, "fsdp", 6)]


def gather_core(near):
    out = []
    for v in near:
        out += [v, xor(v, "fsdp", 1)]
    return out


def add(*terms):
    total = terms[0].astype(F32)
    for term in terms[1:]:
        total = total + term.astype(F32)
    return total.astype(BF)


def to_core(pack):
    return xor(pack[1], "fsdp", 1)


def to_chips(parts):
    return [xor(v, "fsdp", 2 * i + 2) for i, v in enumerate(parts[1:])]


def core_sums(pack, got):
    return [add(pack[0][i], got[i]) for i in range(4)]


def own_lanes(table):
    shards, index = lax.axis_size("fsdp"), lax.axis_index("fsdp")
    part, deep = C // shards, FF // shards
    main = lax.dynamic_slice(table, (0, 0, index * part), (2, B_ROW, part)).reshape(2, B_ROW * part)
    bias = lax.dynamic_slice(table[:, B_ROW : B_ROW + FF // C].reshape(2, FF), (0, index * deep), (2, deep))
    return jnp.concatenate([main, bias], axis=1)


class Direct:
    relative = ((True, True), (False, False))

    def __init__(self, part, deep, packs):
        self.ffn_first = 4 * part
        self.att_first = 4 * part + deep
        self.att0 = gather_near(packs[0])
        self.ffn0 = gather_near(packs[1])
        self.whole1 = lax.all_gather(packs[2], "fsdp", axis=0)

    def att_weights(self, b, u):
        if b == 0:
            return gather_core(self.att0), 0
        return [self.whole1], self.att_first

    def ffn_weights(self, b, r):
        if b == 0:
            bufs = gather_core(join(self.ffn0, [r]))
            return bufs, (len(bufs), 0, 0, self.ffn_first)
        return [self.whole1], (1, 0, 0, self.ffn_first)

    def step(self, b, stage, token, new=None):
        if (b, stage) == (1, 0):
            self.f1_own = lax.psum_scatter(new[0], "fsdp", scatter_dimension=0, tiled=True)[0]
        elif (b, stage) == (1, 2):
            self.a1_own = lax.psum_scatter(new[0], "fsdp", scatter_dimension=0, tiled=True)[0]
        elif (b, stage) == (0, 0):
            core = to_core(new)
            (f1_own,) = join([self.f1_own], [token])
            self.f0_sums = core_sums(new, core)
            self.f0_chips = to_chips(self.f0_sums)
            self.f1_sum = Spread(f1_own)
            self.f1_sum.first()
            return [*self.f0_sums, self.f1_sum.keep]
        elif (b, stage) == (0, 2):
            self.a0, self.a0_core = new, to_core(new)
            *chips, self.f1_sum.got = join([*self.f0_chips, self.f1_sum.got], [token])
            self.f0_sum = Spread(add(self.f0_sums[0], *chips))
            self.f0_sum.first()
            self.f1_sum.second()
            return [self.f0_sum.keep, self.f1_sum.half]
        elif (b, stage) == (0, 4):
            core, self.f0_sum.got, self.f1_sum.got, a1_own = join(
                [self.a0_core, self.f0_sum.got, self.f1_sum.got, self.a1_own], [token]
            )
            a0_sums = core_sums(self.a0, core)
            a0_chips = to_chips(a0_sums)
            self.f0_sum.second()
            self.f1_sum.third()
            a1_sum = Spread(a1_own)
            a1_sum.first()
            (table,) = join([jnp.stack(new).astype(BF)], [a0_sums[0], self.f0_sum.half])
            table = add(table, xor(table, "fsdp", 1))
            *a0_chips, self.f0_sum.got, a1_sum.got, table = join(
                [*a0_chips, self.f0_sum.got, a1_sum.got, table], [table]
            )
            a0_sum = Spread(add(a0_sums[0], *a0_chips))
            a0_sum.first()
            self.f0_sum.third()
            a1_sum.second()
            table = own_lanes(add(table, *[xor(table, "fsdp", turn) for turn in (2, 4, 6)]))
            a0_sum.got, a1_sum.got, table = join([a0_sum.got, a1_sum.got, table], [table])
            a0_sum.second()
            a1_sum.third()
            other, away, across = [xor(table, "dp", turn) for turn in (1, 2, 3)]
            two = [a.astype(F32) + b.astype(F32) for a, b in ((table, other), (away, across))]
            a0_sum.third()
            near = [self.f0_sum.result(), a0_sum.result()]
            self.done = [near, [self.f1_sum.result(), a1_sum.result()]], (two[0] + two[1]).astype(BF)
        return []

    def results(self):
        return self.done


class Spread:
    def __init__(self, v):
        n = v.shape[0] // 2
        self.low = (lax.axis_index("dp") & 1) == 0
        self.keep = jnp.where(self.low, v[:n], v[n:])
        self.send = jnp.where(self.low, v[n:], v[:n])

    def first(self):
        self.got = xor(self.send, "dp", 1)

    def second(self):
        self.half = add(self.keep, self.got)
        self.got = xor(self.half, "dp", 2)

    def third(self):
        self.whole = add(self.half, self.got)
        self.got = xor(self.whole, "dp", 1)

    def result(self):
        whole, other = self.whole, self.got
        return jnp.concatenate([jnp.where(self.low, whole, other), jnp.where(self.low, other, whole)])


class Plain:
    relative = ((False, False), (False, False))

    def __init__(self, part, deep, packs):
        self.packs = [[None, None], [None, None]]
        self.first = 4 * part
        self.cut = 4 * part + deep
        self.whole = [lax.all_gather(pack, "fsdp", axis=0) for pack in packs]

    def att_weights(self, b, u):
        return [self.whole[b]], self.cut

    def ffn_weights(self, b, r):
        return [self.whole[b]], (1, 0, 0, self.first)

    def step(self, b, stage, token, new=None):
        if stage in (0, 2):
            self.packs[b][stage // 2] = new[0]
        if (b, stage) == (0, 4):
            self.table = new
        return []

    def results(self):
        grads = [
            lax.psum([lax.psum_scatter(v, "fsdp", scatter_dimension=0, tiled=True)[0] for v in pair], "dp")
            for pair in self.packs
        ]
        return grads, own_lanes(lax.psum(jnp.stack(self.table).astype(BF), ("dp", "fsdp")))


def body(
    global_tokens,
    local_tokens,
    crop_extent,
    conv_weight,
    vectors,
    gains,
    qkv_weight,
    proj_weight,
    fc1_weight,
    fc1_bias,
    fc2_weight,
    global_cotangent,
    local_cotangent,
):
    shards = lax.axis_size("fsdp")
    direct = shards == 8 and lax.axis_size("dp") == 4
    part = C // shards
    globals_, locals_ = global_tokens.shape[0], local_tokens.shape[0]
    sizes = (globals_, locals_, shards)
    index = lax.axis_index("fsdp")
    me = place_and_extents(index, crop_extent, globals_)

    own_small = jnp.concatenate([conv_weight, vectors, gains], axis=1)
    own_bias = fc1_bias.reshape(2, 1, FF // shards)
    start = index * (FF // shards)

    def att(b):
        table = lax.dynamic_update_slice(jnp.zeros((TAB, C), BF), own_small[b], (0, index * part))
        table = lax.dynamic_update_slice(table, own_bias[b], (B_ROW + start // C, start % C))
        return [qkv_weight[b][:, i * C : (i + 1) * C] for i in range(3)] + [proj_weight[b], table]

    def ffn(b):
        return [fc1_weight[b][:, i * C : (i + 1) * C] for i in range(FF // C)] + [fc2_weight[b]]

    groups = [att(0), ffn(0), ffn(1) + att(1)] if direct else [ffn(b) + att(b) for b in range(2)]
    packs = [jnp.concatenate(group, axis=0) for group in groups]
    plan = (Direct if direct else Plain)(part, FF // shards, packs)
    out, grad = layer(
        sizes, me,
        (global_tokens, local_tokens),
        (global_cotangent, local_cotangent),
        plan,
    )
    grads, table = plan.results()
    deep = FF // shards

    def cut(half, start, n):
        return jnp.stack(
            [
                jnp.concatenate([g[half][(start + i) * part : (start + i + 1) * part] for i in range(n)], axis=1)
                for g in grads
            ]
        ).astype(F32)

    table = table.astype(F32)
    main = table[:, : B_ROW * part].reshape(2, B_ROW, part)
    bias = table[:, B_ROW * part :]
    fc2 = jnp.stack([g[0][4 * part :] for g in grads]).astype(F32)
    proj = jnp.stack([g[1][3 * part :] for g in grads]).astype(F32)
    return (
        out[0], out[1], grad[0], grad[1],
        main[:, 0:9], main[:, 9:16], main[:, 16:18],
        cut(1, 0, 3), proj, cut(0, 0, 4), bias, fc2,
    )


def solution(mesh):
    crops = P(("dp", "fsdp"), None, None, None)
    last = P(None, None, "fsdp")
    middle = P(None, "fsdp", None)
    return jax.shard_map(
        body,
        mesh=mesh,
        in_specs=(
            crops, crops, P(("dp", "fsdp"), None), last, last, last, middle, middle, middle,
            P(None, "fsdp"), middle, crops, crops,
        ),
        out_specs=(
            crops, crops, crops, crops, last, last, last, middle, middle, middle, P(None, "fsdp"), middle,
        ),
        check_vma=False,
    )
```

```python
import functools

import jax
import jax.numpy as jnp
from jax import lax
from jax.experimental import pallas as pl
from jax.experimental.pallas import tpu as pltpu
from jax.sharding import PartitionSpec as P

BF = jnp.bfloat16
F32 = jnp.float32
C = 512
FF = 2048
HEAD = 32
WIN = 7
SIDE = 14
CELL = 64
LANES = 128
GROUPS = C // LANES
PER = LANES // HEAD
EPS = 1e-5
SCALE = HEAD ** -0.5
MIX_UNROLL = 7
NORM_UNROLL = 7
FORWARD, BACKWARD = 1, 3
VMEM = pl.BlockSpec(memory_space=pltpu.VMEM)
HELD = pl.BlockSpec(memory_space=pl.ANY)
NT = (((1,), (1,)), ((), ()))
TN = (((0,), (0,)), ((), ()))
K_ROW, V_ROW, G_ROW, B_ROW, TAB = 0, 9, 16, 18, 32


def mm(a, b):
    return jnp.dot(a, b, preferred_element_type=F32)


def mm_nt(a, b):
    return lax.dot_general(a, b, NT, preferred_element_type=F32)


def mm_tn(a, b):
    return lax.dot_general(a, b, TN, preferred_element_type=F32)


class Copy:
    def __init__(self, src, dst, sems, ref):
        self.src, self.dst, self.sems, self.ref = src, dst, sems, ref
        self.open = {}

    def start(self, k=0, part=None):
        src, dst = (self.src, self.dst) if part is None else (self.src.at[part], self.dst.at[part])
        self.open[k] = pltpu.make_async_copy(src, dst, self.sems.at[k])
        self.open[k].start()

    def wait(self, k=0):
        self.open.pop(k).wait()
        return self.ref

    def wait_all(self):
        for k in list(self.open):
            self.wait(k)


PARTS = 4


def call(kernel, me, ins, outs, held=(), packs=(), scratch=(), micros=1, alias=None, limit=62):
    n_in, n_out, n_held, n_pack = len(ins), len(outs), len(held), len(packs)

    def body(me_ref, *refs):
        src, refs = refs[:n_in], refs[n_in:]
        held_refs, refs = refs[:n_held], refs[n_held:]
        dst, refs = refs[:n_out], refs[n_out:]
        pack_refs, refs = refs[:n_pack], refs[n_pack:]
        in_vmem, refs = refs[:n_in], refs[n_in:]
        out_vmem, refs = refs[:n_out], refs[n_out:]
        in_sem, out_sem, refs = refs[0], refs[1], refs[2:]
        feeds = [Copy(s, v, in_sem.at[i], v) for i, (s, v) in enumerate(zip(src, in_vmem))]
        sends = [Copy(v, d, out_sem.at[i], v) for i, (d, v) in enumerate(zip(dst, out_vmem))]
        kernel(me_ref, feeds, sends, held_refs, pack_refs, *refs)
        for send in sends:
            send.wait_all()

    vmem = lambda v: pltpu.VMEM(v.shape, v.dtype)
    return pl.pallas_call(
        body,
        out_shape=list(outs) + list(packs),
        in_specs=[pl.BlockSpec(memory_space=pltpu.SMEM)] + [HELD] * (n_in + n_held),
        out_specs=[HELD] * (n_out + n_pack),
        scratch_shapes=[vmem(v) for v in ins]
        + [vmem(v) for v in outs]
        + [pltpu.SemaphoreType.DMA((max(n_in, 1), PARTS)), pltpu.SemaphoreType.DMA((max(n_out, 1), PARTS))]
        + list(scratch),
        compiler_params=pltpu.CompilerParams(vmem_limit_bytes=limit * 2**20),
        cost_estimate=pl.CostEstimate(flops=int(micros * 1.1e9), bytes_accessed=2**20, transcendentals=0),
        input_output_aliases=alias or {},
    )(me, *ins, *held)


def start_weights(bufs, me_ref, plan, sem):
    copies = []
    if len(bufs) == 1:
        sources = [(d, bufs[0].at[d]) for d in range(bufs[0].shape[0])]
    else:
        sources = [(me_ref[0] ^ k, buf) for k, buf in enumerate(bufs)]
    for d, src in sources:
        for first, rows, place in plan:
            copies.append(pltpu.make_async_copy(src.at[pl.ds(first, rows), :], place(d), sem))
    for copy in copies:
        copy.start()
    return copies


def rows_of(ref, i, rows):
    return lambda d: ref.at[i, pl.ds(pl.multiple_of(d * rows, rows), rows), :]


def slot_of(d, me_ref, relative):
    if not relative:
        return d
    turn = me_ref[0] ^ d
    return (turn & 1) * 4 + (turn >> 1)


def shape(dims, kind):
    return jax.ShapeDtypeStruct(dims, kind)


def wide(m):
    return jnp.concatenate([m] * GROUPS, axis=1)


def fold8(v):
    return jnp.sum(v.reshape(v.shape[0] // 8, 8, v.shape[1]), axis=0)


def norm_parts(x):
    center = jnp.sum(x, axis=-1, keepdims=True) * (1.0 / C)
    xc = x - center
    var = jnp.sum(xc * xc, axis=-1, keepdims=True) * (1.0 / C)
    rstd = lax.rsqrt(var + EPS)
    return xc * rstd, rstd


def norm_back(dn, xhat, rstd, gain):
    gp = dn * gain
    m1 = jnp.sum(gp, axis=-1, keepdims=True) * (1.0 / C)
    m2 = jnp.sum(gp * xhat, axis=-1, keepdims=True) * (1.0 / C)
    return rstd * (gp - m1 - xhat * m2)


def several(count, at_once, step):
    while count % at_once:
        at_once -= 1

    @pl.loop(0, count // at_once)
    def _(i):
        for j in range(at_once):
            step(i * at_once + j)


def head_masks(rows):
    lane = lax.broadcasted_iota(jnp.int32, (rows, LANES), 1) // HEAD
    return [lane == h for h in range(PER)]


def spread(v, masks):
    zero = jnp.zeros_like(v)
    return jnp.concatenate([jnp.where(m, v, zero) for m in masks], axis=0)


def gather_heads(full, masks):
    n = full.shape[0] // PER
    out = full[3 * n :]
    for h in (2, 1, 0):
        out = jnp.where(masks[h], full[h * n : (h + 1) * n], out)
    return out


def shifted_cols(left, right, j, step):
    if step == 0:
        return left, right
    if step == 1:
        return (
            jnp.where(j == 6, pltpu.roll(right, 6, 1), pltpu.roll(left, 7, 1)),
            pltpu.roll(right, 7, 1),
        )
    return (
        pltpu.roll(left, 1, 1),
        jnp.where(j == 0, pltpu.roll(left, 2, 1), pltpu.roll(right, 1, 1)),
    )


def canvas(ref, crop, lanes):
    base = crop * 32
    parts = [ref[pl.ds(base + 8 * w, 7), :, lanes] for w in range(4)]
    left = jnp.concatenate([parts[0], parts[2]], axis=0)
    right = jnp.concatenate([parts[1], parts[3]], axis=0)
    return left, right


def put_canvas(ref, crop, lanes, left, right, mask_ref):
    base = crop * 32
    zero = jnp.zeros((1, 8, LANES), F32)
    for w in range(4):
        side = right if w % 2 else left
        half = side[(w // 2) * 7 : (w // 2) * 7 + 7]
        rows = pl.ds(base + 8 * w, 8)
        ref[rows, :, lanes] = jnp.concatenate([half, zero], axis=0) * mask_ref[rows]


def conv_forward(u_ref, c_ref, small_ref, mask_ref, globals_, locals_):
    j14 = lax.broadcasted_iota(jnp.int32, (14, 8, LANES), 1)
    for g in range(GROUPS):
        lanes = pl.ds(g * LANES, LANES)
        taps = [small_ref[K_ROW + t : K_ROW + t + 1, lanes][None] for t in range(9)]
        shift = small_ref[V_ROW : V_ROW + 1, lanes][None]

        @pl.loop(0, globals_)
        def _(crop):
            left, right = canvas(u_ref, crop, lanes)
            zero = jnp.zeros((1, 8, LANES), F32)
            acc = [left + shift, right + shift]
            for e in (-1, 0, 1):
                for s, side in enumerate(shifted_cols(left, right, j14, e)):
                    tall = jnp.concatenate([zero, side, zero], axis=0)
                    for a in (-1, 0, 1):
                        acc[s] = acc[s] + taps[3 * (a + 1) + e + 1] * tall[1 + a : 15 + a]
            put_canvas(c_ref, crop, lanes, acc[0], acc[1], mask_ref)

        @pl.loop(0, locals_)
        def _(n):
            rows = pl.ds(globals_ * 32 + n * 8, 8)
            u = u_ref[rows, :, lanes]
            acc = u + shift
            for e in (-1, 0, 1):
                side = u if e == 0 else pltpu.roll(u, 7 if e == 1 else 1, 1)
                for a in (-1, 0, 1):
                    moved = side if a == 0 else jnp.roll(side, -a, axis=0)
                    acc = acc + taps[3 * (a + 1) + e + 1] * moved
            c_ref[rows, :, lanes] = acc * mask_ref[rows]


def conv_backward(d_ref, u_ref, du_ref, small_ref, acc_ref, globals_, locals_):
    j14 = lax.broadcasted_iota(jnp.int32, (14, 8, LANES), 1)
    for g in range(GROUPS):
        lanes = pl.ds(g * LANES, LANES)
        taps = [small_ref[K_ROW + t : K_ROW + t + 1, lanes][None] for t in range(9)]
        nothing = tuple(jnp.zeros((8, LANES), F32) for _ in range(10))

        def one_crop(crop, sums):
            sums = list(sums)
            left, right = canvas(d_ref, crop, lanes)
            own = canvas(u_ref, crop, lanes)
            zero = jnp.zeros((1, 8, LANES), F32)
            acc = [left, right]
            sums[9] = sums[9] + jnp.sum(left + right, axis=0)
            for e in (-1, 0, 1):
                for s, side in enumerate(shifted_cols(left, right, j14, -e)):
                    tall = jnp.concatenate([zero, side, zero], axis=0)
                    for a in (-1, 0, 1):
                        t = 3 * (a + 1) + e + 1
                        moved = tall[1 - a : 15 - a]
                        acc[s] = acc[s] + taps[t] * moved
                        sums[t] = sums[t] + jnp.sum(own[s] * moved, axis=0)
            base = crop * 32
            for w in range(4):
                side = acc[w % 2]
                half = side[(w // 2) * 7 : (w // 2) * 7 + 7]
                du_ref[pl.ds(base + 8 * w, 8), :, lanes] = jnp.concatenate([half, zero], axis=0)
            return tuple(sums)

        def one_local(n, sums):
            sums = list(sums)
            rows = pl.ds(globals_ * 32 + n * 8, 8)
            d = d_ref[rows, :, lanes]
            own = u_ref[rows, :, lanes]
            acc = d
            sums[9] = sums[9] + jnp.sum(d, axis=0)
            for e in (-1, 0, 1):
                side = d if e == 0 else pltpu.roll(d, 7 if e == -1 else 1, 1)
                for a in (-1, 0, 1):
                    t = 3 * (a + 1) + e + 1
                    moved = side if a == 0 else jnp.roll(side, a, axis=0)
                    acc = acc + taps[t] * moved
                    sums[t] = sums[t] + jnp.sum(own * moved, axis=0)
            du_ref[rows, :, lanes] = acc
            return tuple(sums)

        sums = lax.fori_loop(0, globals_, one_crop, nothing)
        sums = lax.fori_loop(0, locals_, one_local, sums)
        for t in range(10):
            acc_ref[t, :, lanes] = sums[t]


def spatial_forward(q_ref, k_ref, v_ref, mask_ref, o_ref, p_ref, windows):
    masks = head_masks(CELL)

    def step(w):
        rows = pl.ds(w * CELL, CELL)
        m = mask_ref[rows, :]
        valid = jnp.concatenate([m, m], axis=1) > 0.5
        for g in range(GROUPS):
            lanes = pl.ds(g * LANES, LANES)
            s = mm_nt(k_ref[rows, lanes], spread(q_ref[rows, lanes], masks))
            s = jnp.where(valid, s * SCALE, -1e9)
            e = jnp.exp(s - jnp.max(s, axis=0, keepdims=True))
            p = (e / jnp.sum(e, axis=0, keepdims=True)).astype(BF)
            p_ref[w, g] = p
            o_ref[rows, lanes] = gather_heads(mm_tn(p, v_ref[rows, lanes]), masks).astype(BF)

    several(windows, MIX_UNROLL, step)


def plus(a, b):
    return b if a is None else a + b


def pick(count, at_once):
    while count % at_once:
        at_once -= 1
    return at_once


def spatial_backward(q_ref, k_ref, v_ref, p_ref, do_ref, dq_ref, dk_ref, dv_ref, acc_ref, s_ref, windows, wait, send):
    masks = head_masks(CELL)
    lanes = [pl.ds(g * LANES, LANES) for g in range(GROUPS)]
    at_once = pick(windows, MIX_UNROLL)
    for ready in wait:
        ready()

    @pl.loop(0, windows // at_once)
    def _(i):
        sums = [None] * GROUPS
        for w in [i * at_once + j for j in range(at_once)]:
            rows = pl.ds(w * CELL, CELL)
            for g in range(GROUPS):
                p = p_ref[w, g]
                dos = spread(do_ref[rows, lanes[g]], masks)
                dp = mm_nt(v_ref[rows, lanes[g]], dos)
                pf = p.astype(F32)
                total = jnp.sum(pf * dp, axis=0, keepdims=True)
                ds = (pf * (dp - total) * SCALE).astype(BF)
                s_ref[w, g] = ds
                dv = mm(p, dos)
                sums[g] = plus(sums[g], fold8(dv))
                dv_ref[rows, lanes[g]] = dv.astype(BF)
                dk_ref[rows, lanes[g]] = mm(ds, spread(q_ref[rows, lanes[g]], masks)).astype(BF)
        for g in range(GROUPS):
            acc_ref[1, :, lanes[g]] += sums[g]

    send[1]()
    send[2]()

    @pl.loop(0, windows // at_once)
    def _(i):
        sums = [None] * GROUPS
        for w in [i * at_once + j for j in range(at_once)]:
            rows = pl.ds(w * CELL, CELL)
            for g in range(GROUPS):
                dq = gather_heads(mm_tn(s_ref[w, g], k_ref[rows, lanes[g]]), masks)
                sums[g] = plus(sums[g], fold8(dq))
                dq_ref[rows, lanes[g]] = dq.astype(BF)
        for g in range(GROUPS):
            acc_ref[0, :, lanes[g]] += sums[g]

    send[0]()


def same_head():
    a = lax.broadcasted_iota(jnp.int32, (LANES, LANES), 0) // HEAD
    b = lax.broadcasted_iota(jnp.int32, (LANES, LANES), 1) // HEAD
    return a == b


def over_crops(globals_, locals_, step):
    several(globals_, 3, lambda n: step(n, n * 4 * CELL, 4 * CELL))
    several(locals_, 9, lambda n: step(globals_ + n, globals_ * 4 * CELL + n * CELL, CELL))


def channel_forward(q_ref, k_ref, v_ref, mask_ref, o_ref, p_ref, globals_, locals_):
    same = same_head()
    lanes = [pl.ds(g * LANES, LANES) for g in range(GROUPS)]

    def weigh(n, start, count):
        rows = pl.ds(start, count)
        m = mask_ref[rows, :].astype(BF)
        for g in range(GROUPS):
            s = mm_tn(v_ref[rows, lanes[g]], k_ref[rows, lanes[g]] * m)
            s = jnp.where(same, s * SCALE, -jnp.inf)
            e = jnp.exp(s - jnp.max(s, axis=0, keepdims=True))
            p_ref[n, g] = (e / jnp.sum(e, axis=0, keepdims=True)).astype(BF)

    over_crops(globals_, locals_, weigh)

    def step(n, start, count):
        rows = pl.ds(start, count)
        for g in range(GROUPS):
            o_ref[rows, lanes[g]] = mm(q_ref[rows, lanes[g]], p_ref[n, g]).astype(BF)

    over_crops(globals_, locals_, step)


def channel_backward(
    q_ref, k_ref, v_ref, mask_ref, p_ref, do_ref, dq_ref, dk_ref, dv_ref, acc_ref, s_ref, globals_, locals_, wait, send
):
    lanes = [pl.ds(g * LANES, LANES) for g in range(GROUPS)]

    def slope(n, start, count):
        rows = pl.ds(start, count)
        for g in range(GROUPS):
            dp = mm_tn(q_ref[rows, lanes[g]], do_ref[rows, lanes[g]])
            pf = p_ref[n, g].astype(F32)
            total = jnp.sum(pf * dp, axis=0, keepdims=True)
            s_ref[n, g] = (pf * (dp - total) * SCALE).astype(BF)

    for ready in wait[:3]:
        ready()
    over_crops(globals_, locals_, slope)
    for ready in wait[3:]:
        ready()

    def step(n, start, count):
        rows = pl.ds(start, count)
        mf = mask_ref[rows, :]
        m = mf.astype(BF)
        for g in range(GROUPS):
            ds = s_ref[n, g]
            dq = mm_nt(do_ref[rows, lanes[g]], p_ref[n, g])
            dk = mm(v_ref[rows, lanes[g]], ds) * mf
            dv = mm_nt(k_ref[rows, lanes[g]] * m, ds)
            acc_ref[0, :, lanes[g]] += fold8(dq)
            acc_ref[1, :, lanes[g]] += fold8(dv)
            dq_ref[rows, lanes[g]] = dq.astype(BF)
            dk_ref[rows, lanes[g]] = dk.astype(BF)
            dv_ref[rows, lanes[g]] = dv.astype(BF)

    over_crops(globals_, locals_, step)
    for go in send:
        go()


def table_of(tabs):
    total = tabs[0].astype(F32)
    for d in range(1, tabs.shape[0]):
        total = total + tabs[d].astype(F32)
    return total


CHUNKS = 3


def crops_out(read, glob_ref, loc_ref, globals_, locals_, tmp):
    @pl.loop(0, globals_ * 2)
    def _(half):
        crop, below = half // 2, half % 2
        for i in range(WIN):
            tmp[i, 0:WIN, :] = read(half * 16 + i)[:WIN]
            tmp[i, WIN:SIDE, :] = read(half * 16 + 8 + i)[:WIN]
        for i in range(WIN):
            glob_ref[crop, below * WIN + i] = tmp[i].astype(glob_ref.dtype)

    @pl.loop(0, locals_)
    def _(n):
        for i in range(WIN):
            loc_ref[n, i] = read(globals_ * 32 + n * 8 + i)[:WIN].astype(loc_ref.dtype)


def crops_in(glob_ref, loc_ref, write, globals_, locals_, tmp):
    tmp[...] = jnp.zeros_like(tmp)
    patch = lax.broadcasted_iota(jnp.int32, (8, C), 0) < WIN
    empty = jnp.zeros((8, C), F32)

    @pl.loop(0, globals_ * 2)
    def _(half):
        crop, below = half // 2, half % 2
        for i in range(WIN):
            tmp[i, 0:SIDE, :] = glob_ref[crop, below * WIN + i].astype(F32)
        for i in range(WIN):
            write(half * 16 + i, jnp.where(patch, tmp[i, 0:8, :], 0.0))
            write(half * 16 + 8 + i, jnp.where(patch, tmp[i, WIN : WIN + 8, :], 0.0))
        write(half * 16 + WIN, empty)
        write(half * 16 + 8 + WIN, empty)

    tmp[...] = jnp.zeros_like(tmp)

    @pl.loop(0, locals_)
    def _(n):
        for i in range(WIN):
            tmp[i, 0:WIN, :] = loc_ref[n, i].astype(F32)
        for i in range(WIN):
            write(globals_ * 32 + n * 8 + i, tmp[i, 0:8, :])
        write(globals_ * 32 + n * 8 + WIN, empty)


CROP_TMP = pltpu.VMEM((WIN, 16, C), F32)


def crop_outs(globals_, locals_, kind):
    return [shape((globals_, SIDE, SIDE, C), kind), shape((locals_, WIN, WIN, C), kind)]


def chunks_of(rows):
    size = rows // CHUNKS
    return [pl.ds(i * size, size) for i in range(CHUNKS)]


def tiles_of(here):
    return pl.ds(here.start // 8, here.size // 8)


def attention_forward(sizes, kind, me, u, mask, bufs, first, last=None):
    globals_, locals_, shards = sizes
    windows = 4 * globals_ + locals_
    rows = windows * CELL
    part = C // shards
    chunks = chunks_of(rows)

    def kernel(me_ref, feeds, sends, held, packs, w, tabs, sem, sem2, *more):
        r_out, small_out, c_out, n_out, q_out, k_out, v_out, o_out, p_out = sends[:9]
        r_ref, small_ref, c_ref, n_ref, q_ref, k_ref, v_ref, o_ref, p_ref = [v.ref for v in sends[:9]]
        feeds[0].start()
        tab = start_weights(held, me_ref, [(first + 4 * part, TAB, lambda d: tabs.at[d])], sem2)
        feeds[1].start()
        plan = [(first + i * part, part, rows_of(w, i, part)) for i in range(4)]
        copies = start_weights(held, me_ref, plan, sem)
        if mask is not None:
            u_ref, mask_ref = feeds[0].wait(), feeds[1].wait()
        else:
            u_ref, mask_ref = sends[9].ref, sends[10].ref
            at = lax.broadcasted_iota(jnp.int32, (CELL, LANES), 0)
            for i in range(windows):
                inside = jnp.logical_and(at // 8 < me_ref[1 + 2 * i], at % 8 < me_ref[2 + 2 * i])
                mask_ref[i * CELL : (i + 1) * CELL, :] = jnp.where(inside, 1.0, 0.0)
            sends[10].start()
            glob_ref, loc_ref = feeds[0].wait(), feeds[1].wait()

            def write(tile, v):
                u_ref[tile] = v * wide(mask_ref[pl.ds(pl.multiple_of(tile * 8, 8), 8), :])

            crops_in(glob_ref, loc_ref, write, globals_, locals_, more[0])
            sends[9].start()
        for copy in tab:
            copy.wait()
        small_ref[...] = table_of(tabs)
        small_out.start()
        conv_forward(u_ref, c_ref, small_ref, mask_ref.reshape(windows * 8, 8, LANES), globals_, locals_)
        c_out.start()
        gain = small_ref[G_ROW : G_ROW + 1]
        shift = small_ref[V_ROW + 1 : V_ROW + 2]

        def step(i):
            x = c_ref[pl.ds(i * 8, 8)].reshape(CELL, C)
            xhat, _ = norm_parts(x)
            n_ref[pl.ds(i * CELL, CELL), :] = (xhat * gain + shift).astype(BF)

        several(windows, NORM_UNROLL, step)
        n_out.start()
        for copy in copies:
            copy.wait()
        for here in chunks:
            n1 = n_ref[here, :]
            q_ref[here, :] = (mm(n1, w[0]) + small_ref[V_ROW + 2 : V_ROW + 3]).astype(BF)
            k_ref[here, :] = mm(n1, w[1]).astype(BF)
            v_ref[here, :] = (mm(n1, w[2]) + small_ref[V_ROW + 3 : V_ROW + 4]).astype(BF)
        for send in (q_out, k_out, v_out):
            send.start()
        if kind == 0:
            spatial_forward(q_ref, k_ref, v_ref, mask_ref, o_ref, p_ref, windows)
        else:
            channel_forward(q_ref, k_ref, v_ref, mask_ref, o_ref, p_ref, globals_, locals_)
        p_out.start()
        o_out.start()
        for i, here in enumerate(chunks):
            c = c_ref[tiles_of(here)].reshape(here.size, C)
            r_ref[here, :] = c + mm(o_ref[here, :], w[3]) + small_ref[V_ROW + 4 : V_ROW + 5]
            r_out.start(i, here)
        if last is not None:
            w1, w2, sem_w, x_ref, tmp = more
            late = start_ffn_weights(held, me_ref, last, part, FF // shards, w1, w2, sem_w)
            ffn_stage(sizes, r_ref, mask_ref, small_ref, w1, w2, late, sends[9:], x_ref, tmp)

    low = shape((rows, C), BF)
    probs = (windows, GROUPS, CELL, PER * CELL) if kind == 0 else (globals_ + locals_, GROUPS, LANES, LANES)
    outs = [
        shape((rows, C), F32), shape((TAB, C), F32), shape((windows * 8, 8, C), F32),
        low, low, low, low, low, shape(probs, BF),
    ]
    scratch = [
        pltpu.VMEM((4, C, C), BF),
        pltpu.VMEM((shards, TAB, C), BF),
        pltpu.SemaphoreType.DMA,
        pltpu.SemaphoreType.DMA,
    ]
    if mask is None:
        outs += [shape((windows * 8, 8, C), F32), shape((rows, LANES), F32)]
        scratch.append(CROP_TMP)
    if last is not None:
        outs += ffn_outs(sizes, True)
        scratch += ffn_scratch(sizes, True)
    ins = list(u) if mask is None else [u, mask]
    return call(kernel, me, ins, outs, held=bufs, scratch=scratch, micros=FORWARD)


def start_ffn_weights(held, me_ref, where, part, deep, w1, w2, sem):
    n1, first1, n2, first2 = where
    plan1 = [(first1 + i * part, part, rows_of(w1, i, part)) for i in range(FF // C)]
    plan2 = [(first2, deep, lambda d: w2.at[pl.ds(pl.multiple_of(d * deep, deep), deep), :])]
    if n2 == 0:
        return start_weights(held[:n1], me_ref, plan1 + plan2, sem)
    return start_weights(held[:n1], me_ref, plan1, sem) + start_weights(held[n1 : n1 + n2], me_ref, plan2, sem)


def ffn_stage(sizes, r_ref, mask_ref, small_ref, w1, w2, copies, sends, x_ref, tmp):
    globals_, locals_, _ = sizes
    windows = 4 * globals_ + locals_
    n_out, g_out, s_out = sends[:3]
    n_ref, g_ref, s_ref = [v.ref for v in sends[:3]]
    gain = small_ref[G_ROW + 1 : G_ROW + 2]
    shift = small_ref[V_ROW + 5 : V_ROW + 6]

    def step(i):
        here = pl.ds(i * CELL, CELL)
        xhat, _ = norm_parts(r_ref[here, :])
        n_ref[here, :] = (xhat * gain + shift).astype(BF)

    several(windows, NORM_UNROLL, step)
    n_out.start()
    for copy in copies:
        copy.wait()
    for i, here in enumerate(chunks_of(windows * CELL)):
        n2 = n_ref[here, :]
        for t in range(FF // C):
            h = mm(n2, w1[t]) + small_ref[B_ROW + t : B_ROW + t + 1]
            h2 = h * h
            inner = 0.7978845608 + (0.7978845608 * 0.044715) * h2
            a = 0.5 + 0.5 * jnp.tanh(h * inner)
            g = h * a
            slope = a + (g - g * a) * (6.0 * inner - 4 * 0.7978845608)
            g_ref[here, t * C : (t + 1) * C] = g.astype(BF)
            s_ref[here, t * C : (t + 1) * C] = slope.astype(BF)
        g_out.start(i, here)
        s_out.start(i, here)
        y = r_ref[here, :] + mm(g_ref[here, :], w2[...]) + small_ref[V_ROW + 6 : V_ROW + 7]
        x_ref[here, :] = y * wide(mask_ref[here, :])
        if tmp is None:
            sends[3].start(i, here)
    if tmp is not None:
        crops_out(
            lambda tile: x_ref[pl.ds(pl.multiple_of(tile * 8, 8), 8), :],
            sends[3].ref, sends[4].ref, globals_, locals_, tmp,
        )
        sends[3].start()
        sends[4].start()


def ffn_outs(sizes, crops):
    globals_, locals_, _ = sizes
    rows = (4 * globals_ + locals_) * CELL
    high = shape((rows, FF), BF)
    out = crop_outs(globals_, locals_, BF) if crops else [shape((rows, C), F32)]
    return [shape((rows, C), BF), high, high] + out


def ffn_scratch(sizes, crops):
    rows = (4 * sizes[0] + sizes[1]) * CELL
    scratch = [pltpu.VMEM((FF // C, C, C), BF), pltpu.VMEM((FF, C), BF), pltpu.SemaphoreType.DMA]
    return scratch + ([pltpu.VMEM((rows, C), F32), pltpu.VMEM((WIN, SIDE, C), F32)] if crops else [])


def ffn_forward(sizes, me, r, mask, small, bufs, where):
    shards = sizes[2]

    def kernel(me_ref, feeds, sends, held, packs, w1, w2, sem):
        r_in, m_in, small_in = feeds
        small_in.start()
        r_in.start()
        copies = start_ffn_weights(held, me_ref, where, C // shards, FF // shards, w1, w2, sem)
        m_in.start()
        small_in.wait()
        r_in.wait()
        m_in.wait()
        ffn_stage(sizes, r_in.ref, m_in.ref, small_in.ref, w1, w2, copies, sends, sends[3].ref, None)

    return call(
        kernel, me, [r, mask, small], ffn_outs(sizes, False), held=bufs, scratch=ffn_scratch(sizes, False),
        micros=FORWARD,
    )


def pack_outs(shards, count, relative):
    if relative:
        return [shape((4, count, C), BF)] * 2
    return [shape((shards, count, C), BF)]


def send_pack(dw, outs, rows, sem):
    each = len(outs) == 2
    copies = []
    for i, out in enumerate(outs):
        src = dw.at[pl.ds(4 * i, 4), rows] if each else dw.at[:, rows]
        copies.append(pltpu.make_async_copy(src, out.at[:, rows], sem))
    for copy in copies:
        copy.start()
    return copies


def ffn_backward(sizes, me, relative, dy, n2, g, slope, mask, w_ffn, where, rest, deps):
    raw = isinstance(dy, tuple)
    globals_, locals_, shards = sizes
    windows = 4 * globals_ + locals_
    rows = windows * CELL
    part = C // shards
    deep = FF // shards
    count = 4 * part + deep
    chunks = chunks_of(rows)
    packs = pack_outs(shards, count, relative)
    n_ffn = len(w_ffn)

    def kernel(me_ref, feeds, sends, held, dw_out, w1, w2, dw, dyl, dh, acc, acc1, sem, sem2, *more):
        n_in, g_in, s_in, m_in = feeds[:4]
        dy_feeds = feeds[4 : 6 if raw else 5]
        ds_out = sends[0]
        ds_ref = ds_out.ref
        more = list(more)
        tmp = more.pop(0) if raw else None
        dy_ref = more.pop(0) if raw else dy_feeds[0].ref
        dn_ref = sends[1].ref if rest is None else more.pop(0)
        for feed in dy_feeds:
            feed.start()
        m_in.start()
        copies = start_ffn_weights(held[:n_ffn], me_ref, where, part, deep, w1, w2, sem)
        for i, here in enumerate(chunks):
            s_in.start(i, here)
        n_in.start()
        g_in.start()
        acc[...] = jnp.zeros_like(acc)
        acc1[...] = jnp.zeros_like(acc1)
        mask_ref = m_in.wait()
        if raw:

            def write(tile, v):
                dy_ref[pl.ds(pl.multiple_of(tile * 8, 8), 8), :] = v

            crops_in(dy_feeds[0].wait(), dy_feeds[1].wait(), write, globals_, locals_, tmp)
        else:
            dy_feeds[0].wait()

        def step(i):
            here = pl.ds(i * CELL, CELL)
            d = dy_ref[here, :] * wide(mask_ref[here, :])
            dyl[here, :] = d.astype(BF)
            acc[...] += fold8(d)

        several(windows, NORM_UNROLL, step)
        for copy in copies:
            copy.wait()
        for i, here in enumerate(chunks):
            s_ref = s_in.wait(i)
            for t in range(FF // C):
                cols = slice(t * C, (t + 1) * C)
                d = mm_nt(dyl[here, :], w2[cols, :]) * s_ref[here, cols].astype(F32)
                acc1[:, cols] += fold8(d)
                dh[here, cols] = d.astype(BF)
            dn = None
            for t in range(FF // C):
                one = mm_nt(dh[here, t * C : (t + 1) * C], w1[t])
                dn = one if dn is None else dn + one
            dn_ref[here, :] = dn
            if rest is None:
                sends[1].start(i, here)

        if rest is not None:
            wp, acc2, sem3 = more
            r_in, small_in = feeds[-2:]
            r_in.start()
            small_in.start()
            plan = [(rest[3] + 3 * part, part, rows_of(wp, 0, part))]
            late = start_weights(held[n_ffn : n_ffn + len(rest[2])], me_ref, plan, sem3)
        n_ref = n_in.wait()
        g_ref = g_in.wait()
        going = []
        for t in range(FF // C):
            cols = slice(t * C, (t + 1) * C)
            one = mm_tn(n_ref[...], dh[:, cols]).astype(BF)
            for d in range(shards):
                dw[slot_of(d, me_ref, relative), t * part : (t + 1) * part, :] = one[d * part : (d + 1) * part]
            going += send_pack(dw, dw_out, pl.ds(t * part, part), sem2)
        for t in range(FF // C):
            cols = slice(t * C, (t + 1) * C)
            two = mm_tn(g_ref[:, cols], dyl[...]).astype(BF)
            for d in range(C // deep):
                here = pl.ds(4 * part, deep)
                dw[slot_of(t * (C // deep) + d, me_ref, relative), here, :] = two[d * deep : (d + 1) * deep]
        going += send_pack(dw, dw_out, pl.ds(4 * part, deep), sem2)
        ds_ref[0:1, :] = jnp.sum(acc[...], axis=0, keepdims=True)
        for t in range(FF // C):
            ds_ref[1 + t : 2 + t, :] = jnp.sum(acc1[:, t * C : (t + 1) * C], axis=0, keepdims=True)
        ds_ref[5:8, :] = jnp.zeros((3, C), F32)
        ds_out.start()
        if rest is not None:
            r_in.wait()
            gain = small_in.wait()[G_ROW + 1 : G_ROW + 2]
            ready = [Ready(v) for v in (dn_ref, dy_ref, r_in.ref, mask_ref)]
            norm_two_stage(rows, ready, gain, wp, late, acc2, sends[1:])
        for copy in going:
            copy.wait()

    full = pltpu.VMEM((rows, C), F32)
    outs = [shape((8, C), F32)] + ([shape((rows, C), F32)] if rest is None else norm_two_outs(rows))
    scratch = [
        pltpu.VMEM((FF // C, C, C), BF),
        pltpu.VMEM((FF, C), BF),
        pltpu.VMEM((shards, count, C), BF),
        pltpu.VMEM((rows, C), BF),
        pltpu.VMEM((rows, FF), BF),
        pltpu.VMEM((8, C), F32),
        pltpu.VMEM((8, FF), F32),
        pltpu.SemaphoreType.DMA,
        pltpu.SemaphoreType.DMA,
    ] + ([CROP_TMP, full] if raw else [])
    ins = [n2, g, slope, mask, *(dy if raw else [dy])]
    held = list(w_ffn)
    if rest is not None:
        scratch += [full, *NORM_TWO]
        ins += rest[:2]
        held += rest[2]
    return call(
        kernel, me, ins, outs, held=held + list(deps), packs=packs, scratch=scratch, micros=BACKWARD,
    )


def norm_two_stage(rows, feeds, gain, wp, copies, acc, sends):
    dn_in, dy_in, r_in, m_in = feeds
    dn_ref, dy_ref, r_ref, mask_ref = [v.ref for v in feeds]
    dr_out, drl_out, do_out, ds_out = sends
    dr_ref, drl, do_ref, ds_ref = [v.ref for v in sends]
    chunks = chunks_of(rows)
    each = chunks[0].size // CELL
    acc[...] = jnp.zeros_like(acc)
    for i, here in enumerate(chunks):
        for feed in feeds:
            feed.wait(i)
        sums = [None] * 3
        for w in range(i * each, (i + 1) * each):
            at = pl.ds(w * CELL, CELL)
            dn = dn_ref[at, :]
            xhat, rstd = norm_parts(r_ref[at, :])
            dr = norm_back(dn, xhat, rstd, gain) + dy_ref[at, :] * wide(mask_ref[at, :])
            sums = [plus(a, fold8(v)) for a, v in zip(sums, (dn * xhat, dn, dr))]
            dr_ref[at, :] = dr
            drl[at, :] = dr.astype(BF)
        for t in range(3):
            acc[t] += sums[t]
        dr_out.start(i, here)
        drl_out.start(i, here)
        if i == 0:
            for copy in copies:
                copy.wait()
        do_ref[here, :] = mm_nt(drl[here, :], wp[0]).astype(BF)
        do_out.start(i, here)
    for t in range(3):
        ds_ref[t : t + 1, :] = jnp.sum(acc[t], axis=0, keepdims=True)
    ds_ref[3:8, :] = jnp.zeros((5, C), F32)
    ds_out.start()


def norm_two_outs(rows):
    low = shape((rows, C), BF)
    return [shape((rows, C), F32), low, low, shape((8, C), F32)]


NORM_TWO = [pltpu.VMEM((1, C, C), BF), pltpu.VMEM((3, 8, C), F32), pltpu.SemaphoreType.DMA]


def norm_two_backward(sizes, me, dn, dy, r, mask, small, w_att, first, deps):
    globals_, locals_, shards = sizes
    rows = (4 * globals_ + locals_) * CELL
    part = C // shards

    def kernel(me_ref, feeds, sends, held, packs, wp, acc, sem):
        dn_in, dy_in, r_in, m_in, small_in = feeds
        small_in.start()
        for i, here in enumerate(chunks_of(rows)):
            for feed in (r_in, dn_in, dy_in, m_in):
                feed.start(i, here)
            if i == 0:
                plan = [(first + 3 * part, part, rows_of(wp, 0, part))]
                copies = start_weights(held[: len(w_att)], me_ref, plan, sem)
        gain = small_in.wait()[G_ROW + 1 : G_ROW + 2]
        norm_two_stage(rows, feeds[:4], gain, wp, copies, acc, sends)

    return call(
        kernel, me, [dn, dy, r, mask, small], norm_two_outs(rows), held=[*w_att, *deps], micros=BACKWARD,
        scratch=NORM_TWO,
    )


def norm_one_stage(rows, feeds, gain, w, dq, dk, dv, acc, dc_out, ds_out):
    dr_in, c_in, m_in = feeds
    dr_ref, c_ref, mask_ref = [v.ref for v in feeds]
    dc, ds_ref = dc_out.ref, ds_out.ref
    chunks = chunks_of(rows)
    each = chunks[0].size // CELL
    for i, here in enumerate(chunks):
        total = mm_nt(dq(i)[here, :], w[0]) + mm_nt(dk(i)[here, :], w[1]) + mm_nt(dv(i)[here, :], w[2])
        for feed in feeds:
            feed.wait(i)
        sums = [None] * 2
        for j in range(each):
            window = i * each + j
            at, tiles = pl.ds(window * CELL, CELL), pl.ds(window * 8, 8)
            d = total[j * CELL : (j + 1) * CELL]
            xhat, rstd = norm_parts(c_ref[tiles].reshape(CELL, C))
            sums = [plus(a, fold8(v)) for a, v in zip(sums, (d * xhat, d))]
            full = norm_back(d, xhat, rstd, gain) + dr_ref[at, :]
            dc[tiles] = (full * wide(mask_ref[at, :])).reshape(8, 8, C)
        for t in range(2):
            acc[t] += sums[t]
        dc_out.start(i, tiles_of(here))
    for t in range(2):
        ds_ref[t : t + 1, :] = jnp.sum(acc[t], axis=0, keepdims=True)
    ds_ref[2:8, :] = jnp.zeros((6, C), F32)
    ds_out.start()


def start_norm_one(rows, feeds):
    dr_in, c_in, m_in = feeds
    for i, here in enumerate(chunks_of(rows)):
        dr_in.start(i, here)
        m_in.start(i, here)
        c_in.start(i, tiles_of(here))


def mix_backward(sizes, kind, me, relative, q, k, v, p, do, n1, o, drl, mask, rest, last, deps):
    globals_, locals_, shards = sizes
    windows = 4 * globals_ + locals_
    rows = windows * CELL
    part = C // shards
    packs = pack_outs(shards, 4 * part, relative)
    low = shape((rows, C), BF)
    eight = shape((8, C), F32)

    def kernel(me_ref, feeds, sends, held, dw_out, acc, slope, dw, sem, *more):
        q_in, k_in, v_in, p_in, do_in, n_in, o_in, drl_in, m_in = feeds[:9]
        q_ref, k_ref, v_ref, p_ref, do_ref, n_ref, o_ref, drl, mask_ref = [v.ref for v in feeds[:9]]
        if rest is None:
            dq, dk, dv = [v.ref for v in sends[:3]]
            go = [send.start for send in sends[:3]]
            ds_out = sends[3]
        else:
            dq, dk, dv, w, acc1, sem_w = more[:6]
            go = [lambda: None] * 3
            dc_out, ds_out, one_out = sends if last is None else [Ready(v) for v in more[6:9]]
        ds_ref = ds_out.ref
        order = (v_in, do_in, p_in, q_in, k_in) if kind == 0 else (q_in, do_in, p_in, v_in, k_in)
        waits = [feed.wait for feed in order]
        for feed in order:
            feed.start()
        if rest is None:
            m_in.start()
            waits.append(m_in.wait)
        else:
            for i, here in enumerate(chunks_of(rows)):
                m_in.start(i, here)
            plan = [(rest[4] + i * part, part, rows_of(w, i, part)) for i in range(3)]
            copies = start_weights(held[: len(rest[3])], me_ref, plan, sem_w)
            dr_in, c_in, small_in = feeds[9:12]
            small_in.start()
            waits += [m_in.wait_all, small_in.wait]
        for feed in (n_in, o_in, drl_in):
            feed.start()
        if rest is not None:
            dr_in.start()
            c_in.start()
            for feed in feeds[12:]:
                feed.start()
        acc[...] = jnp.zeros_like(acc)
        if kind == 0:
            spatial_backward(q_ref, k_ref, v_ref, p_ref, do_ref, dq, dk, dv, acc, slope, windows, waits, go)
        else:
            channel_backward(
                q_ref, k_ref, v_ref, mask_ref, p_ref, do_ref, dq, dk, dv, acc, slope, globals_, locals_, waits, go
            )
        for t in range(2):
            ds_ref[t : t + 1, :] = jnp.sum(acc[t], axis=0, keepdims=True)
        ds_ref[2:8, :] = jnp.zeros((6, C), F32)
        ds_out.start()
        for feed in (n_in, o_in, drl_in):
            feed.wait()
        going = []
        for i, left, right in ((1, n_ref, dk), (2, n_ref, dv), (0, n_ref, dq), (3, o_ref, drl)):
            one = mm_tn(left[...], right[...]).astype(BF)
            for d in range(shards):
                dw[slot_of(d, me_ref, relative), i * part : (i + 1) * part, :] = one[d * part : (d + 1) * part]
            going += send_pack(dw, dw_out, pl.ds(i * part, part), sem)
        if rest is not None:
            acc1[...] = jnp.zeros_like(acc1)
            for copy in copies:
                copy.wait()
            dr_in.wait()
            c_in.wait()
            feeds_one = [Ready(v.ref) for v in (dr_in, c_in, m_in)]
            gain = small_in.ref[G_ROW : G_ROW + 1]
            norm_one_stage(
                rows, feeds_one, gain, w, lambda i: dq, lambda i: dk, lambda i: dv, acc1, dc_out, one_out
            )
        if last is not None:
            u_ref, ffn, two = [feed.wait() for feed in feeds[12:]]
            acck = more[9]
            conv_backward(dc_out.ref, u_ref, sends[1].ref, small_in.ref, acck, globals_, locals_)
            sends[1].start()
            write_table(sends[0].ref, acck, one_out.ref, ds_ref, two, ffn)
            sends[0].start()
        for copy in going:
            copy.wait()

    scratch = [
        pltpu.VMEM((2, 8, C), F32), pltpu.VMEM(p.shape, BF), pltpu.VMEM((shards, 4 * part, C), BF),
        pltpu.SemaphoreType.DMA,
    ]
    ins = [q, k, v, p, do, n1, o, drl, mask]
    if rest is None:
        outs, held = [low, low, low, eight], list(deps)
    else:
        outs, held = [shape((windows * 8, 8, C), F32), eight, eight], [*rest[3], *deps]
        ins += [rest[0], rest[1], rest[2]]
        scratch += [pltpu.VMEM((rows, C), BF)] * 3
        scratch += [pltpu.VMEM((3, C, C), BF), pltpu.VMEM((2, 8, C), F32), pltpu.SemaphoreType.DMA]
    if last is not None:
        ins += last
        outs = [shape((TAB, C), F32), shape((windows * 8, 8, C), F32)]
        eight = pltpu.VMEM((8, C), F32)
        scratch += [pltpu.VMEM((windows * 8, 8, C), F32), eight, eight, pltpu.VMEM((10, 8, C), F32)]
    return call(kernel, me, ins, outs, held=held, packs=packs, scratch=scratch, micros=BACKWARD)


class Ready:
    def __init__(self, ref):
        self.ref = ref

    def start(self, k=0, part=None):
        pass

    def wait(self, k=0):
        return self.ref


def norm_one_backward(sizes, me, dr, c, dq, dk, dv, mask, small, bufs, first, deps):
    globals_, locals_, shards = sizes
    windows = 4 * globals_ + locals_
    rows = windows * CELL
    part = C // shards

    def kernel(me_ref, feeds, sends, held, packs, w, acc, sem):
        dr_in, c_in, dq_in, dk_in, dv_in, m_in, small_in = feeds
        plan = [(first + i * part, part, rows_of(w, i, part)) for i in range(3)]
        copies = start_weights(held[: len(bufs)], me_ref, plan, sem)
        small_in.start()
        for i, here in enumerate(chunks_of(rows)):
            for feed in (dq_in, dk_in, dv_in):
                feed.start(i, here)
        start_norm_one(rows, (dr_in, c_in, m_in))
        acc[...] = jnp.zeros_like(acc)
        gain = small_in.wait()[G_ROW : G_ROW + 1]
        for copy in copies:
            copy.wait()
        norm_one_stage(rows, (dr_in, c_in, m_in), gain, w, dq_in.wait, dk_in.wait, dv_in.wait, acc, *sends)

    return call(
        kernel, me, [dr, c, dq, dk, dv, mask, small], [shape((windows * 8, 8, C), F32), shape((8, C), F32)],
        held=[*bufs, *deps], micros=BACKWARD,
        scratch=[pltpu.VMEM((3, C, C), BF), pltpu.VMEM((2, 8, C), F32), pltpu.SemaphoreType.DMA],
    )


def write_table(tab, acck, one, mix, two, ffn):
    rows = [jnp.sum(acck[t], axis=0, keepdims=True) for t in range(10)]
    rows += [one[1:2, :], mix[0:1, :], mix[1:2, :], two[2:3, :], two[1:2, :], ffn[0:1, :], one[0:1, :], two[0:1, :]]
    rows += [ffn[1 + t : 2 + t, :] for t in range(FF // C)]
    tab[...] = jnp.zeros_like(tab)
    for t, row in enumerate(rows):
        tab[t : t + 1, :] = row


def position_backward(sizes, me, dc, u, mask, small, ds_ffn, ds_two, ds_mix, ds_one, last, deps):
    globals_, locals_, _ = sizes
    windows = 4 * globals_ + locals_

    def kernel(me_ref, feeds, sends, held, packs, acck, *more):
        dc_ref, u_ref, small_ref, ffn, two, mix, one = [v.ref for v in feeds[:7]]
        tab = sends[0].ref
        du_ref = more[0] if last else sends[1].ref
        for feed in feeds:
            feed.start()
        for feed in feeds:
            feed.wait()
        conv_backward(dc_ref, u_ref, du_ref, small_ref, acck, globals_, locals_)
        if last:
            mask_ref = feeds[7].ref

            def read(tile):
                here = pl.ds(pl.multiple_of(tile * 8, 8), 8)
                return du_ref[tile] * wide(mask_ref[here, :])

            crops_out(read, sends[1].ref, sends[2].ref, globals_, locals_, more[1])
            sends[2].start()
        sends[1].start()
        write_table(tab, acck, one, mix, two, ffn)
        sends[0].start()

    full = (windows * 8, 8, C)
    ins = [dc, u, small, ds_ffn, ds_two, ds_mix, ds_one]
    outs = [shape((TAB, C), F32)]
    scratch = [pltpu.VMEM((10, 8, C), F32)]
    if last:
        ins.append(mask)
        outs += crop_outs(globals_, locals_, F32)
        scratch += [pltpu.VMEM(full, F32), pltpu.VMEM((WIN, SIDE, C), F32)]
    else:
        outs.append(shape(full, F32))
    return call(kernel, me, ins, outs, held=deps, scratch=scratch, micros=BACKWARD)


def join(values, deps):
    values, deps = list(values), list(deps)

    def kernel(*refs):
        pass

    return pl.pallas_call(
        kernel,
        out_shape=[shape(v.shape, v.dtype) for v in values],
        in_specs=[HELD] * (len(values) + len(deps)),
        out_specs=[HELD] * len(values),
        input_output_aliases={i: i for i in range(len(values))},
    )(*values, *deps)


def place_and_extents(index, extent, globals_):
    sizes = jnp.concatenate([jnp.full((globals_ * 4, 2), WIN, jnp.int32), extent.astype(jnp.int32)], axis=0)
    return jnp.concatenate([index.astype(jnp.int32).reshape(1), sizes.reshape(-1)])


def layer(sizes, me, tokens, cotangent, plan):
    windows = 4 * sizes[0] + sizes[1]
    rows = windows * CELL
    dy = cotangent
    kept = []
    places = []
    mask = None
    u = tokens
    for b in range(2):
        att, att_first = plan.att_weights(b, u)
        if b == 0:
            r, small, *saved, u, mask = attention_forward(sizes, b, me, u, mask, att, att_first)
            ffn, where = plan.ffn_weights(b, r)
            n2, g, slope, out = ffn_forward(sizes, me, r, mask, small, ffn, where)
        else:
            ffn, where = plan.ffn_weights(b, u)
            r, small, *saved, n2, g, slope, out_global, out_local = attention_forward(
                sizes, b, me, u, mask, att, att_first, where
            )
        places.append((att, att_first, ffn, where))
        kept.append((u, r, small, saved, (n2, g, slope)))
        if b == 0:
            u = out.reshape(windows * 8, 8, C)
    out = (out_global, out_local)
    tables = [None, None]
    deps = []
    for b in (1, 0):
        u, r, small, (c, n1, q, k, v, o, p), (n2, g, slope) = kept[b]
        att, att_first, ffn, where = places[b]
        rel_ffn, rel_att = plan.relative[b]
        rest = (r, small, att, att_first)
        ds_ffn, dr, drl, do, ds_two, *dw = ffn_backward(
            sizes, me, rel_ffn, dy, n2, g, slope, mask, ffn, where, rest, deps
        )
        deps = plan.step(b, 0, dr, dw)
        mixed = (q, k, v, p, do, n1, o, drl, mask)
        rest = (dr, c, small, att, att_first)
        if b == 1:
            tables[b], *du, dw = mix_backward(
                sizes, b, me, rel_att, *mixed, rest, (u, ds_ffn, ds_two), deps
            )
            plan.step(b, 2, du[0], [dw])
        else:
            dc, ds_mix, ds_one, *dw = mix_backward(sizes, b, me, rel_att, *mixed, rest, None, deps)
            deps = plan.step(b, 2, dc, dw)
            tables[b], *du = position_backward(
                sizes, me, dc, u, mask, small, ds_ffn, ds_two, ds_mix, ds_one, True, deps
            )
        deps = plan.step(b, 4, du[0], tables)
        if b == 1:
            dy = du[0].reshape(rows, C)
    return out, du


def xor(v, axis, turn):
    size = lax.axis_size(axis)
    return lax.ppermute(v, axis, [(i, i ^ turn) for i in range(size)])


def gather_near(own):
    return [own, xor(own, "fsdp", 2), xor(own, "fsdp", 4), xor(own, "fsdp", 6)]


def gather_core(near):
    out = []
    for v in near:
        out += [v, xor(v, "fsdp", 1)]
    return out


def add(*terms):
    total = terms[0].astype(F32)
    for term in terms[1:]:
        total = total + term.astype(F32)
    return total.astype(BF)


def to_core(pack):
    return xor(pack[1], "fsdp", 1)


def to_chips(parts):
    return [xor(v, "fsdp", 2 * i + 2) for i, v in enumerate(parts[1:])]


def core_sums(pack, got):
    return [add(pack[0][i], got[i]) for i in range(4)]


def own_lanes(table):
    shards, index = lax.axis_size("fsdp"), lax.axis_index("fsdp")
    part, deep = C // shards, FF // shards
    main = lax.dynamic_slice(table, (0, 0, index * part), (2, B_ROW, part)).reshape(2, B_ROW * part)
    bias = lax.dynamic_slice(table[:, B_ROW : B_ROW + FF // C].reshape(2, FF), (0, index * deep), (2, deep))
    return jnp.concatenate([main, bias], axis=1)


class Direct:
    relative = ((True, True), (False, False))

    def __init__(self, part, deep, packs):
        self.ffn_first = 4 * part
        self.att_first = 4 * part + deep
        self.att0 = gather_near(packs[0])
        self.ffn0 = gather_near(packs[1])
        self.whole1 = lax.all_gather(packs[2], "fsdp", axis=0)

    def att_weights(self, b, u):
        if b == 0:
            return gather_core(self.att0), 0
        return [self.whole1], self.att_first

    def ffn_weights(self, b, r):
        if b == 0:
            bufs = gather_core(join(self.ffn0, [r]))
            return bufs, (len(bufs), 0, 0, self.ffn_first)
        return [self.whole1], (1, 0, 0, self.ffn_first)

    def step(self, b, stage, token, new=None):
        if (b, stage) == (1, 0):
            self.f1_own = lax.psum_scatter(new[0], "fsdp", scatter_dimension=0, tiled=True)[0]
        elif (b, stage) == (1, 2):
            self.a1_own = lax.psum_scatter(new[0], "fsdp", scatter_dimension=0, tiled=True)[0]
        elif (b, stage) == (0, 0):
            core = to_core(new)
            (f1_own,) = join([self.f1_own], [token])
            self.f0_sums = core_sums(new, core)
            self.f0_chips = to_chips(self.f0_sums)
            self.f1_sum = Spread(f1_own)
            self.f1_sum.first()
            return [*self.f0_sums, self.f1_sum.keep]
        elif (b, stage) == (0, 2):
            self.a0, self.a0_core = new, to_core(new)
            *chips, self.f1_sum.got = join([*self.f0_chips, self.f1_sum.got], [token])
            self.f0_sum = Spread(add(self.f0_sums[0], *chips))
            self.f0_sum.first()
            self.f1_sum.second()
            return [self.f0_sum.keep, self.f1_sum.half]
        elif (b, stage) == (0, 4):
            core, self.f0_sum.got, self.f1_sum.got, a1_own = join(
                [self.a0_core, self.f0_sum.got, self.f1_sum.got, self.a1_own], [token]
            )
            a1 = lax.psum(a1_own, "dp")
            a0_sums = core_sums(self.a0, core)
            a0_chips = to_chips(a0_sums)
            *tables, self.f0_sum.got, self.f1_sum.got = join(
                [*new, self.f0_sum.got, self.f1_sum.got], [a0_sums[0]]
            )
            self.f0_sum.second()
            self.f1_sum.third()
            table = jnp.stack(tables).astype(BF)
            for turn in (1, 2, 4):
                table = add(table, xor(table, "fsdp", turn))
            *a0_chips, self.f0_sum.got, table = join([*a0_chips, self.f0_sum.got, table], [])
            a0_sum = Spread(add(a0_sums[0], *a0_chips))
            a0_sum.first()
            self.f0_sum.third()
            table = own_lanes(table)
            other = xor(table, "dp", 1)
            a0_sum.got, other = join([a0_sum.got, other], [])
            a0_sum.second()
            table = add(table, other)
            table = add(table, xor(table, "dp", 2))
            a0_sum.third()
            (a1,) = join([a1], [a0_sum.whole])
            near = [self.f0_sum.result(), a0_sum.result()]
            self.done = [near, [self.f1_sum.result(), a1]], table
        return []

    def results(self):
        return self.done


class Spread:
    def __init__(self, v):
        n = v.shape[0] // 2
        bit = lax.axis_index("dp") & 1
        self.low = bit == 0
        self.keep = lax.dynamic_slice(v, (bit * n, 0), (n, C))
        self.send = lax.dynamic_slice(v, ((1 - bit) * n, 0), (n, C))

    def first(self):
        self.got = xor(self.send, "dp", 1)

    def second(self):
        self.half = add(self.keep, self.got)
        self.got = xor(self.half, "dp", 2)

    def third(self):
        self.whole = add(self.half, self.got)
        self.got = xor(self.whole, "dp", 1)

    def result(self):
        whole, other = self.whole, self.got
        return jnp.concatenate([jnp.where(self.low, whole, other), jnp.where(self.low, other, whole)])


class Plain:
    relative = ((False, False), (False, False))

    def __init__(self, part, deep, packs):
        self.packs = [[None, None], [None, None]]
        self.first = 4 * part
        self.cut = 4 * part + deep
        self.whole = [lax.all_gather(pack, "fsdp", axis=0) for pack in packs]

    def att_weights(self, b, u):
        return [self.whole[b]], self.cut

    def ffn_weights(self, b, r):
        return [self.whole[b]], (1, 0, 0, self.first)

    def step(self, b, stage, token, new=None):
        if stage in (0, 2):
            self.packs[b][stage // 2] = new[0]
        if (b, stage) == (0, 4):
            self.table = new
        return []

    def results(self):
        grads = [
            lax.psum([lax.psum_scatter(v, "fsdp", scatter_dimension=0, tiled=True)[0] for v in pair], "dp")
            for pair in self.packs
        ]
        return grads, own_lanes(lax.psum(jnp.stack(self.table).astype(BF), ("dp", "fsdp")))


def body(
    global_tokens,
    local_tokens,
    crop_extent,
    conv_weight,
    vectors,
    gains,
    qkv_weight,
    proj_weight,
    fc1_weight,
    fc1_bias,
    fc2_weight,
    global_cotangent,
    local_cotangent,
):
    shards = lax.axis_size("fsdp")
    direct = shards == 8 and lax.axis_size("dp") == 4
    part = C // shards
    globals_, locals_ = global_tokens.shape[0], local_tokens.shape[0]
    sizes = (globals_, locals_, shards)
    index = lax.axis_index("fsdp")
    me = place_and_extents(index, crop_extent, globals_)

    own_small = jnp.concatenate([conv_weight, vectors, gains], axis=1)
    own_bias = fc1_bias.reshape(2, 1, FF // shards)
    start = index * (FF // shards)

    def att(b):
        table = lax.dynamic_update_slice(jnp.zeros((TAB, C), BF), own_small[b], (0, index * part))
        table = lax.dynamic_update_slice(table, own_bias[b], (B_ROW + start // C, start % C))
        return [qkv_weight[b][:, i * C : (i + 1) * C] for i in range(3)] + [proj_weight[b], table]

    def ffn(b):
        return [fc1_weight[b][:, i * C : (i + 1) * C] for i in range(FF // C)] + [fc2_weight[b]]

    groups = [att(0), ffn(0), ffn(1) + att(1)] if direct else [ffn(b) + att(b) for b in range(2)]
    packs = [jnp.concatenate(group, axis=0) for group in groups]
    plan = (Direct if direct else Plain)(part, FF // shards, packs)
    out, grad = layer(
        sizes, me,
        (global_tokens, local_tokens),
        (global_cotangent, local_cotangent),
        plan,
    )
    grads, table = plan.results()
    deep = FF // shards

    def cut(half, start, n):
        return jnp.stack(
            [
                jnp.concatenate([g[half][(start + i) * part : (start + i + 1) * part] for i in range(n)], axis=1)
                for g in grads
            ]
        ).astype(F32)

    table = table.astype(F32)
    main = table[:, : B_ROW * part].reshape(2, B_ROW, part)
    bias = table[:, B_ROW * part :]
    fc2 = jnp.stack([g[0][4 * part :] for g in grads]).astype(F32)
    proj = jnp.stack([g[1][3 * part :] for g in grads]).astype(F32)
    return (
        out[0], out[1], grad[0], grad[1],
        main[:, 0:9], main[:, 9:16], main[:, 16:18],
        cut(1, 0, 3), proj, cut(0, 0, 4), bias, fc2,
    )


def solution(mesh):
    crops = P(("dp", "fsdp"), None, None, None)
    last = P(None, None, "fsdp")
    middle = P(None, "fsdp", None)
    return jax.shard_map(
        body,
        mesh=mesh,
        in_specs=(
            crops, crops, P(("dp", "fsdp"), None), last, last, last, middle, middle, middle,
            P(None, "fsdp"), middle, crops, crops,
        ),
        out_specs=(
            crops, crops, crops, crops, last, last, last, middle, middle, middle, P(None, "fsdp"), middle,
        ),
        check_vma=False,
    )
```

```python
import functools

import jax
import jax.numpy as jnp
from jax import lax
from jax.experimental import pallas as pl
from jax.experimental.pallas import tpu as pltpu
from jax.sharding import PartitionSpec as P

BF = jnp.bfloat16
F32 = jnp.float32
C = 512
FF = 2048
HEAD = 32
WIN = 7
SIDE = 14
CELL = 64
LANES = 128
GROUPS = C // LANES
PER = LANES // HEAD
EPS = 1e-5
SCALE = HEAD ** -0.5
MIX_UNROLL = 21
NORM_UNROLL = 7
FORWARD, BACKWARD = 1, 3
VMEM = pl.BlockSpec(memory_space=pltpu.VMEM)
HELD = pl.BlockSpec(memory_space=pl.ANY)
NT = (((1,), (1,)), ((), ()))
TN = (((0,), (0,)), ((), ()))
K_ROW, V_ROW, G_ROW, B_ROW, TAB = 0, 9, 16, 18, 32


def mm(a, b):
    return jnp.dot(a, b, preferred_element_type=F32)


def mm_nt(a, b):
    return lax.dot_general(a, b, NT, preferred_element_type=F32)


def mm_tn(a, b):
    return lax.dot_general(a, b, TN, preferred_element_type=F32)


class Copy:
    def __init__(self, src, dst, sems, ref):
        self.src, self.dst, self.sems, self.ref = src, dst, sems, ref
        self.open = {}

    def start(self, k=0, part=None):
        src, dst = (self.src, self.dst) if part is None else (self.src.at[part], self.dst.at[part])
        self.open[k] = pltpu.make_async_copy(src, dst, self.sems.at[k])
        self.open[k].start()

    def wait(self, k=0):
        self.open.pop(k).wait()
        return self.ref

    def wait_all(self):
        for k in list(self.open):
            self.wait(k)


PARTS = 4


def call(kernel, me, ins, outs, held=(), packs=(), scratch=(), micros=1, alias=None, limit=62):
    n_in, n_out, n_held, n_pack = len(ins), len(outs), len(held), len(packs)

    def body(me_ref, *refs):
        src, refs = refs[:n_in], refs[n_in:]
        held_refs, refs = refs[:n_held], refs[n_held:]
        dst, refs = refs[:n_out], refs[n_out:]
        pack_refs, refs = refs[:n_pack], refs[n_pack:]
        in_vmem, refs = refs[:n_in], refs[n_in:]
        out_vmem, refs = refs[:n_out], refs[n_out:]
        in_sem, out_sem, refs = refs[0], refs[1], refs[2:]
        feeds = [Copy(s, v, in_sem.at[i], v) for i, (s, v) in enumerate(zip(src, in_vmem))]
        sends = [Copy(v, d, out_sem.at[i], v) for i, (d, v) in enumerate(zip(dst, out_vmem))]
        kernel(me_ref, feeds, sends, held_refs, pack_refs, *refs)
        for send in sends:
            send.wait_all()

    vmem = lambda v: pltpu.VMEM(v.shape, v.dtype)
    return pl.pallas_call(
        body,
        out_shape=list(outs) + list(packs),
        in_specs=[pl.BlockSpec(memory_space=pltpu.SMEM)] + [HELD] * (n_in + n_held),
        out_specs=[HELD] * (n_out + n_pack),
        scratch_shapes=[vmem(v) for v in ins]
        + [vmem(v) for v in outs]
        + [pltpu.SemaphoreType.DMA((max(n_in, 1), PARTS)), pltpu.SemaphoreType.DMA((max(n_out, 1), PARTS))]
        + list(scratch),
        compiler_params=pltpu.CompilerParams(vmem_limit_bytes=limit * 2**20),
        cost_estimate=pl.CostEstimate(flops=int(micros * 1.1e9), bytes_accessed=2**20, transcendentals=0),
        input_output_aliases=alias or {},
    )(me, *ins, *held)


def start_weights(bufs, me_ref, plan, sem):
    copies = []
    if len(bufs) == 1:
        sources = [(d, bufs[0].at[d]) for d in range(bufs[0].shape[0])]
    else:
        sources = [(me_ref[0] ^ k, buf) for k, buf in enumerate(bufs)]
    for d, src in sources:
        for first, rows, place in plan:
            copies.append(pltpu.make_async_copy(src.at[pl.ds(first, rows), :], place(d), sem))
    for copy in copies:
        copy.start()
    return copies


def rows_of(ref, i, rows):
    return lambda d: ref.at[i, pl.ds(pl.multiple_of(d * rows, rows), rows), :]


def slot_of(d, me_ref, relative):
    if not relative:
        return d
    turn = me_ref[0] ^ d
    return (turn & 1) * 4 + (turn >> 1)


def shape(dims, kind):
    return jax.ShapeDtypeStruct(dims, kind)


def wide(m):
    return jnp.concatenate([m] * GROUPS, axis=1)


def fold8(v):
    return jnp.sum(v.reshape(v.shape[0] // 8, 8, v.shape[1]), axis=0)


def norm_parts(x):
    center = jnp.sum(x, axis=-1, keepdims=True) * (1.0 / C)
    xc = x - center
    var = jnp.sum(xc * xc, axis=-1, keepdims=True) * (1.0 / C)
    rstd = lax.rsqrt(var + EPS)
    return xc * rstd, rstd


def norm_back(dn, xhat, rstd, gain):
    gp = dn * gain
    m1 = jnp.sum(gp, axis=-1, keepdims=True) * (1.0 / C)
    m2 = jnp.sum(gp * xhat, axis=-1, keepdims=True) * (1.0 / C)
    return rstd * (gp - m1 - xhat * m2)


def several(count, at_once, step):
    while count % at_once:
        at_once -= 1

    @pl.loop(0, count // at_once)
    def _(i):
        for j in range(at_once):
            step(i * at_once + j)


def head_masks(rows):
    lane = lax.broadcasted_iota(jnp.int32, (rows, LANES), 1) // HEAD
    return [lane == h for h in range(PER)]


def spread(v, masks):
    zero = jnp.zeros_like(v)
    return jnp.concatenate([jnp.where(m, v, zero) for m in masks], axis=0)


def gather_heads(full, masks):
    n = full.shape[0] // PER
    out = full[3 * n :]
    for h in (2, 1, 0):
        out = jnp.where(masks[h], full[h * n : (h + 1) * n], out)
    return out


def shifted_cols(left, right, j, step):
    if step == 0:
        return left, right
    if step == 1:
        return (
            jnp.where(j == 6, pltpu.roll(right, 6, 1), pltpu.roll(left, 7, 1)),
            pltpu.roll(right, 7, 1),
        )
    return (
        pltpu.roll(left, 1, 1),
        jnp.where(j == 0, pltpu.roll(left, 2, 1), pltpu.roll(right, 1, 1)),
    )


def canvas(ref, crop, lanes):
    base = crop * 32
    parts = [ref[pl.ds(base + 8 * w, 7), :, lanes] for w in range(4)]
    left = jnp.concatenate([parts[0], parts[2]], axis=0)
    right = jnp.concatenate([parts[1], parts[3]], axis=0)
    return left, right


def put_canvas(ref, crop, lanes, left, right, mask_ref):
    base = crop * 32
    zero = jnp.zeros((1, 8, LANES), F32)
    for w in range(4):
        side = right if w % 2 else left
        half = side[(w // 2) * 7 : (w // 2) * 7 + 7]
        rows = pl.ds(base + 8 * w, 8)
        ref[rows, :, lanes] = jnp.concatenate([half, zero], axis=0) * mask_ref[rows]


def conv_forward(u_ref, c_ref, small_ref, mask_ref, globals_, locals_):
    j14 = lax.broadcasted_iota(jnp.int32, (14, 8, LANES), 1)
    for g in range(GROUPS):
        lanes = pl.ds(g * LANES, LANES)
        taps = [small_ref[K_ROW + t : K_ROW + t + 1, lanes][None] for t in range(9)]
        shift = small_ref[V_ROW : V_ROW + 1, lanes][None]

        @pl.loop(0, globals_)
        def _(crop):
            left, right = canvas(u_ref, crop, lanes)
            zero = jnp.zeros((1, 8, LANES), F32)
            acc = [left + shift, right + shift]
            for e in (-1, 0, 1):
                for s, side in enumerate(shifted_cols(left, right, j14, e)):
                    tall = jnp.concatenate([zero, side, zero], axis=0)
                    for a in (-1, 0, 1):
                        acc[s] = acc[s] + taps[3 * (a + 1) + e + 1] * tall[1 + a : 15 + a]
            put_canvas(c_ref, crop, lanes, acc[0], acc[1], mask_ref)

        @pl.loop(0, locals_)
        def _(n):
            rows = pl.ds(globals_ * 32 + n * 8, 8)
            u = u_ref[rows, :, lanes]
            acc = u + shift
            for e in (-1, 0, 1):
                side = u if e == 0 else pltpu.roll(u, 7 if e == 1 else 1, 1)
                for a in (-1, 0, 1):
                    moved = side if a == 0 else jnp.roll(side, -a, axis=0)
                    acc = acc + taps[3 * (a + 1) + e + 1] * moved
            c_ref[rows, :, lanes] = acc * mask_ref[rows]


def conv_backward(d_ref, u_ref, du_ref, small_ref, acc_ref, globals_, locals_):
    j14 = lax.broadcasted_iota(jnp.int32, (14, 8, LANES), 1)
    for g in range(GROUPS):
        lanes = pl.ds(g * LANES, LANES)
        taps = [small_ref[K_ROW + t : K_ROW + t + 1, lanes][None] for t in range(9)]
        nothing = tuple(jnp.zeros((8, LANES), F32) for _ in range(10))

        def one_crop(crop, sums):
            sums = list(sums)
            left, right = canvas(d_ref, crop, lanes)
            own = canvas(u_ref, crop, lanes)
            zero = jnp.zeros((1, 8, LANES), F32)
            acc = [left, right]
            sums[9] = sums[9] + jnp.sum(left + right, axis=0)
            for e in (-1, 0, 1):
                for s, side in enumerate(shifted_cols(left, right, j14, -e)):
                    tall = jnp.concatenate([zero, side, zero], axis=0)
                    for a in (-1, 0, 1):
                        t = 3 * (a + 1) + e + 1
                        moved = tall[1 - a : 15 - a]
                        acc[s] = acc[s] + taps[t] * moved
                        sums[t] = sums[t] + jnp.sum(own[s] * moved, axis=0)
            base = crop * 32
            for w in range(4):
                side = acc[w % 2]
                half = side[(w // 2) * 7 : (w // 2) * 7 + 7]
                du_ref[pl.ds(base + 8 * w, 8), :, lanes] = jnp.concatenate([half, zero], axis=0)
            return tuple(sums)

        def one_local(n, sums):
            sums = list(sums)
            rows = pl.ds(globals_ * 32 + n * 8, 8)
            d = d_ref[rows, :, lanes]
            own = u_ref[rows, :, lanes]
            acc = d
            sums[9] = sums[9] + jnp.sum(d, axis=0)
            for e in (-1, 0, 1):
                side = d if e == 0 else pltpu.roll(d, 7 if e == -1 else 1, 1)
                for a in (-1, 0, 1):
                    t = 3 * (a + 1) + e + 1
                    moved = side if a == 0 else jnp.roll(side, a, axis=0)
                    acc = acc + taps[t] * moved
                    sums[t] = sums[t] + jnp.sum(own * moved, axis=0)
            du_ref[rows, :, lanes] = acc
            return tuple(sums)

        sums = lax.fori_loop(0, globals_, one_crop, nothing)
        sums = lax.fori_loop(0, locals_, one_local, sums)
        for t in range(10):
            acc_ref[t, :, lanes] = sums[t]


def spatial_forward(q_ref, k_ref, v_ref, mask_ref, o_ref, p_ref, windows):
    masks = head_masks(CELL)

    def step(w):
        rows = pl.ds(w * CELL, CELL)
        m = mask_ref[rows, :]
        valid = jnp.concatenate([m, m], axis=1) > 0.5
        for g in range(GROUPS):
            lanes = pl.ds(g * LANES, LANES)
            s = mm_nt(k_ref[rows, lanes], spread(q_ref[rows, lanes], masks))
            s = jnp.where(valid, s * SCALE, -1e9)
            e = jnp.exp(s - jnp.max(s, axis=0, keepdims=True))
            p = (e / jnp.sum(e, axis=0, keepdims=True)).astype(BF)
            p_ref[w, g] = p
            o_ref[rows, lanes] = gather_heads(mm_tn(p, v_ref[rows, lanes]), masks).astype(BF)

    several(windows, MIX_UNROLL, step)


def plus(a, b):
    return b if a is None else a + b


def pick(count, at_once):
    while count % at_once:
        at_once -= 1
    return at_once


def spatial_backward(q_ref, k_ref, v_ref, p_ref, do_ref, dq_ref, dk_ref, dv_ref, acc_ref, s_ref, windows, wait, send):
    masks = head_masks(CELL)
    lanes = [pl.ds(g * LANES, LANES) for g in range(GROUPS)]
    at_once = pick(windows, MIX_UNROLL)
    for ready in wait:
        ready()

    @pl.loop(0, windows // at_once)
    def _(i):
        sums = [None] * GROUPS
        for w in [i * at_once + j for j in range(at_once)]:
            rows = pl.ds(w * CELL, CELL)
            for g in range(GROUPS):
                p = p_ref[w, g]
                dos = spread(do_ref[rows, lanes[g]], masks)
                dp = mm_nt(v_ref[rows, lanes[g]], dos)
                pf = p.astype(F32)
                total = jnp.sum(pf * dp, axis=0, keepdims=True)
                ds = (pf * (dp - total) * SCALE).astype(BF)
                s_ref[w, g] = ds
                dv = mm(p, dos)
                sums[g] = plus(sums[g], fold8(dv))
                dv_ref[rows, lanes[g]] = dv.astype(BF)
                dk_ref[rows, lanes[g]] = mm(ds, spread(q_ref[rows, lanes[g]], masks)).astype(BF)
        for g in range(GROUPS):
            acc_ref[1, :, lanes[g]] += sums[g]

    send[1]()
    send[2]()

    @pl.loop(0, windows // at_once)
    def _(i):
        sums = [None] * GROUPS
        for w in [i * at_once + j for j in range(at_once)]:
            rows = pl.ds(w * CELL, CELL)
            for g in range(GROUPS):
                dq = gather_heads(mm_tn(s_ref[w, g], k_ref[rows, lanes[g]]), masks)
                sums[g] = plus(sums[g], fold8(dq))
                dq_ref[rows, lanes[g]] = dq.astype(BF)
        for g in range(GROUPS):
            acc_ref[0, :, lanes[g]] += sums[g]

    send[0]()


def same_head():
    a = lax.broadcasted_iota(jnp.int32, (LANES, LANES), 0) // HEAD
    b = lax.broadcasted_iota(jnp.int32, (LANES, LANES), 1) // HEAD
    return a == b


def over_crops(globals_, locals_, step):
    several(globals_, 3, lambda n: step(n, n * 4 * CELL, 4 * CELL))
    several(locals_, 9, lambda n: step(globals_ + n, globals_ * 4 * CELL + n * CELL, CELL))


def channel_forward(q_ref, k_ref, v_ref, mask_ref, o_ref, p_ref, globals_, locals_):
    same = same_head()
    lanes = [pl.ds(g * LANES, LANES) for g in range(GROUPS)]

    def weigh(n, start, count):
        rows = pl.ds(start, count)
        m = mask_ref[rows, :].astype(BF)
        for g in range(GROUPS):
            s = mm_tn(v_ref[rows, lanes[g]], k_ref[rows, lanes[g]] * m)
            s = jnp.where(same, s * SCALE, -jnp.inf)
            e = jnp.exp(s - jnp.max(s, axis=0, keepdims=True))
            p_ref[n, g] = (e / jnp.sum(e, axis=0, keepdims=True)).astype(BF)

    over_crops(globals_, locals_, weigh)

    def step(n, start, count):
        rows = pl.ds(start, count)
        for g in range(GROUPS):
            o_ref[rows, lanes[g]] = mm(q_ref[rows, lanes[g]], p_ref[n, g]).astype(BF)

    over_crops(globals_, locals_, step)


def channel_backward(
    q_ref, k_ref, v_ref, mask_ref, p_ref, do_ref, dq_ref, dk_ref, dv_ref, acc_ref, s_ref, globals_, locals_, wait, send
):
    lanes = [pl.ds(g * LANES, LANES) for g in range(GROUPS)]

    def slope(n, start, count):
        rows = pl.ds(start, count)
        for g in range(GROUPS):
            dp = mm_tn(q_ref[rows, lanes[g]], do_ref[rows, lanes[g]])
            pf = p_ref[n, g].astype(F32)
            total = jnp.sum(pf * dp, axis=0, keepdims=True)
            s_ref[n, g] = (pf * (dp - total) * SCALE).astype(BF)

    for ready in wait[:3]:
        ready()
    over_crops(globals_, locals_, slope)
    for ready in wait[3:]:
        ready()

    def step(n, start, count):
        rows = pl.ds(start, count)
        mf = mask_ref[rows, :]
        m = mf.astype(BF)
        for g in range(GROUPS):
            ds = s_ref[n, g]
            dq = mm_nt(do_ref[rows, lanes[g]], p_ref[n, g])
            dk = mm(v_ref[rows, lanes[g]], ds) * mf
            dv = mm_nt(k_ref[rows, lanes[g]] * m, ds)
            acc_ref[0, :, lanes[g]] += fold8(dq)
            acc_ref[1, :, lanes[g]] += fold8(dv)
            dq_ref[rows, lanes[g]] = dq.astype(BF)
            dk_ref[rows, lanes[g]] = dk.astype(BF)
            dv_ref[rows, lanes[g]] = dv.astype(BF)

    over_crops(globals_, locals_, step)
    for go in send:
        go()


def table_of(tabs):
    total = tabs[0].astype(F32)
    for d in range(1, tabs.shape[0]):
        total = total + tabs[d].astype(F32)
    return total


CHUNKS = 3


def crops_out(read, glob_ref, loc_ref, globals_, locals_, tmp):
    @pl.loop(0, globals_ * 2)
    def _(half):
        crop, below = half // 2, half % 2
        for i in range(WIN):
            tmp[i, 0:WIN, :] = read(half * 16 + i)[:WIN]
            tmp[i, WIN:SIDE, :] = read(half * 16 + 8 + i)[:WIN]
        for i in range(WIN):
            glob_ref[crop, below * WIN + i] = tmp[i].astype(glob_ref.dtype)

    @pl.loop(0, locals_)
    def _(n):
        for i in range(WIN):
            loc_ref[n, i] = read(globals_ * 32 + n * 8 + i)[:WIN].astype(loc_ref.dtype)


def crops_in(glob_ref, loc_ref, write, globals_, locals_, tmp):
    tmp[...] = jnp.zeros_like(tmp)
    patch = lax.broadcasted_iota(jnp.int32, (8, C), 0) < WIN
    empty = jnp.zeros((8, C), F32)

    @pl.loop(0, globals_ * 2)
    def _(half):
        crop, below = half // 2, half % 2
        for i in range(WIN):
            tmp[i, 0:SIDE, :] = glob_ref[crop, below * WIN + i].astype(F32)
        for i in range(WIN):
            write(half * 16 + i, jnp.where(patch, tmp[i, 0:8, :], 0.0))
            write(half * 16 + 8 + i, jnp.where(patch, tmp[i, WIN : WIN + 8, :], 0.0))
        write(half * 16 + WIN, empty)
        write(half * 16 + 8 + WIN, empty)

    tmp[...] = jnp.zeros_like(tmp)

    @pl.loop(0, locals_)
    def _(n):
        for i in range(WIN):
            tmp[i, 0:WIN, :] = loc_ref[n, i].astype(F32)
        for i in range(WIN):
            write(globals_ * 32 + n * 8 + i, tmp[i, 0:8, :])
        write(globals_ * 32 + n * 8 + WIN, empty)


CROP_TMP = pltpu.VMEM((WIN, 16, C), F32)


def crop_outs(globals_, locals_, kind):
    return [shape((globals_, SIDE, SIDE, C), kind), shape((locals_, WIN, WIN, C), kind)]


def chunks_of(rows):
    size = rows // CHUNKS
    return [pl.ds(i * size, size) for i in range(CHUNKS)]


def tiles_of(here):
    return pl.ds(here.start // 8, here.size // 8)


def attention_forward(sizes, kind, me, u, mask, bufs, first, last=None):
    globals_, locals_, shards = sizes
    windows = 4 * globals_ + locals_
    rows = windows * CELL
    part = C // shards
    chunks = chunks_of(rows)

    def kernel(me_ref, feeds, sends, held, packs, w, tabs, sem, sem2, *more):
        r_out, small_out, c_out, n_out, q_out, k_out, v_out, o_out, p_out = sends[:9]
        r_ref, small_ref, c_ref, n_ref, q_ref, k_ref, v_ref, o_ref, p_ref = [v.ref for v in sends[:9]]
        feeds[0].start()
        tab = start_weights(held, me_ref, [(first + 4 * part, TAB, lambda d: tabs.at[d])], sem2)
        feeds[1].start()
        plan = [(first + i * part, part, rows_of(w, i, part)) for i in range(4)]
        copies = start_weights(held, me_ref, plan, sem)
        if mask is not None:
            u_ref, mask_ref = feeds[0].wait(), feeds[1].wait()
        else:
            u_ref, mask_ref = sends[9].ref, sends[10].ref
            at = lax.broadcasted_iota(jnp.int32, (CELL, LANES), 0)
            for i in range(windows):
                inside = jnp.logical_and(at // 8 < me_ref[1 + 2 * i], at % 8 < me_ref[2 + 2 * i])
                mask_ref[i * CELL : (i + 1) * CELL, :] = jnp.where(inside, 1.0, 0.0)
            sends[10].start()
            glob_ref, loc_ref = feeds[0].wait(), feeds[1].wait()

            def write(tile, v):
                u_ref[tile] = v * wide(mask_ref[pl.ds(pl.multiple_of(tile * 8, 8), 8), :])

            crops_in(glob_ref, loc_ref, write, globals_, locals_, more[0])
            sends[9].start()
        for copy in tab:
            copy.wait()
        small_ref[...] = table_of(tabs)
        small_out.start()
        conv_forward(u_ref, c_ref, small_ref, mask_ref.reshape(windows * 8, 8, LANES), globals_, locals_)
        c_out.start()
        gain = small_ref[G_ROW : G_ROW + 1]
        shift = small_ref[V_ROW + 1 : V_ROW + 2]

        def step(i):
            x = c_ref[pl.ds(i * 8, 8)].reshape(CELL, C)
            xhat, _ = norm_parts(x)
            n_ref[pl.ds(i * CELL, CELL), :] = (xhat * gain + shift).astype(BF)

        several(windows, NORM_UNROLL, step)
        n_out.start()
        for copy in copies:
            copy.wait()
        for here in chunks:
            n1 = n_ref[here, :]
            q_ref[here, :] = (mm(n1, w[0]) + small_ref[V_ROW + 2 : V_ROW + 3]).astype(BF)
            k_ref[here, :] = mm(n1, w[1]).astype(BF)
            v_ref[here, :] = (mm(n1, w[2]) + small_ref[V_ROW + 3 : V_ROW + 4]).astype(BF)
        for send in (q_out, k_out, v_out):
            send.start()
        if kind == 0:
            spatial_forward(q_ref, k_ref, v_ref, mask_ref, o_ref, p_ref, windows)
        else:
            channel_forward(q_ref, k_ref, v_ref, mask_ref, o_ref, p_ref, globals_, locals_)
        p_out.start()
        o_out.start()
        for i, here in enumerate(chunks):
            c = c_ref[tiles_of(here)].reshape(here.size, C)
            r_ref[here, :] = c + mm(o_ref[here, :], w[3]) + small_ref[V_ROW + 4 : V_ROW + 5]
            r_out.start(i, here)
        if last is not None:
            w1, w2, sem_w, x_ref, tmp = more
            late = start_ffn_weights(held, me_ref, last, part, FF // shards, w1, w2, sem_w)
            ffn_stage(sizes, r_ref, mask_ref, small_ref, w1, w2, late, sends[9:], x_ref, tmp)

    low = shape((rows, C), BF)
    probs = (windows, GROUPS, CELL, PER * CELL) if kind == 0 else (globals_ + locals_, GROUPS, LANES, LANES)
    outs = [
        shape((rows, C), F32), shape((TAB, C), F32), shape((windows * 8, 8, C), F32),
        low, low, low, low, low, shape(probs, BF),
    ]
    scratch = [
        pltpu.VMEM((4, C, C), BF),
        pltpu.VMEM((shards, TAB, C), BF),
        pltpu.SemaphoreType.DMA,
        pltpu.SemaphoreType.DMA,
    ]
    if mask is None:
        outs += [shape((windows * 8, 8, C), F32), shape((rows, LANES), F32)]
        scratch.append(CROP_TMP)
    if last is not None:
        outs += ffn_outs(sizes, True)
        scratch += ffn_scratch(sizes, True)
    ins = list(u) if mask is None else [u, mask]
    return call(kernel, me, ins, outs, held=bufs, scratch=scratch, micros=FORWARD)


def start_ffn_weights(held, me_ref, where, part, deep, w1, w2, sem):
    n1, first1, n2, first2 = where
    plan1 = [(first1 + i * part, part, rows_of(w1, i, part)) for i in range(FF // C)]
    plan2 = [(first2, deep, lambda d: w2.at[pl.ds(pl.multiple_of(d * deep, deep), deep), :])]
    if n2 == 0:
        return start_weights(held[:n1], me_ref, plan1 + plan2, sem)
    return start_weights(held[:n1], me_ref, plan1, sem) + start_weights(held[n1 : n1 + n2], me_ref, plan2, sem)


def ffn_stage(sizes, r_ref, mask_ref, small_ref, w1, w2, copies, sends, x_ref, tmp):
    globals_, locals_, _ = sizes
    windows = 4 * globals_ + locals_
    n_out, g_out, s_out = sends[:3]
    n_ref, g_ref, s_ref = [v.ref for v in sends[:3]]
    gain = small_ref[G_ROW + 1 : G_ROW + 2]
    shift = small_ref[V_ROW + 5 : V_ROW + 6]

    def step(i):
        here = pl.ds(i * CELL, CELL)
        xhat, _ = norm_parts(r_ref[here, :])
        n_ref[here, :] = (xhat * gain + shift).astype(BF)

    several(windows, NORM_UNROLL, step)
    n_out.start()
    for copy in copies:
        copy.wait()
    for i, here in enumerate(chunks_of(windows * CELL)):
        n2 = n_ref[here, :]
        for t in range(FF // C):
            h = mm(n2, w1[t]) + small_ref[B_ROW + t : B_ROW + t + 1]
            h2 = h * h
            inner = 0.7978845608 + (0.7978845608 * 0.044715) * h2
            a = 0.5 + 0.5 * jnp.tanh(h * inner)
            g = h * a
            slope = a + (g - g * a) * (6.0 * inner - 4 * 0.7978845608)
            g_ref[here, t * C : (t + 1) * C] = g.astype(BF)
            s_ref[here, t * C : (t + 1) * C] = slope.astype(BF)
        g_out.start(i, here)
        s_out.start(i, here)
        y = r_ref[here, :] + mm(g_ref[here, :], w2[...]) + small_ref[V_ROW + 6 : V_ROW + 7]
        x_ref[here, :] = y * wide(mask_ref[here, :])
        if tmp is None:
            sends[3].start(i, here)
    if tmp is not None:
        crops_out(
            lambda tile: x_ref[pl.ds(pl.multiple_of(tile * 8, 8), 8), :],
            sends[3].ref, sends[4].ref, globals_, locals_, tmp,
        )
        sends[3].start()
        sends[4].start()


def ffn_outs(sizes, crops):
    globals_, locals_, _ = sizes
    rows = (4 * globals_ + locals_) * CELL
    high = shape((rows, FF), BF)
    out = crop_outs(globals_, locals_, BF) if crops else [shape((rows, C), F32)]
    return [shape((rows, C), BF), high, high] + out


def ffn_scratch(sizes, crops):
    rows = (4 * sizes[0] + sizes[1]) * CELL
    scratch = [pltpu.VMEM((FF // C, C, C), BF), pltpu.VMEM((FF, C), BF), pltpu.SemaphoreType.DMA]
    return scratch + ([pltpu.VMEM((rows, C), F32), pltpu.VMEM((WIN, SIDE, C), F32)] if crops else [])


def ffn_forward(sizes, me, r, mask, small, bufs, where):
    shards = sizes[2]

    def kernel(me_ref, feeds, sends, held, packs, w1, w2, sem):
        r_in, m_in, small_in = feeds
        small_in.start()
        r_in.start()
        copies = start_ffn_weights(held, me_ref, where, C // shards, FF // shards, w1, w2, sem)
        m_in.start()
        small_in.wait()
        r_in.wait()
        m_in.wait()
        ffn_stage(sizes, r_in.ref, m_in.ref, small_in.ref, w1, w2, copies, sends, sends[3].ref, None)

    return call(
        kernel, me, [r, mask, small], ffn_outs(sizes, False), held=bufs, scratch=ffn_scratch(sizes, False),
        micros=FORWARD,
    )


def pack_outs(shards, count, relative):
    if relative:
        return [shape((4, count, C), BF)] * 2
    return [shape((shards, count, C), BF)]


def send_pack(dw, outs, rows, sem):
    each = len(outs) == 2
    copies = []
    for i, out in enumerate(outs):
        src = dw.at[pl.ds(4 * i, 4), rows] if each else dw.at[:, rows]
        copies.append(pltpu.make_async_copy(src, out.at[:, rows], sem))
    for copy in copies:
        copy.start()
    return copies


def ffn_backward(sizes, me, relative, dy, n2, g, slope, mask, w_ffn, where, rest, deps):
    raw = isinstance(dy, tuple)
    globals_, locals_, shards = sizes
    windows = 4 * globals_ + locals_
    rows = windows * CELL
    part = C // shards
    deep = FF // shards
    count = 4 * part + deep
    chunks = chunks_of(rows)
    packs = pack_outs(shards, count, relative)
    n_ffn = len(w_ffn)

    def kernel(me_ref, feeds, sends, held, dw_out, w1, w2, dw, dyl, dh, acc, acc1, sem, sem2, *more):
        n_in, g_in, s_in, m_in = feeds[:4]
        dy_feeds = feeds[4 : 6 if raw else 5]
        ds_out = sends[0]
        ds_ref = ds_out.ref
        more = list(more)
        tmp = more.pop(0) if raw else None
        dy_ref = more.pop(0) if raw else dy_feeds[0].ref
        dn_ref = sends[1].ref if rest is None else more.pop(0)
        for feed in dy_feeds:
            feed.start()
        m_in.start()
        copies = start_ffn_weights(held[:n_ffn], me_ref, where, part, deep, w1, w2, sem)
        for i, here in enumerate(chunks):
            s_in.start(i, here)
        n_in.start()
        g_in.start()
        acc[...] = jnp.zeros_like(acc)
        acc1[...] = jnp.zeros_like(acc1)
        mask_ref = m_in.wait()
        if raw:

            def write(tile, v):
                dy_ref[pl.ds(pl.multiple_of(tile * 8, 8), 8), :] = v

            crops_in(dy_feeds[0].wait(), dy_feeds[1].wait(), write, globals_, locals_, tmp)
        else:
            dy_feeds[0].wait()

        def step(i):
            here = pl.ds(i * CELL, CELL)
            d = dy_ref[here, :] * wide(mask_ref[here, :])
            dyl[here, :] = d.astype(BF)
            acc[...] += fold8(d)

        several(windows, NORM_UNROLL, step)
        for copy in copies:
            copy.wait()
        for i, here in enumerate(chunks):
            s_ref = s_in.wait(i)
            for t in range(FF // C):
                cols = slice(t * C, (t + 1) * C)
                d = mm_nt(dyl[here, :], w2[cols, :]) * s_ref[here, cols].astype(F32)
                acc1[:, cols] += fold8(d)
                dh[here, cols] = d.astype(BF)
            dn = None
            for t in range(FF // C):
                one = mm_nt(dh[here, t * C : (t + 1) * C], w1[t])
                dn = one if dn is None else dn + one
            dn_ref[here, :] = dn
            if rest is None:
                sends[1].start(i, here)

        if rest is not None:
            wp, acc2, sem3 = more
            r_in, small_in = feeds[-2:]
            r_in.start()
            small_in.start()
            plan = [(rest[3] + 3 * part, part, rows_of(wp, 0, part))]
            late = start_weights(held[n_ffn : n_ffn + len(rest[2])], me_ref, plan, sem3)
        n_ref = n_in.wait()
        g_ref = g_in.wait()
        going = []
        for t in range(FF // C):
            cols = slice(t * C, (t + 1) * C)
            one = mm_tn(n_ref[...], dh[:, cols]).astype(BF)
            for d in range(shards):
                dw[slot_of(d, me_ref, relative), t * part : (t + 1) * part, :] = one[d * part : (d + 1) * part]
            going += send_pack(dw, dw_out, pl.ds(t * part, part), sem2)
        for t in range(FF // C):
            cols = slice(t * C, (t + 1) * C)
            two = mm_tn(g_ref[:, cols], dyl[...]).astype(BF)
            for d in range(C // deep):
                here = pl.ds(4 * part, deep)
                dw[slot_of(t * (C // deep) + d, me_ref, relative), here, :] = two[d * deep : (d + 1) * deep]
        going += send_pack(dw, dw_out, pl.ds(4 * part, deep), sem2)
        ds_ref[0:1, :] = jnp.sum(acc[...], axis=0, keepdims=True)
        for t in range(FF // C):
            ds_ref[1 + t : 2 + t, :] = jnp.sum(acc1[:, t * C : (t + 1) * C], axis=0, keepdims=True)
        ds_ref[5:8, :] = jnp.zeros((3, C), F32)
        ds_out.start()
        if rest is not None:
            r_in.wait()
            gain = small_in.wait()[G_ROW + 1 : G_ROW + 2]
            ready = [Ready(v) for v in (dn_ref, dy_ref, r_in.ref, mask_ref)]
            norm_two_stage(rows, ready, gain, wp, late, acc2, sends[1:])
        for copy in going:
            copy.wait()

    full = pltpu.VMEM((rows, C), F32)
    outs = [shape((8, C), F32)] + ([shape((rows, C), F32)] if rest is None else norm_two_outs(rows))
    scratch = [
        pltpu.VMEM((FF // C, C, C), BF),
        pltpu.VMEM((FF, C), BF),
        pltpu.VMEM((shards, count, C), BF),
        pltpu.VMEM((rows, C), BF),
        pltpu.VMEM((rows, FF), BF),
        pltpu.VMEM((8, C), F32),
        pltpu.VMEM((8, FF), F32),
        pltpu.SemaphoreType.DMA,
        pltpu.SemaphoreType.DMA,
    ] + ([CROP_TMP, full] if raw else [])
    ins = [n2, g, slope, mask, *(dy if raw else [dy])]
    held = list(w_ffn)
    if rest is not None:
        scratch += [full, *NORM_TWO]
        ins += rest[:2]
        held += rest[2]
    return call(
        kernel, me, ins, outs, held=held + list(deps), packs=packs, scratch=scratch, micros=BACKWARD,
    )


def norm_two_stage(rows, feeds, gain, wp, copies, acc, sends):
    dn_in, dy_in, r_in, m_in = feeds
    dn_ref, dy_ref, r_ref, mask_ref = [v.ref for v in feeds]
    dr_out, drl_out, do_out, ds_out = sends
    dr_ref, drl, do_ref, ds_ref = [v.ref for v in sends]
    chunks = chunks_of(rows)
    each = chunks[0].size // CELL
    acc[...] = jnp.zeros_like(acc)
    for i, here in enumerate(chunks):
        for feed in feeds:
            feed.wait(i)
        sums = [None] * 3
        for w in range(i * each, (i + 1) * each):
            at = pl.ds(w * CELL, CELL)
            dn = dn_ref[at, :]
            xhat, rstd = norm_parts(r_ref[at, :])
            dr = norm_back(dn, xhat, rstd, gain) + dy_ref[at, :] * wide(mask_ref[at, :])
            sums = [plus(a, fold8(v)) for a, v in zip(sums, (dn * xhat, dn, dr))]
            dr_ref[at, :] = dr
            drl[at, :] = dr.astype(BF)
        for t in range(3):
            acc[t] += sums[t]
        dr_out.start(i, here)
        drl_out.start(i, here)
        if i == 0:
            for copy in copies:
                copy.wait()
        do_ref[here, :] = mm_nt(drl[here, :], wp[0]).astype(BF)
        do_out.start(i, here)
    for t in range(3):
        ds_ref[t : t + 1, :] = jnp.sum(acc[t], axis=0, keepdims=True)
    ds_ref[3:8, :] = jnp.zeros((5, C), F32)
    ds_out.start()


def norm_two_outs(rows):
    low = shape((rows, C), BF)
    return [shape((rows, C), F32), low, low, shape((8, C), F32)]


NORM_TWO = [pltpu.VMEM((1, C, C), BF), pltpu.VMEM((3, 8, C), F32), pltpu.SemaphoreType.DMA]


def norm_two_backward(sizes, me, dn, dy, r, mask, small, w_att, first, deps):
    globals_, locals_, shards = sizes
    rows = (4 * globals_ + locals_) * CELL
    part = C // shards

    def kernel(me_ref, feeds, sends, held, packs, wp, acc, sem):
        dn_in, dy_in, r_in, m_in, small_in = feeds
        small_in.start()
        for i, here in enumerate(chunks_of(rows)):
            for feed in (r_in, dn_in, dy_in, m_in):
                feed.start(i, here)
            if i == 0:
                plan = [(first + 3 * part, part, rows_of(wp, 0, part))]
                copies = start_weights(held[: len(w_att)], me_ref, plan, sem)
        gain = small_in.wait()[G_ROW + 1 : G_ROW + 2]
        norm_two_stage(rows, feeds[:4], gain, wp, copies, acc, sends)

    return call(
        kernel, me, [dn, dy, r, mask, small], norm_two_outs(rows), held=[*w_att, *deps], micros=BACKWARD,
        scratch=NORM_TWO,
    )


def norm_one_stage(rows, feeds, gain, w, dq, dk, dv, acc, dc_out, ds_out):
    dr_in, c_in, m_in = feeds
    dr_ref, c_ref, mask_ref = [v.ref for v in feeds]
    dc, ds_ref = dc_out.ref, ds_out.ref
    chunks = chunks_of(rows)
    each = chunks[0].size // CELL
    for i, here in enumerate(chunks):
        total = mm_nt(dq(i)[here, :], w[0]) + mm_nt(dk(i)[here, :], w[1]) + mm_nt(dv(i)[here, :], w[2])
        for feed in feeds:
            feed.wait(i)
        sums = [None] * 2
        for j in range(each):
            window = i * each + j
            at, tiles = pl.ds(window * CELL, CELL), pl.ds(window * 8, 8)
            d = total[j * CELL : (j + 1) * CELL]
            xhat, rstd = norm_parts(c_ref[tiles].reshape(CELL, C))
            sums = [plus(a, fold8(v)) for a, v in zip(sums, (d * xhat, d))]
            full = norm_back(d, xhat, rstd, gain) + dr_ref[at, :]
            dc[tiles] = (full * wide(mask_ref[at, :])).reshape(8, 8, C)
        for t in range(2):
            acc[t] += sums[t]
        dc_out.start(i, tiles_of(here))
    for t in range(2):
        ds_ref[t : t + 1, :] = jnp.sum(acc[t], axis=0, keepdims=True)
    ds_ref[2:8, :] = jnp.zeros((6, C), F32)
    ds_out.start()


def start_norm_one(rows, feeds):
    dr_in, c_in, m_in = feeds
    for i, here in enumerate(chunks_of(rows)):
        dr_in.start(i, here)
        m_in.start(i, here)
        c_in.start(i, tiles_of(here))


def mix_backward(sizes, kind, me, relative, q, k, v, p, do, n1, o, drl, mask, rest, last, deps):
    globals_, locals_, shards = sizes
    windows = 4 * globals_ + locals_
    rows = windows * CELL
    part = C // shards
    packs = pack_outs(shards, 4 * part, relative)
    low = shape((rows, C), BF)
    eight = shape((8, C), F32)

    def kernel(me_ref, feeds, sends, held, dw_out, acc, slope, dw, sem, *more):
        q_in, k_in, v_in, p_in, do_in, n_in, o_in, drl_in, m_in = feeds[:9]
        q_ref, k_ref, v_ref, p_ref, do_ref, n_ref, o_ref, drl, mask_ref = [v.ref for v in feeds[:9]]
        if rest is None:
            dq, dk, dv = [v.ref for v in sends[:3]]
            go = [send.start for send in sends[:3]]
            ds_out = sends[3]
        else:
            dq, dk, dv, w, acc1, sem_w = more[:6]
            go = [lambda: None] * 3
            dc_out, ds_out, one_out = sends if last is None else [Ready(v) for v in more[6:9]]
        ds_ref = ds_out.ref
        order = (v_in, do_in, p_in, q_in, k_in) if kind == 0 else (q_in, do_in, p_in, v_in, k_in)
        waits = [feed.wait for feed in order]
        for feed in order:
            feed.start()
        if rest is None:
            m_in.start()
            waits.append(m_in.wait)
        else:
            for i, here in enumerate(chunks_of(rows)):
                m_in.start(i, here)
            plan = [(rest[4] + i * part, part, rows_of(w, i, part)) for i in range(3)]
            copies = start_weights(held[: len(rest[3])], me_ref, plan, sem_w)
            dr_in, c_in, small_in = feeds[9:12]
            small_in.start()
            waits += [m_in.wait_all, small_in.wait]
        for feed in (n_in, o_in, drl_in):
            feed.start()
        if rest is not None:
            dr_in.start()
            c_in.start()
            for feed in feeds[12:]:
                feed.start()
        acc[...] = jnp.zeros_like(acc)
        if kind == 0:
            spatial_backward(q_ref, k_ref, v_ref, p_ref, do_ref, dq, dk, dv, acc, slope, windows, waits, go)
        else:
            channel_backward(
                q_ref, k_ref, v_ref, mask_ref, p_ref, do_ref, dq, dk, dv, acc, slope, globals_, locals_, waits, go
            )
        for t in range(2):
            ds_ref[t : t + 1, :] = jnp.sum(acc[t], axis=0, keepdims=True)
        ds_ref[2:8, :] = jnp.zeros((6, C), F32)
        ds_out.start()
        for feed in (n_in, o_in, drl_in):
            feed.wait()
        going = []
        for i, left, right in ((1, n_ref, dk), (2, n_ref, dv), (0, n_ref, dq), (3, o_ref, drl)):
            one = mm_tn(left[...], right[...]).astype(BF)
            for d in range(shards):
                dw[slot_of(d, me_ref, relative), i * part : (i + 1) * part, :] = one[d * part : (d + 1) * part]
            going += send_pack(dw, dw_out, pl.ds(i * part, part), sem)
        if rest is not None:
            acc1[...] = jnp.zeros_like(acc1)
            for copy in copies:
                copy.wait()
            dr_in.wait()
            c_in.wait()
            feeds_one = [Ready(v.ref) for v in (dr_in, c_in, m_in)]
            gain = small_in.ref[G_ROW : G_ROW + 1]
            norm_one_stage(
                rows, feeds_one, gain, w, lambda i: dq, lambda i: dk, lambda i: dv, acc1, dc_out, one_out
            )
        if last is not None:
            u_ref, ffn, two = [feed.wait() for feed in feeds[12:]]
            acck = more[9]
            conv_backward(dc_out.ref, u_ref, sends[1].ref, small_in.ref, acck, globals_, locals_)
            sends[1].start()
            write_table(sends[0].ref, acck, one_out.ref, ds_ref, two, ffn)
            sends[0].start()
        for copy in going:
            copy.wait()

    scratch = [
        pltpu.VMEM((2, 8, C), F32), pltpu.VMEM(p.shape, BF), pltpu.VMEM((shards, 4 * part, C), BF),
        pltpu.SemaphoreType.DMA,
    ]
    ins = [q, k, v, p, do, n1, o, drl, mask]
    if rest is None:
        outs, held = [low, low, low, eight], list(deps)
    else:
        outs, held = [shape((windows * 8, 8, C), F32), eight, eight], [*rest[3], *deps]
        ins += [rest[0], rest[1], rest[2]]
        scratch += [pltpu.VMEM((rows, C), BF)] * 3
        scratch += [pltpu.VMEM((3, C, C), BF), pltpu.VMEM((2, 8, C), F32), pltpu.SemaphoreType.DMA]
    if last is not None:
        ins += last
        outs = [shape((TAB, C), F32), shape((windows * 8, 8, C), F32)]
        eight = pltpu.VMEM((8, C), F32)
        scratch += [pltpu.VMEM((windows * 8, 8, C), F32), eight, eight, pltpu.VMEM((10, 8, C), F32)]
    return call(kernel, me, ins, outs, held=held, packs=packs, scratch=scratch, micros=BACKWARD)


class Ready:
    def __init__(self, ref):
        self.ref = ref

    def start(self, k=0, part=None):
        pass

    def wait(self, k=0):
        return self.ref


def norm_one_backward(sizes, me, dr, c, dq, dk, dv, mask, small, bufs, first, deps):
    globals_, locals_, shards = sizes
    windows = 4 * globals_ + locals_
    rows = windows * CELL
    part = C // shards

    def kernel(me_ref, feeds, sends, held, packs, w, acc, sem):
        dr_in, c_in, dq_in, dk_in, dv_in, m_in, small_in = feeds
        plan = [(first + i * part, part, rows_of(w, i, part)) for i in range(3)]
        copies = start_weights(held[: len(bufs)], me_ref, plan, sem)
        small_in.start()
        for i, here in enumerate(chunks_of(rows)):
            for feed in (dq_in, dk_in, dv_in):
                feed.start(i, here)
        start_norm_one(rows, (dr_in, c_in, m_in))
        acc[...] = jnp.zeros_like(acc)
        gain = small_in.wait()[G_ROW : G_ROW + 1]
        for copy in copies:
            copy.wait()
        norm_one_stage(rows, (dr_in, c_in, m_in), gain, w, dq_in.wait, dk_in.wait, dv_in.wait, acc, *sends)

    return call(
        kernel, me, [dr, c, dq, dk, dv, mask, small], [shape((windows * 8, 8, C), F32), shape((8, C), F32)],
        held=[*bufs, *deps], micros=BACKWARD,
        scratch=[pltpu.VMEM((3, C, C), BF), pltpu.VMEM((2, 8, C), F32), pltpu.SemaphoreType.DMA],
    )


def write_table(tab, acck, one, mix, two, ffn):
    rows = [jnp.sum(acck[t], axis=0, keepdims=True) for t in range(10)]
    rows += [one[1:2, :], mix[0:1, :], mix[1:2, :], two[2:3, :], two[1:2, :], ffn[0:1, :], one[0:1, :], two[0:1, :]]
    rows += [ffn[1 + t : 2 + t, :] for t in range(FF // C)]
    tab[...] = jnp.zeros_like(tab)
    for t, row in enumerate(rows):
        tab[t : t + 1, :] = row


def position_backward(sizes, me, dc, u, mask, small, ds_ffn, ds_two, ds_mix, ds_one, last, deps):
    globals_, locals_, _ = sizes
    windows = 4 * globals_ + locals_

    def kernel(me_ref, feeds, sends, held, packs, acck, *more):
        dc_ref, u_ref, small_ref, ffn, two, mix, one = [v.ref for v in feeds[:7]]
        tab = sends[0].ref
        du_ref = more[0] if last else sends[1].ref
        for feed in feeds:
            feed.start()
        for feed in feeds:
            feed.wait()
        conv_backward(dc_ref, u_ref, du_ref, small_ref, acck, globals_, locals_)
        if last:
            mask_ref = feeds[7].ref

            def read(tile):
                here = pl.ds(pl.multiple_of(tile * 8, 8), 8)
                return du_ref[tile] * wide(mask_ref[here, :])

            crops_out(read, sends[1].ref, sends[2].ref, globals_, locals_, more[1])
            sends[2].start()
        sends[1].start()
        write_table(tab, acck, one, mix, two, ffn)
        sends[0].start()

    full = (windows * 8, 8, C)
    ins = [dc, u, small, ds_ffn, ds_two, ds_mix, ds_one]
    outs = [shape((TAB, C), F32)]
    scratch = [pltpu.VMEM((10, 8, C), F32)]
    if last:
        ins.append(mask)
        outs += crop_outs(globals_, locals_, F32)
        scratch += [pltpu.VMEM(full, F32), pltpu.VMEM((WIN, SIDE, C), F32)]
    else:
        outs.append(shape(full, F32))
    return call(kernel, me, ins, outs, held=deps, scratch=scratch, micros=BACKWARD)


def join(values, deps):
    values, deps = list(values), list(deps)

    def kernel(*refs):
        pass

    return pl.pallas_call(
        kernel,
        out_shape=[shape(v.shape, v.dtype) for v in values],
        in_specs=[HELD] * (len(values) + len(deps)),
        out_specs=[HELD] * len(values),
        input_output_aliases={i: i for i in range(len(values))},
    )(*values, *deps)


def place_and_extents(index, extent, globals_):
    sizes = jnp.concatenate([jnp.full((globals_ * 4, 2), WIN, jnp.int32), extent.astype(jnp.int32)], axis=0)
    return jnp.concatenate([index.astype(jnp.int32).reshape(1), sizes.reshape(-1)])


def layer(sizes, me, tokens, cotangent, plan):
    windows = 4 * sizes[0] + sizes[1]
    rows = windows * CELL
    dy = cotangent
    kept = []
    places = []
    mask = None
    u = tokens
    for b in range(2):
        att, att_first = plan.att_weights(b, u)
        if b == 0:
            r, small, *saved, u, mask = attention_forward(sizes, b, me, u, mask, att, att_first)
            ffn, where = plan.ffn_weights(b, r)
            n2, g, slope, out = ffn_forward(sizes, me, r, mask, small, ffn, where)
        else:
            ffn, where = plan.ffn_weights(b, u)
            r, small, *saved, n2, g, slope, out_global, out_local = attention_forward(
                sizes, b, me, u, mask, att, att_first, where
            )
        places.append((att, att_first, ffn, where))
        kept.append((u, r, small, saved, (n2, g, slope)))
        if b == 0:
            u = out.reshape(windows * 8, 8, C)
    out = (out_global, out_local)
    tables = [None, None]
    deps = []
    for b in (1, 0):
        u, r, small, (c, n1, q, k, v, o, p), (n2, g, slope) = kept[b]
        att, att_first, ffn, where = places[b]
        rel_ffn, rel_att = plan.relative[b]
        rest = (r, small, att, att_first)
        ds_ffn, dr, drl, do, ds_two, *dw = ffn_backward(
            sizes, me, rel_ffn, dy, n2, g, slope, mask, ffn, where, rest, deps
        )
        deps = plan.step(b, 0, dr, dw)
        mixed = (q, k, v, p, do, n1, o, drl, mask)
        rest = (dr, c, small, att, att_first)
        if b == 1:
            tables[b], *du, dw = mix_backward(
                sizes, b, me, rel_att, *mixed, rest, (u, ds_ffn, ds_two), deps
            )
            plan.step(b, 2, du[0], [dw])
        else:
            dc, ds_mix, ds_one, *dw = mix_backward(sizes, b, me, rel_att, *mixed, rest, None, deps)
            deps = plan.step(b, 2, dc, dw)
            tables[b], *du = position_backward(
                sizes, me, dc, u, mask, small, ds_ffn, ds_two, ds_mix, ds_one, True, deps
            )
        deps = plan.step(b, 4, du[0], tables)
        if b == 1:
            dy = du[0].reshape(rows, C)
    return out, du


def xor(v, axis, turn):
    size = lax.axis_size(axis)
    return lax.ppermute(v, axis, [(i, i ^ turn) for i in range(size)])


def gather_near(own):
    return [own, xor(own, "fsdp", 2), xor(own, "fsdp", 4), xor(own, "fsdp", 6)]


def gather_core(near):
    out = []
    for v in near:
        out += [v, xor(v, "fsdp", 1)]
    return out


def add(*terms):
    total = terms[0].astype(F32)
    for term in terms[1:]:
        total = total + term.astype(F32)
    return total.astype(BF)


def to_core(pack):
    return xor(pack[1], "fsdp", 1)


def to_chips(parts):
    return [xor(v, "fsdp", 2 * i + 2) for i, v in enumerate(parts[1:])]


def core_sums(pack, got):
    return [add(pack[0][i], got[i]) for i in range(4)]


def own_lanes(table):
    shards, index = lax.axis_size("fsdp"), lax.axis_index("fsdp")
    part, deep = C // shards, FF // shards
    main = lax.dynamic_slice(table, (0, 0, index * part), (2, B_ROW, part)).reshape(2, B_ROW * part)
    bias = lax.dynamic_slice(table[:, B_ROW : B_ROW + FF // C].reshape(2, FF), (0, index * deep), (2, deep))
    return jnp.concatenate([main, bias], axis=1)


class Direct:
    relative = ((True, True), (False, False))

    def __init__(self, part, deep, packs):
        self.ffn_first = 4 * part
        self.att_first = 4 * part + deep
        self.att0 = gather_near(packs[0])
        self.ffn0 = gather_near(packs[1])
        self.whole1 = lax.all_gather(packs[2], "fsdp", axis=0)

    def att_weights(self, b, u):
        if b == 0:
            return gather_core(self.att0), 0
        return [self.whole1], self.att_first

    def ffn_weights(self, b, r):
        if b == 0:
            bufs = gather_core(join(self.ffn0, [r]))
            return bufs, (len(bufs), 0, 0, self.ffn_first)
        return [self.whole1], (1, 0, 0, self.ffn_first)

    def step(self, b, stage, token, new=None):
        if (b, stage) == (1, 0):
            self.f1_own = lax.psum_scatter(new[0], "fsdp", scatter_dimension=0, tiled=True)[0]
        elif (b, stage) == (1, 2):
            self.a1_own = lax.psum_scatter(new[0], "fsdp", scatter_dimension=0, tiled=True)[0]
        elif (b, stage) == (0, 0):
            core = to_core(new)
            (f1_own,) = join([self.f1_own], [token])
            self.f0_sums = core_sums(new, core)
            self.f0_chips = to_chips(self.f0_sums)
            self.f1_sum = Spread(f1_own)
            self.f1_sum.first()
            return [*self.f0_sums, self.f1_sum.keep]
        elif (b, stage) == (0, 2):
            self.a0, self.a0_core = new, to_core(new)
            *chips, self.f1_sum.got = join([*self.f0_chips, self.f1_sum.got], [token])
            self.f0_sum = Spread(add(self.f0_sums[0], *chips))
            self.f0_sum.first()
            self.f1_sum.second()
            return [self.f0_sum.keep, self.f1_sum.half]
        elif (b, stage) == (0, 4):
            core, self.f0_sum.got, self.f1_sum.got, a1_own = join(
                [self.a0_core, self.f0_sum.got, self.f1_sum.got, self.a1_own], [token]
            )
            a1 = lax.psum(a1_own, "dp")
            a0_sums = core_sums(self.a0, core)
            a0_chips = to_chips(a0_sums)
            *tables, self.f0_sum.got, self.f1_sum.got = join(
                [*new, self.f0_sum.got, self.f1_sum.got], [a0_sums[0]]
            )
            self.f0_sum.second()
            self.f1_sum.third()
            table = jnp.stack(tables).astype(BF)
            for turn in (1, 2, 4):
                table = add(table, xor(table, "fsdp", turn))
            *a0_chips, self.f0_sum.got, table = join([*a0_chips, self.f0_sum.got, table], [])
            a0_sum = Spread(add(a0_sums[0], *a0_chips))
            a0_sum.first()
            self.f0_sum.third()
            table = own_lanes(table)
            other = xor(table, "dp", 1)
            a0_sum.got, other = join([a0_sum.got, other], [])
            a0_sum.second()
            table = add(table, other)
            table = add(table, xor(table, "dp", 2))
            a0_sum.third()
            (a1,) = join([a1], [a0_sum.whole])
            near = [self.f0_sum.result(), a0_sum.result()]
            self.done = [near, [self.f1_sum.result(), a1]], table
        return []

    def results(self):
        return self.done


class Spread:
    def __init__(self, v):
        n = v.shape[0] // 2
        bit = lax.axis_index("dp") & 1
        self.low = bit == 0
        self.keep = lax.dynamic_slice(v, (bit * n, 0), (n, C))
        self.send = lax.dynamic_slice(v, ((1 - bit) * n, 0), (n, C))

    def first(self):
        self.got = xor(self.send, "dp", 1)

    def second(self):
        self.half = add(self.keep, self.got)
        self.got = xor(self.half, "dp", 2)

    def third(self):
        self.whole = add(self.half, self.got)
        self.got = xor(self.whole, "dp", 1)

    def result(self):
        whole, other = self.whole, self.got
        return jnp.concatenate([jnp.where(self.low, whole, other), jnp.where(self.low, other, whole)])


class Plain:
    relative = ((False, False), (False, False))

    def __init__(self, part, deep, packs):
        self.packs = [[None, None], [None, None]]
        self.first = 4 * part
        self.cut = 4 * part + deep
        self.whole = [lax.all_gather(pack, "fsdp", axis=0) for pack in packs]

    def att_weights(self, b, u):
        return [self.whole[b]], self.cut

    def ffn_weights(self, b, r):
        return [self.whole[b]], (1, 0, 0, self.first)

    def step(self, b, stage, token, new=None):
        if stage in (0, 2):
            self.packs[b][stage // 2] = new[0]
        if (b, stage) == (0, 4):
            self.table = new
        return []

    def results(self):
        grads = [
            lax.psum([lax.psum_scatter(v, "fsdp", scatter_dimension=0, tiled=True)[0] for v in pair], "dp")
            for pair in self.packs
        ]
        return grads, own_lanes(lax.psum(jnp.stack(self.table).astype(BF), ("dp", "fsdp")))


def body(
    global_tokens,
    local_tokens,
    crop_extent,
    conv_weight,
    vectors,
    gains,
    qkv_weight,
    proj_weight,
    fc1_weight,
    fc1_bias,
    fc2_weight,
    global_cotangent,
    local_cotangent,
):
    shards = lax.axis_size("fsdp")
    direct = shards == 8 and lax.axis_size("dp") == 4
    part = C // shards
    globals_, locals_ = global_tokens.shape[0], local_tokens.shape[0]
    sizes = (globals_, locals_, shards)
    index = lax.axis_index("fsdp")
    me = place_and_extents(index, crop_extent, globals_)

    own_small = jnp.concatenate([conv_weight, vectors, gains], axis=1)
    own_bias = fc1_bias.reshape(2, 1, FF // shards)
    start = index * (FF // shards)

    def att(b):
        table = lax.dynamic_update_slice(jnp.zeros((TAB, C), BF), own_small[b], (0, index * part))
        table = lax.dynamic_update_slice(table, own_bias[b], (B_ROW + start // C, start % C))
        return [qkv_weight[b][:, i * C : (i + 1) * C] for i in range(3)] + [proj_weight[b], table]

    def ffn(b):
        return [fc1_weight[b][:, i * C : (i + 1) * C] for i in range(FF // C)] + [fc2_weight[b]]

    groups = [att(0), ffn(0), ffn(1) + att(1)] if direct else [ffn(b) + att(b) for b in range(2)]
    packs = [jnp.concatenate(group, axis=0) for group in groups]
    plan = (Direct if direct else Plain)(part, FF // shards, packs)
    out, grad = layer(
        sizes, me,
        (global_tokens, local_tokens),
        (global_cotangent, local_cotangent),
        plan,
    )
    grads, table = plan.results()
    deep = FF // shards

    def cut(half, start, n):
        return jnp.stack(
            [
                jnp.concatenate([g[half][(start + i) * part : (start + i + 1) * part] for i in range(n)], axis=1)
                for g in grads
            ]
        ).astype(F32)

    table = table.astype(F32)
    main = table[:, : B_ROW * part].reshape(2, B_ROW, part)
    bias = table[:, B_ROW * part :]
    fc2 = jnp.stack([g[0][4 * part :] for g in grads]).astype(F32)
    proj = jnp.stack([g[1][3 * part :] for g in grads]).astype(F32)
    return (
        out[0], out[1], grad[0], grad[1],
        main[:, 0:9], main[:, 9:16], main[:, 16:18],
        cut(1, 0, 3), proj, cut(0, 0, 4), bias, fc2,
    )


def solution(mesh):
    crops = P(("dp", "fsdp"), None, None, None)
    last = P(None, None, "fsdp")
    middle = P(None, "fsdp", None)
    return jax.shard_map(
        body,
        mesh=mesh,
        in_specs=(
            crops, crops, P(("dp", "fsdp"), None), last, last, last, middle, middle, middle,
            P(None, "fsdp"), middle, crops, crops,
        ),
        out_specs=(
            crops, crops, crops, crops, last, last, last, middle, middle, middle, P(None, "fsdp"), middle,
        ),
        check_vma=False,
    )
```
